32 devices in a mesh: dp: 4 (over x, core), fsdp: 8 (over z, y).
Axes of the slice: x: 2, y: 2, z: 4, core: 2. Of those that a mesh axis runs over, the one named last changes fastest.
Arguments:
- frames: bfloat16 [51200, 640], P(('dp', 'fsdp')), may hold values from -6 to 6
- cotangent: bfloat16 [51200, 640], P(('dp', 'fsdp')), may hold values from -6 to 6
- span_starts: int32 [128, 32], P(('dp', 'fsdp')), may hold values from 0 to 390
- query_weight: bfloat16 [768, 768], P('fsdp'), may hold values from -0.25 to 0.25
- key_weight: bfloat16 [768, 768], P('fsdp'), may hold values from -0.25 to 0.25
- value_weight: bfloat16 [768, 768], P('fsdp'), may hold values from -0.25 to 0.25
- out_weight: bfloat16 [768, 768], P('fsdp'), may hold values from -3 to 3
- query_bias: bfloat16 [768], P('fsdp'), may hold values from -2.390625 to 2.390625
- value_bias: bfloat16 [768], P('fsdp'), may hold values from -2.390625 to 2.390625
- out_bias: bfloat16 [768], P('fsdp'), may hold values from -2.390625 to 2.390625
- first_gain: bfloat16 [768], P('fsdp'), may hold values from 0.3984375 to 1.59375
- first_shift: bfloat16 [768], P('fsdp'), may hold values from -2.390625 to 2.390625
- up_weight: bfloat16 [768, 3072], P('fsdp'), may hold values from -0.25 to 0.25
- up_bias: bfloat16 [3072], P('fsdp'), may hold values from -2.390625 to 2.390625
- down_weight: bfloat16 [3072, 768], P('fsdp'), may hold values from -0.15625 to 0.15625
- down_bias: bfloat16 [768], P('fsdp'), may hold values from -2.390625 to 2.390625
- second_gain: bfloat16 [768], P('fsdp'), may hold values from 0.3984375 to 1.59375
- second_shift: bfloat16 [768], P('fsdp'), may hold values from -2.390625 to 2.390625
- mask_vector: bfloat16 [768], P('fsdp'), may hold values from -5 to 5
Outputs:
- output: bfloat16 [51200, 640], P(('dp', 'fsdp'))
- frames_grad: bfloat16 [51200, 640], P(('dp', 'fsdp'))
- query_weight_grad: float32 [768, 768], P('fsdp')
- key_weight_grad: float32 [768, 768], P('fsdp')
- value_weight_grad: float32 [768, 768], P('fsdp')
- out_weight_grad: float32 [768, 768], P('fsdp')
- query_bias_grad: float32 [768], P('fsdp')
- value_bias_grad: float32 [768], P('fsdp')
- out_bias_grad: float32 [768], P('fsdp')
- first_gain_grad: float32 [768], P('fsdp')
- first_shift_grad: float32 [768], P('fsdp')
- up_weight_grad: float32 [768, 3072], P('fsdp')
- up_bias_grad: float32 [3072], P('fsdp')
- down_weight_grad: float32 [3072, 768], P('fsdp')
- down_bias_grad: float32 [768], P('fsdp')
- second_gain_grad: float32 [768], P('fsdp')
- second_shift_grad: float32 [768], P('fsdp')
- mask_vector_grad: float32 [768], P('fsdp')
The draws below stay inside these ranges and needn't reach their ends.
Inputs may be any that keep to these rules, and one draw needn't show every extreme that they name: `span_starts`: first frame of a masked span of 10 frames within its utterance; spans may intersect.
All inputs are finite; a program needn't handle non-finite values.
Results may differ from the reference program's by a relative error of at most 0.015.
Values may be sent and summed in bfloat16 or wider, within the bound.
No kernel may reach another device: no remote copies, remote signals or barrier semaphores. Data moves between devices by JAX's collectives and lax.ppermute only.
A program may use at most 256 MiB of HBM per device.

```python
import math
import jax
import jax.numpy as jnp
from jax import lax

D_MAX = 768
FF_MAX = 3072
HEADS = 10
HEAD_DIM = 64
FF = 2560
D = 640
FRAMES = 400
SPAN = 10
SPANS = 32
UTTERANCES = 128
TOKENS = 51200


def place_ends(entries, stream_key, smallest, high):
    longest = entries.shape.index(max(entries.shape))
    spots = []
    for shift in (0, 1):
        where = [jax.random.randint(jax.random.fold_in(stream_key, axis), (), 0, length) for axis, length in enumerate(entries.shape)]
        where[longest] = (where[longest] + shift) % entries.shape[longest]
        spots.append(tuple(where))
    return entries.at[spots[0]].set(smallest).at[spots[1]].set(high)


def strengthened(drawn, rng, source, target, shards_of, factor):
    def block_of(axis_at):
        return (jnp.arange(drawn.shape[axis_at]) // (drawn.shape[axis_at] // shards_of)).reshape((-1,) + (1,) * (drawn.ndim - 1 - axis_at))

    one_side = jax.random.permutation(rng, shards_of)[block_of(target)]
    other_side = (block_of(target) + shards_of // 2) % shards_of
    return jnp.where((block_of(source) == one_side) | (block_of(source) == other_side), factor * drawn, drawn)


def steps_of(stream_key, dims, cuts, smallest, largest):
    level = 1.0
    for dim, blocks in cuts:
        heights = jax.random.uniform(jax.random.fold_in(jax.random.fold_in(stream_key, 6), dim), (blocks,), jnp.float32, smallest / len(cuts), largest / len(cuts))
        level = level * jnp.repeat(jnp.exp(heights), dims[dim] // blocks).reshape((-1,) + (1,) * (len(dims) - 1 - dim))
    return level


def normal_values(key, extent, deviation, reach, shards=(), held_as=jnp.bfloat16):
    factor_of = steps_of(key, extent, shards, -0.22, 0.18) if shards else 1.0
    drawn = jax.random.normal(key, extent, jnp.float32) * deviation * factor_of
    return jnp.minimum(jnp.maximum(drawn, -reach), reach).astype(held_as)


def noise_with(rng, extent, scale, reach, cuts, heavy, kind=jnp.bfloat16):
    entries = scale * jax.random.normal(rng, extent, jnp.float32)
    if cuts:
        entries = entries * steps_of(rng, extent, cuts, -0.22, 0.18)
    return jnp.clip(strengthened(entries, jax.random.fold_in(rng, 3), *heavy), -reach, reach).astype(kind)


def setup_inputs(seed: int = 0) -> dict:
    arg_keys = jax.random.split(jax.random.key(seed), 20)
    return {
        "frames": noise_with(arg_keys[0], (TOKENS, D), 1.0, 6.0, ((0, 32),), (0, 1, 32, 2.75)),
        "cotangent": normal_values(arg_keys[1], (TOKENS, D), 1.0, 6.0, ((0, 32),)),
        "span_starts": place_ends(jax.random.randint(arg_keys[2], (UTTERANCES, SPANS), 0, FRAMES - SPAN + 1), jax.random.fold_in(arg_keys[2], 1), 0, FRAMES - SPAN).astype(jnp.int32),
        "query_weight": normal_values(arg_keys[3], (D_MAX, D_MAX), D ** -0.5, 0.25, ((0, 8),)),
        "key_weight": normal_values(arg_keys[4], (D_MAX, D_MAX), D ** -0.5, 0.25, ((0, 8),)),
        "value_weight": normal_values(arg_keys[5], (D_MAX, D_MAX), D ** -0.5, 0.25, ((0, 8),)),
        "out_weight": normal_values(arg_keys[6], (D_MAX, D_MAX), 4 ** -0.5, 3.0, ((0, 8),)),
        "query_bias": normal_values(arg_keys[7], (D_MAX,), 0.4, 2.390625, ((0, 8),)),
        "value_bias": normal_values(arg_keys[8], (D_MAX,), 0.4, 2.390625, ((0, 8),)),
        "out_bias": normal_values(arg_keys[9], (D_MAX,), 0.4, 2.390625, ((0, 8),)),
        "first_gain": jnp.clip(1.0 + 0.12 * jax.random.normal(arg_keys[10], (D_MAX,), jnp.float32), 0.3984375, 1.59375).astype(jnp.bfloat16),
        "first_shift": normal_values(arg_keys[11], (D_MAX,), 0.4, 2.390625, ((0, 8),)),
        "up_weight": normal_values(arg_keys[12], (D_MAX, FF_MAX), D ** -0.5, 0.25, ((0, 8),)),
        "up_bias": normal_values(arg_keys[13], (FF_MAX,), 0.4, 2.390625, ((0, 8),)),
        "down_weight": normal_values(arg_keys[14], (FF_MAX, D_MAX), (FF // 2) ** -0.5, 0.15625, ((0, 8),)),
        "down_bias": normal_values(arg_keys[15], (D_MAX,), 0.4, 2.390625, ((0, 8),)),
        "second_gain": jnp.clip(1.0 + 0.12 * jax.random.normal(arg_keys[16], (D_MAX,), jnp.float32), 0.3984375, 1.59375).astype(jnp.bfloat16),
        "second_shift": normal_values(arg_keys[17], (D_MAX,), 0.4, 2.390625, ((0, 8),)),
        "mask_vector": normal_values(arg_keys[18], (D_MAX,), 1.0, 5.0, ((0, 8),)),
    }


@jax.custom_vjp
def low(v):
    return lax.optimization_barrier(v.astype(jnp.bfloat16)).astype(jnp.float32)

@jax.custom_vjp
def low_back(v):
    return v

def low_keep(v):
    return (low(v), None)

def low_pass(kept, grad):
    return (grad,)

def back_keep(v):
    return (v, None)

def back_low(kept, grad):
    return (low(grad),)
low.defvjp(low_keep, low_pass)
low_back.defvjp(back_keep, back_low)

def matmul_high(left, right):
    return jnp.dot(left, right, precision=lax.Precision.HIGHEST, preferred_element_type=jnp.float32)

def layer_norm(value, gain, shift):
    center = value - lax.optimization_barrier(jnp.mean(value, axis=-1, keepdims=True))
    spread = lax.optimization_barrier(jnp.mean(center * center, axis=-1, keepdims=True))
    return center * lax.rsqrt(spread + 1e-05) * gain + shift

def span_mask(starts):
    places = jnp.arange(FRAMES, dtype=jnp.int32)[None, :, None]
    inside = (places >= starts[:, None, :]) & (places < starts[:, None, :] + SPAN)
    return jnp.any(inside, axis=2)

def attend(query, key_rows, value_rows):
    query_heads = query.reshape(FRAMES, HEADS, HEAD_DIM)
    key_heads = key_rows.reshape(FRAMES, HEADS, HEAD_DIM)
    value_heads = value_rows.reshape(FRAMES, HEADS, HEAD_DIM)
    raw = jnp.einsum('qhd,khd->hqk', query_heads, key_heads, precision=lax.Precision.HIGHEST) * HEAD_DIM ** (-0.5)
    scores = low_back(raw)
    top = lax.optimization_barrier(jnp.max(scores, axis=-1, keepdims=True))
    expo = jnp.exp(scores - top)
    attn_prob = low(expo / lax.optimization_barrier(jnp.sum(expo, axis=-1, keepdims=True)))
    mixed = jnp.einsum('hqk,khd->qhd', attn_prob, value_heads, precision=lax.Precision.HIGHEST)
    return mixed.reshape(FRAMES, HEADS * HEAD_DIM)
attend_saved = jax.checkpoint(attend)

def layer(params, inputs, masked):
    query_w, key_w, value_w, out_w, query_b, value_b, out_b, gain_one, shift_one, up_w, up_b, down_w, down_b, gain_two, shift_two, mask_vec = params
    start_rows = jnp.where(masked[:, None], mask_vec[None, :D], inputs)
    start_low = low(start_rows)
    query = low(low_back(matmul_high(start_low, query_w[:D, :D]) + query_b[:D]))
    key_rows = low(low_back(matmul_high(start_low, key_w[:D, :D])))
    value_rows = low(low_back(matmul_high(start_low, value_w[:D, :D]) + value_b[:D]))
    count = inputs.shape[0] // FRAMES
    mixed = lax.map(lambda item: attend_saved(item[0], item[1], item[2]), (query.reshape(count, FRAMES, D), key_rows.reshape(count, FRAMES, D), value_rows.reshape(count, FRAMES, D)))
    mixed = low(low_back(mixed.reshape(count * FRAMES, D)))
    branch_one = low_back(matmul_high(mixed, out_w[:D, :D]) + out_b[:D])
    first_out = layer_norm(start_rows + branch_one, gain_one[:D], shift_one[:D])
    hidden_pre = low_back(matmul_high(low(first_out), up_w[:D, :FF]) + up_b[:FF])
    hidden_low = low(jax.nn.gelu(hidden_pre, approximate=False))
    branch_two = low_back(matmul_high(hidden_low, down_w[:FF, :D]) + down_b[:D])
    return layer_norm(first_out + branch_two, gain_two[:D], shift_two[:D])

def reference(frames, cotangent, span_starts, query_weight, key_weight, value_weight, out_weight, query_bias, value_bias, out_bias, first_gain, first_shift, up_weight, up_bias, down_weight, down_bias, second_gain, second_shift, mask_vector):
    params = tuple((piece.astype(jnp.float32) for piece in (query_weight, key_weight, value_weight, out_weight, query_bias, value_bias, out_bias, first_gain, first_shift, up_weight, up_bias, down_weight, down_bias, second_gain, second_shift, mask_vector)))
    group = math.gcd(UTTERANCES, 8)
    blocks = UTTERANCES // group
    inputs_all = frames.astype(jnp.float32).reshape(blocks, group * FRAMES, D)
    cotan_all = cotangent.astype(jnp.float32).reshape(blocks, group * FRAMES, D)
    starts_all = span_starts.reshape(blocks, group, SPANS)

    def step(totals, item):
        inputs, cotan, starts = item
        masked = span_mask(starts).reshape(group * FRAMES)
        result, pull = jax.vjp(lambda prm, xin: layer(prm, xin, masked), params, inputs)
        grads, grad_in = pull(cotan)
        totals = jax.tree.map(jnp.add, totals, grads)
        return (totals, (result.astype(jnp.bfloat16), grad_in.astype(jnp.bfloat16)))
    zeros = tuple((jnp.zeros(piece.shape, jnp.float32) for piece in params))
    totals, (results, grads_in) = lax.scan(step, zeros, (inputs_all, cotan_all, starts_all))
    return (results.reshape(TOKENS, D), grads_in.reshape(TOKENS, D), totals[0], totals[1], totals[2], totals[3], totals[4], totals[5], totals[6], totals[7], totals[8], totals[9], totals[10], totals[11], totals[12], totals[13], totals[14], totals[15])
```

```python
import functools
import jax
import jax.numpy as jnp
from jax import lax
from jax.experimental import pallas as pl
from jax.experimental.pallas import tpu as pltpu
from jax.sharding import PartitionSpec as P

HEADS = 10
HEAD_DIM = 64
FF = 2560
D = 640
FRAMES = 400
SPAN = 10
PAIR = 2 * HEAD_DIM
EPS = 1e-05
F32 = jnp.float32
BF16 = jnp.bfloat16
VMEM_LIMIT = 60 * 1024 * 1024
HID = 512


def dot_nn(a, b):
    return lax.dot_general(a, b, (((1,), (0,)), ((), ())), preferred_element_type=F32)


def dot_nt(a, b):
    return lax.dot_general(a, b, (((1,), (1,)), ((), ())), preferred_element_type=F32)


def dot_tn(a, b):
    return lax.dot_general(a, b, (((0,), (0,)), ((), ())), preferred_element_type=F32)


def mean_last(a):
    return jnp.mean(a, axis=-1, keepdims=True)


def rows_sum(a):
    return jnp.sum(a, axis=0, keepdims=True)


def masked_rows(frames_ref, starts_ref, mask_row):
    places = lax.broadcasted_iota(jnp.int32, (FRAMES, starts_ref.shape[-1]), 0)
    ahead = places - starts_ref[0]
    inside = jnp.where((ahead >= 0) & (ahead < SPAN), 1.0, 0.0)
    masked = jnp.max(inside, axis=1, keepdims=True) > 0.5
    return masked, jnp.where(masked, mask_row, frames_ref[...].astype(F32))


def fetch(place_ref, mine, other, sem, parts):
    pieces = mine.shape[0]

    def copies(source, half):
        for core, first, count, column, target in parts:
            if core != half:
                continue
            for piece in range(pieces):
                rows = min(count, target.shape[0] - piece * count)
                if rows > 0:
                    yield pltpu.make_async_copy(
                        source.at[place_ref[1 + piece], pl.ds(first, rows), :],
                        target.at[pl.ds(piece * count, rows), pl.ds(column, D)],
                        sem,
                    )

    for core in (0, 1):

        @pl.when(place_ref[0] == core)
        def _(core=core):
            started = list(copies(mine, core)) + list(copies(other, 1 - core))
            for copy in started:
                copy.start()
            for copy in started:
                copy.wait()


def fetch_attn(place_ref, mine, other, sem, wq, wk, wv, wo):
    count = mine.shape[1] // 2
    parts = []
    for target, core, first in ((wq, 0, 0), (wk, 0, count), (wv, 1, 0), (wo, 1, count)):
        if target is not None:
            parts.append((core, first, count, 0, target))
    fetch(place_ref, mine, other, sem, parts)


def fetch_ffn(place_ref, mine, other, sem, w1, w2):
    count = mine.shape[1]
    part = count // (FF // D)
    parts = [(0, j * part, part, j * D, w1) for j in range(FF // D)]
    fetch(place_ref, mine, other, sem, parts + [(1, 0, count, 0, w2)])


def attn_forward(
    place_ref, mine_ref, other_ref, starts_ref, frames_ref, vec_ref,
    q_ref, k_ref, v_ref, o_ref, lse_ref, n1_ref, rstd_ref,
    wq_ref, wk_ref, wv_ref, wo_ref, sem,
):
    @pl.when(pl.program_id(0) == 0)
    def _():
        fetch_attn(place_ref, mine_ref, other_ref, sem, wq_ref, wk_ref, wv_ref, wo_ref)

    bq, bv, bo = vec_ref[0:1, :], vec_ref[1:2, :], vec_ref[2:3, :]
    masked, x0 = masked_rows(frames_ref, starts_ref, vec_ref[5:6, :])
    h = x0.astype(BF16)
    scale = HEAD_DIM ** (-0.5)
    q_ref[...] = ((dot_nn(h, wq_ref[...]) + bq).astype(BF16).astype(F32) * scale).astype(BF16)
    k_ref[...] = dot_nn(h, wk_ref[...]).astype(BF16)
    v_ref[...] = (dot_nn(h, wv_ref[...]) + bv).astype(BF16)
    low_lanes = lax.broadcasted_iota(jnp.int32, (FRAMES, PAIR), 1) < HEAD_DIM
    lanes = lax.broadcasted_iota(jnp.int32, (FRAMES, 128), 1)
    lse = jnp.zeros((FRAMES, 128), F32)
    for pair in range(HEADS // 2):
        cols = slice(pair * PAIR, (pair + 1) * PAIR)
        qp, kp, vp = q_ref[:, cols], k_ref[:, cols], v_ref[:, cols]
        parts = []
        for half in range(2):
            keep = low_lanes if half == 0 else jnp.logical_not(low_lanes)
            qh = jnp.where(keep, qp.astype(F32), 0.0).astype(BF16)
            scores = dot_nt(qh, kp)
            top = jnp.max(scores, axis=-1, keepdims=True)
            expo = jnp.exp(scores - top)
            total = jnp.sum(expo, axis=-1, keepdims=True)
            parts.append(dot_nn(expo.astype(BF16), vp) * (1.0 / total))
            lse = jnp.where(lanes == 2 * pair + half, top + jnp.log(total), lse)
        o_ref[:, cols] = jnp.where(low_lanes, parts[0], parts[1]).astype(BF16)
    lse_ref[0] = jnp.transpose(lse)[0:16, :]
    r1 = x0 + (dot_nn(o_ref[...], wo_ref[...]) + bo)
    center = r1 - mean_last(r1)
    rstd = lax.rsqrt(mean_last(center * center) + EPS)
    n1_ref[...] = center * rstd
    rstd_ref[...] = rstd


def gelu_parts(u):
    bell = jnp.exp(u * u * -0.5)
    t = 1.0 / (1.0 + (0.3275911 * 0.7071067811865476) * jnp.abs(u))
    poly = t * (
        0.5 * 0.254829592
        + t * (0.5 * -0.284496736 + t * (0.5 * 1.421413741 + t * (0.5 * -1.453152027 + t * (0.5 * 1.061405429))))
    )
    tail = poly * bell
    phi = jnp.where(u >= 0, 1.0 - tail, tail)
    return u * phi, phi + u * bell * 0.3989422804014327


def ffn_forward(
    place_ref, mine_ref, other_ref, n1_ref, cot_ref, vec_ref, b1_ref,
    out_ref, slope_ref, dz_ref, dr2_ref, dw2_ref, small_ref,
    hidden, acc, w1_ref, w2_ref, sem,
):
    step = pl.program_id(0)

    @pl.when(step == 0)
    def _():
        fetch_ffn(place_ref, mine_ref, other_ref, sem, w1_ref, w2_ref)

    g1, s1, g2, s2, b2 = (vec_ref[i : i + 1, :] for i in (3, 4, 6, 7, 8))
    y1 = g1 * n1_ref[...] + s1
    y1b = y1.astype(BF16)
    for c in range(FF // HID):
        cols = slice(c * HID, (c + 1) * HID)
        u = dot_nn(y1b, w1_ref[:, cols]) + b1_ref[0:1, cols]
        act, slope = gelu_parts(u)
        hidden[:, cols] = act.astype(BF16)
        slope_ref[:, cols] = slope.astype(BF16)
    r2 = y1 + (dot_nn(hidden[...], w2_ref[...]) + b2)
    center = r2 - mean_last(r2)
    rstd = lax.rsqrt(mean_last(center * center) + EPS)
    n2 = center * rstd
    out_ref[...] = (n2 * g2 + s2).astype(BF16)
    dy = cot_ref[...].astype(F32)
    e = dy * g2
    dr2 = (e - mean_last(e) - n2 * mean_last(e * n2)) * rstd
    dz = dr2.astype(BF16)
    dr2_ref[...] = dr2
    dz_ref[...] = dz

    @pl.when(step == 0)
    def _():
        small_ref[...] = jnp.zeros_like(small_ref)
        acc[...] = jnp.zeros_like(acc)

    small_ref[0:1, :] += rows_sum(dz.astype(F32))
    small_ref[1:2, :] += rows_sum(dy * n2)
    small_ref[2:3, :] += rows_sum(dy)
    acc[...] += dot_tn(hidden[...], dz)

    @pl.when(step == pl.num_programs(0) - 1)
    def _():
        dw2_ref[0:FF, :] = acc[...].astype(BF16)
        dw2_ref[FF:, :] = jnp.zeros((dw2_ref.shape[0] - FF, D), BF16)


def spread(target, first, count, grad):
    for block in range(target.shape[0]):
        low = block * count
        rows = max(0, min(count, D - low))
        if rows:
            target[block, first : first + rows, :] = grad(low, low + rows).astype(BF16)
        if rows < count:
            target[block, first + rows : first + count, :] = jnp.zeros((count - rows, D), BF16)


def ffn_backward(
    aplace_ref, fplace_ref, amine_ref, aother_ref, fmine_ref, fother_ref,
    n1_ref, rstd_ref, dz_ref, dr2_ref, slope_ref, o_ref, vec_ref,
    dr1_ref, do_ref, grads_ref, small_ref, db1_ref,
    grad_pre, acc1, acco, w1_ref, w2_ref, wo_ref, sem,
):
    step = pl.program_id(0)

    @pl.when(step == 0)
    def _():
        fetch_ffn(fplace_ref, fmine_ref, fother_ref, sem, w1_ref, w2_ref)
        fetch_attn(aplace_ref, amine_ref, aother_ref, sem, None, None, None, wo_ref)
        small_ref[...] = jnp.zeros_like(small_ref)
        db1_ref[...] = jnp.zeros_like(db1_ref)
        acc1[...] = jnp.zeros_like(acc1)
        acco[...] = jnp.zeros_like(acco)

    g1, s1 = vec_ref[3:4, :], vec_ref[4:5, :]
    n1 = n1_ref[...]
    y1b = (g1 * n1 + s1).astype(BF16)
    dz = dz_ref[...]
    for c in range(FF // HID):
        cols = slice(c * HID, (c + 1) * HID)
        du = (dot_nt(dz, w2_ref[cols, :]) * slope_ref[:, cols].astype(F32)).astype(BF16)
        grad_pre[:, cols] = du
        db1_ref[0:1, cols] += rows_sum(du.astype(F32))
    acc1[...] += dot_tn(y1b, grad_pre[...])
    dy1 = dot_nt(grad_pre[...], w1_ref[...]) + dr2_ref[...]
    e = dy1 * g1
    dr1 = (e - mean_last(e) - n1 * mean_last(e * n1)) * rstd_ref[...]
    dr1_ref[...] = dr1
    da = dr1.astype(BF16)
    small_ref[0:1, :] += rows_sum(da.astype(F32))
    small_ref[1:2, :] += rows_sum(dy1 * n1)
    small_ref[2:3, :] += rows_sum(dy1)
    acco[...] += dot_tn(o_ref[...], da)
    do_ref[...] = dot_nt(da, wo_ref[...]).astype(BF16)

    @pl.when(step == pl.num_programs(0) - 1)
    def _():
        count = grads_ref.shape[1] // 5
        for j in range(FF // D):
            spread(grads_ref, j * count, count, lambda low, high: acc1[low:high, j * D : (j + 1) * D])
        spread(grads_ref, 4 * count, count, lambda low, high: acco[low:high, :])


def attn_backward(
    first, starts_ref, frames_ref, vec_ref, q_ref, k_ref, v_ref, do_ref, lse_ref,
    dq_ref, dk_ref, dv_ref, grads_ref, small_ref,
    accq, acck, accv,
):
    step = pl.program_id(0)

    @pl.when(step == 0)
    def _():
        small_ref[...] = jnp.zeros_like(small_ref)
        accq[...] = jnp.zeros_like(accq)
        acck[...] = jnp.zeros_like(acck)
        accv[...] = jnp.zeros_like(accv)

    scale = HEAD_DIM ** (-0.5)
    low_lanes = lax.broadcasted_iota(jnp.int32, (FRAMES, PAIR), 1) < HEAD_DIM
    for pair in range(q_ref.shape[1] // PAIR):
        cols = slice(pair * PAIR, (pair + 1) * PAIR)
        qp, kp, vp, dop = q_ref[:, cols], k_ref[:, cols], v_ref[:, cols], do_ref[:, cols]
        parts = []
        for half in range(2):
            keep = low_lanes if half == 0 else jnp.logical_not(low_lanes)
            kh = jnp.where(keep, kp.astype(F32), 0.0).astype(BF16)
            vh = jnp.where(keep, vp.astype(F32), 0.0).astype(BF16)
            head = first + 2 * pair + half
            prob = jnp.exp(dot_nt(kh, qp) - lse_ref[0, head : head + 1, :])
            dprob = dot_nt(vh, dop)
            inner = jnp.sum(prob * dprob, axis=0, keepdims=True)
            dscore = (prob * (dprob - inner)).astype(BF16)
            parts.append((dot_nn(prob.astype(BF16), dop), dot_nn(dscore, qp), dot_tn(dscore, kp) * scale))
        for ref, one, two in zip((dv_ref, dk_ref, dq_ref), *parts):
            ref[:, cols] = jnp.where(low_lanes, one, two).astype(BF16)
    masked, x0 = masked_rows(frames_ref, starts_ref, vec_ref[5:6, :])
    h = x0.astype(BF16)
    accq[...] += dot_tn(h, dq_ref[...])
    acck[...] += dot_tn(h, dk_ref[...])
    accv[...] += dot_tn(h, dv_ref[...])
    small_ref[0:1, :] += rows_sum(dq_ref[...].astype(F32))
    small_ref[1:2, :] += rows_sum(dv_ref[...].astype(F32))

    @pl.when(step == pl.num_programs(0) - 1)
    def _():
        count = grads_ref.shape[1] // 3
        for j, acc in enumerate((accq, acck, accv)):
            spread(grads_ref, j * count, count, lambda low, high: acc[low:high, :])


def input_backward(
    place_ref, mine_ref, other_ref, starts_ref, dr1_ref, dq_ref, dk_ref, dv_ref,
    grad_ref, small_ref,
    wq_ref, wk_ref, wv_ref, sem,
):
    step = pl.program_id(0)

    @pl.when(step == 0)
    def _():
        fetch_attn(place_ref, mine_ref, other_ref, sem, wq_ref, wk_ref, wv_ref, None)
        small_ref[...] = jnp.zeros_like(small_ref)

    places = lax.broadcasted_iota(jnp.int32, (FRAMES, starts_ref.shape[-1]), 0)
    ahead = places - starts_ref[0]
    inside = jnp.where((ahead >= 0) & (ahead < SPAN), 1.0, 0.0)
    masked = jnp.max(inside, axis=1, keepdims=True) > 0.5
    dx0 = (
        dot_nt(dq_ref[...], wq_ref[...])
        + dot_nt(dk_ref[...], wk_ref[...])
        + dot_nt(dv_ref[...], wv_ref[...])
        + dr1_ref[...]
    )
    grad_ref[...] = jnp.where(masked, 0.0, dx0).astype(BF16)
    small_ref[0:1, :] += rows_sum(jnp.where(masked, dx0, 0.0))


def row_blocks(width):
    return pl.BlockSpec((FRAMES, width), lambda i: (i, 0))


def kept(rows, cols):
    return pl.BlockSpec((rows, cols), lambda i: (0, 0), pipeline_mode=pl.Buffered(1))


def held(rows, cols):
    return pl.BlockSpec((rows, cols), lambda i: (0, 0))


def held3(first, rows, cols):
    return pl.BlockSpec((first, rows, cols), lambda i: (0, 0, 0))


def shape(*sizes, dtype=BF16):
    return jax.ShapeDtypeStruct(sizes, dtype)


SCALARS = pl.BlockSpec(memory_space=pltpu.SMEM)
WHOLE = pl.BlockSpec(memory_space=pl.ANY)
COPIES = pltpu.SemaphoreType.DMA(())


def call(body, utters, in_specs, out_specs, out_shape, scratch=(), flops=0, moved=0, exps=0):
    return pl.pallas_call(
        body,
        grid=(utters,),
        in_specs=in_specs,
        out_specs=out_specs,
        out_shape=out_shape,
        scratch_shapes=list(scratch),
        compiler_params=pltpu.CompilerParams(
            dimension_semantics=("arbitrary",), vmem_limit_bytes=VMEM_LIMIT
        ),
        cost_estimate=pl.CostEstimate(
            flops=int(flops), bytes_accessed=int(moved), transcendentals=int(exps)
        ),
    )


def starts_spec(starts):
    return pl.BlockSpec((1, 1, starts.shape[-1]), lambda i: (i, 0, 0))


def lse_spec():
    return pl.BlockSpec((1, 16, FRAMES), lambda i: (i, 0, 0))


def weights(*sizes):
    return [pltpu.VMEM(size, BF16) for size in sizes] + [COPIES]


def run_attn_forward(place, attn, starts, frames, vec):
    rows = frames.shape[0]
    utters = rows // FRAMES
    return call(
        attn_forward, utters,
        [SCALARS, WHOLE, WHOLE, starts_spec(starts), row_blocks(D), kept(16, D)],
        [row_blocks(D)] * 4 + [lse_spec(), row_blocks(D), row_blocks(1)],
        [shape(rows, D)] * 4
        + [shape(utters, 16, FRAMES, dtype=F32), shape(rows, D, dtype=F32), shape(rows, 1, dtype=F32)],
        weights(*[(D, D)] * 4),
        flops=rows * D * D * 8 + rows * FRAMES * D * 16, moved=rows * D * 14,
    )(place, *attn, starts, frames, vec)


def run_ffn_forward(place, ffn, n1, cot, vec, b1, ff_rows):
    rows = n1.shape[0]
    return call(
        ffn_forward, rows // FRAMES,
        [SCALARS, WHOLE, WHOLE, row_blocks(D), row_blocks(D), kept(16, D), kept(8, FF)],
        [row_blocks(D), row_blocks(FF), row_blocks(D), row_blocks(D), held(ff_rows, D), held(8, D)],
        [shape(rows, D), shape(rows, FF), shape(rows, D), shape(rows, D, dtype=F32),
         shape(ff_rows, D), shape(8, D, dtype=F32)],
        [pltpu.VMEM((FRAMES, FF), BF16), pltpu.VMEM((FF, D), F32)] + weights((D, FF), (FF, D)),
        flops=rows * D * FF * 6, moved=rows * D * 40,
    )(place, *ffn, n1, cot, vec, b1)


def run_ffn_backward(attn_place, ffn_place, attn, ffn, n1, rstd, dz, dr2, slope, o, vec, blocks, count):
    rows = n1.shape[0]
    return call(
        ffn_backward, rows // FRAMES,
        [SCALARS] * 2 + [WHOLE] * 4
        + [row_blocks(D), row_blocks(1), row_blocks(D), row_blocks(D), row_blocks(FF), row_blocks(D), kept(16, D)],
        [row_blocks(D), row_blocks(D), held3(blocks, 5 * count, D), held(8, D), held(8, FF)],
        [shape(rows, D, dtype=F32), shape(rows, D), shape(blocks, 5 * count, D),
         shape(8, D, dtype=F32), shape(8, FF, dtype=F32)],
        [pltpu.VMEM((FRAMES, FF), BF16), pltpu.VMEM((D, FF), F32), pltpu.VMEM((D, D), F32)]
        + weights((D, FF), (FF, D), (D, D)),
        flops=rows * D * FF * 6 + rows * D * D * 4, moved=rows * D * 40,
    )(attn_place, ffn_place, *attn, *ffn, n1, rstd, dz, dr2, slope, o, vec)


def run_attn_backward(starts, frames, vec, q, k, v, do, lse, blocks, count):
    rows = frames.shape[0]
    utters = rows // FRAMES
    return call(
        functools.partial(attn_backward, 0), utters,
        [starts_spec(starts), row_blocks(D), kept(16, D)] + [row_blocks(D)] * 4 + [lse_spec()],
        [row_blocks(D)] * 3 + [held3(blocks, 3 * count, D), held(8, D)],
        [shape(rows, D)] * 3 + [shape(blocks, 3 * count, D), shape(8, D, dtype=F32)],
        [pltpu.VMEM((D, D), F32)] * 3,
        flops=rows * D * D * 6 + rows * FRAMES * D * 10, moved=rows * D * 10,
    )(starts, frames, vec, q, k, v, do, lse)


def run_input_backward(place, attn, starts, dr1, dq, dk, dv):
    rows = dr1.shape[0]
    return call(
        input_backward, rows // FRAMES,
        [SCALARS, WHOLE, WHOLE, starts_spec(starts)] + [row_blocks(D)] * 4,
        [row_blocks(D), held(8, D)],
        [shape(rows, D), shape(8, D, dtype=F32)],
        weights(*[(D, D)] * 3),
        flops=rows * D * D * 6, moved=rows * D * 12,
    )(place, *attn, starts, dr1, dq, dk, dv)


def in_order(value, order):
    return jnp.concatenate([lax.dynamic_slice_in_dim(value, order[i], 1) for i in range(value.shape[0])])


class Grid:
    def __init__(self, dp, fsdp):
        self.dp, self.fsdp = dp, fsdp
        self.dp_bits = [1 << i for i in range(dp.bit_length() - 1)]
        self.fsdp_bits = [1 << i for i in range(fsdp.bit_length() - 1)]

    def bit(self, axis, bit):
        return (lax.axis_index(axis) // bit) % 2

    def swap(self, value, dp_mask, fsdp_mask):
        if not dp_mask:
            return lax.ppermute(value, "fsdp", [(i, i ^ fsdp_mask) for i in range(self.fsdp)])
        if not fsdp_mask:
            return lax.ppermute(value, "dp", [(i, i ^ dp_mask) for i in range(self.dp)])
        pairs = [
            (i * self.fsdp + j, (i ^ dp_mask) * self.fsdp + (j ^ fsdp_mask))
            for i in range(self.dp)
            for j in range(self.fsdp)
        ]
        return lax.ppermute(value, ("dp", "fsdp"), pairs)

    def gather(self, piece):
        gathered = piece[None]
        for bit in reversed(self.fsdp_bits):
            gathered = jnp.concatenate([gathered, self.swap(gathered, 0, bit)])
        return gathered

    def places(self):
        me = lax.axis_index("fsdp")
        code = me ^ jnp.arange(self.fsdp, dtype=jnp.int32)
        place = jnp.zeros_like(code)
        for step, bit in enumerate(reversed(self.fsdp_bits)):
            place = place + ((code // bit) % 2) * (1 << step)
        return place

    def stages(self):
        dp_left, fsdp_left = self.dp_bits[1:], list(self.fsdp_bits)
        order = [[("dp", 1)]]
        while dp_left and fsdp_left:
            order.append([("dp", dp_left.pop(0)), ("fsdp", fsdp_left.pop(0))])
        order += [[("dp", bit)] for bit in dp_left]
        while fsdp_left:
            order.append([("fsdp", bit) for bit in fsdp_left[:2]])
            fsdp_left = fsdp_left[2:]
        return order

    def reduce(self, grads):
        rows, width = grads.shape[1:]
        left = list(reversed(self.fsdp_bits))
        value = grads.reshape((2,) * len(left) + (rows, width))
        halved = []
        for stage in self.stages():
            for axis, bit in stage:
                if axis == "dp":
                    value = value.reshape(value.shape[:-2] + (2, value.shape[-2] // 2, width))
                    halved.append(bit)
            spots = {}
            extra = len(left)
            for axis, bit in stage:
                if axis == "dp":
                    spots[(axis, bit)] = extra
                    extra += 1
                else:
                    spots[(axis, bit)] = left.index(bit)
            total = None
            for code in range(1 << len(stage)):
                starts = [0] * value.ndim
                sizes = list(value.shape)
                masks = {"dp": 0, "fsdp": 0}
                for place, (axis, bit) in enumerate(stage):
                    other = (code >> place) & 1
                    starts[spots[(axis, bit)]] = self.bit(axis, bit) ^ other
                    sizes[spots[(axis, bit)]] = 1
                    masks[axis] += bit * other
                part = lax.dynamic_slice(value, starts, sizes)
                if code:
                    part = self.swap(part, masks["dp"], masks["fsdp"])
                part = part.astype(F32)
                total = part if total is None else total + part
            total = jnp.squeeze(total, tuple(spots.values()))
            left = [bit for bit in left if ("fsdp", bit) not in spots]
            value = total.astype(BF16)
        for bit in reversed(halved):
            other = self.swap(value, bit, 0)
            first = self.bit("dp", bit) == 0
            value = jnp.concatenate([jnp.where(first, value, other), jnp.where(first, other, value)])
        return value.astype(F32)

    def total(self, value):
        for bit in self.dp_bits:
            value = value + self.swap(value, bit, 0)
        for bit in self.fsdp_bits:
            value = value + self.swap(value, 0, bit)
        return value


def on_device(
    sizes, frames, cotangent, span_starts, query_weight, key_weight, value_weight, out_weight,
    query_bias, value_bias, out_bias, first_gain, first_shift, up_weight, up_bias, down_weight,
    down_bias, second_gain, second_shift, mask_vector,
):
    grid = Grid(*sizes)
    owners = grid.fsdp
    count = query_weight.shape[0]
    wide = down_weight.shape[0]
    d_max = count * owners
    core = lax.axis_index("dp") % 2
    direct = count % 16 == 0

    vectors = [query_bias, value_bias, out_bias, first_gain, first_shift, mask_vector,
               second_gain, second_shift, down_bias]
    packed = jnp.concatenate(vectors + [up_bias]).reshape(1, -1)
    attn_half = jnp.where(
        core == 0,
        jnp.concatenate([query_weight[:, :D], key_weight[:, :D]]),
        jnp.concatenate([value_weight[:, :D], out_weight[:, :D]]),
    )
    ffn_half = jnp.where(
        core == 0,
        jnp.concatenate([up_weight[:, j * D : (j + 1) * D] for j in range(FF // D)]),
        down_weight[:, :D],
    )
    packed_all = grid.gather(packed)
    attn_mine = grid.gather(attn_half)
    attn_other = grid.swap(attn_mine, 1, 0)
    ffn_mine = lax.all_gather(ffn_half, "fsdp", axis=0, tiled=False)
    ffn_other = grid.swap(ffn_mine, 1, 0)

    places = grid.places()
    packed_all = in_order(packed_all[:, 0], places)
    vec = packed_all[:, : len(vectors) * count].reshape(owners, len(vectors), count)
    vec = jnp.swapaxes(vec, 0, 1).reshape(len(vectors), d_max)[:, :D].astype(F32)
    vec = jnp.pad(vec, ((0, 16 - len(vectors)), (0, 0)))
    b1 = packed_all[:, len(vectors) * count :].reshape(1, -1)[:, :FF].astype(F32)
    b1 = jnp.broadcast_to(b1, (8, FF))

    if direct:
        attn = (attn_mine, attn_other)
        ffn = (ffn_mine, ffn_other)
        attn_place = jnp.concatenate([core[None], places])
        ffn_place = jnp.concatenate([core[None], jnp.arange(owners, dtype=jnp.int32)])
        blocks, block = owners, count
    else:
        def whole(value, split, order):
            value = (value if order is None else in_order(value, order)).reshape(owners, split, -1, D)
            return jnp.swapaxes(value, 0, 1).reshape(1, -1, D)

        attn = (whole(attn_mine, 2, places), whole(attn_other, 2, places))
        first = core == 0
        up_all = whole(jnp.where(first, ffn_mine, ffn_other), FF // D, None)
        down_all = whole(jnp.where(first, ffn_other, ffn_mine), 1, None)
        ffn = (jnp.where(first, up_all, down_all), jnp.where(first, down_all, up_all))
        attn_place = ffn_place = jnp.stack([core, jnp.zeros_like(core)])
        blocks, block = 1, d_max

    def owner_rows(grads, split):
        if direct:
            return grads
        grads = grads.reshape(split, owners, -1, D)
        return jnp.swapaxes(grads, 0, 1).reshape(owners, -1, D)

    starts = span_starts[:, None, :]
    q, k, v, o, lse, n1, rstd = run_attn_forward(attn_place, attn, starts, frames, vec)
    output, slope, dz, dr2, down_grad, small2 = run_ffn_forward(
        ffn_place, ffn, n1, cotangent, vec, b1, wide * owners
    )
    dr1, do, up_out_grads, small1, up_bias_grad = run_ffn_backward(
        attn_place, ffn_place, attn, ffn, n1, rstd, dz, dr2, slope, o, vec, blocks, block
    )
    dq, dk, dv, qkv_grads, small_a = run_attn_backward(
        starts, frames, vec, q, k, v, do, lse, blocks, block
    )
    frames_grad, small_m = run_input_backward(attn_place, attn, starts, dr1, dq, dk, dv)

    small = jnp.concatenate(
        [small_a[0:2], small1[0:3], small_m[0:1], small2[1:3], small2[0:1],
         up_bias_grad[0].reshape(FF // D, D), jnp.zeros((3, D), F32)]
    )
    down_sum = grid.reduce(down_grad.reshape(owners, wide, D))
    up_out_sum = grid.reduce(owner_rows(up_out_grads, 5))
    qkv_sum = grid.reduce(owner_rows(qkv_grads, 3))
    small = grid.total(small)

    def wide_rows(value):
        return jnp.pad(value, ((0, 0), (0, d_max - D)))

    me = lax.axis_index("fsdp")
    rows = jnp.pad(small[: len(vectors)], ((0, 0), (0, d_max - D)))
    rows = lax.dynamic_slice(rows, (0, me * count), (len(vectors), count))
    names = ("qb", "vb", "ob", "g1", "s1", "m", "g2", "s2", "b2")
    vec_grads = {name: rows[i] for i, name in enumerate(names)}
    b1_grad = jnp.pad(small[len(vectors) : len(vectors) + FF // D].reshape(-1), (0, wide * owners - FF))
    b1_grad = lax.dynamic_slice(b1_grad, (me * wide,), (wide,))
    up_grad = jnp.concatenate(
        [up_out_sum[j * count : (j + 1) * count] for j in range(FF // D)]
        + [jnp.zeros((count, up_weight.shape[1] - FF), F32)],
        axis=1,
    )
    return (
        output,
        frames_grad,
        wide_rows(qkv_sum[:count]),
        wide_rows(qkv_sum[count : 2 * count]),
        wide_rows(qkv_sum[2 * count :]),
        wide_rows(up_out_sum[4 * count :]),
        vec_grads["qb"],
        vec_grads["vb"],
        vec_grads["ob"],
        vec_grads["g1"],
        vec_grads["s1"],
        up_grad,
        b1_grad,
        wide_rows(down_sum),
        vec_grads["b2"],
        vec_grads["g2"],
        vec_grads["s2"],
        vec_grads["m"],
    )


def solution(mesh):
    sizes = (mesh.shape["dp"], mesh.shape["fsdp"])
    tokens = P(("dp", "fsdp"), None)
    matrix, vector = P("fsdp", None), P("fsdp")
    return jax.shard_map(
        functools.partial(on_device, sizes),
        mesh=mesh,
        in_specs=(tokens,) * 3 + (matrix,) * 4 + (vector,) * 5 + (matrix, vector, matrix) + (vector,) * 4,
        out_specs=(tokens,) * 2 + (matrix,) * 4 + (vector,) * 5 + (matrix, vector, matrix) + (vector,) * 4,
        check_vma=False,
    )
```

```python
import functools
import jax
import jax.numpy as jnp
from jax import lax
from jax.experimental import pallas as pl
from jax.experimental.pallas import tpu as pltpu
from jax.sharding import PartitionSpec as P

HEADS = 10
HEAD_DIM = 64
FF = 2560
D = 640
FRAMES = 400
SPAN = 10
PAIR = 2 * HEAD_DIM
FIRST_PAIRS = 3
EPS = 1e-05
F32 = jnp.float32
BF16 = jnp.bfloat16
VMEM_LIMIT = 60 * 1024 * 1024
HID = 512


def dot_nn(a, b):
    return lax.dot_general(a, b, (((1,), (0,)), ((), ())), preferred_element_type=F32)


def dot_nt(a, b):
    return lax.dot_general(a, b, (((1,), (1,)), ((), ())), preferred_element_type=F32)


def dot_tn(a, b):
    return lax.dot_general(a, b, (((0,), (0,)), ((), ())), preferred_element_type=F32)


def mean_last(a):
    return jnp.mean(a, axis=-1, keepdims=True)


def rows_sum(a):
    return jnp.sum(a, axis=0, keepdims=True)


def masked_frames(starts_ref):
    places = lax.broadcasted_iota(jnp.int32, (FRAMES, starts_ref.shape[-1]), 0)
    ahead = places - starts_ref[0]
    inside = jnp.where((ahead >= 0) & (ahead < SPAN), 1.0, 0.0)
    return jnp.max(inside, axis=1, keepdims=True) > 0.5


def fetch(place_ref, sem, *wanted):
    def copies(arrays, role, parts):
        for group, source in enumerate(arrays):
            for piece in range(source.shape[0]):
                owner = place_ref[1] ^ (piece * len(arrays) + group)
                for core, first, rows, stride, row, column, target in parts:
                    if core == role:
                        low = pl.multiple_of(owner * stride + row, 16)
                        yield pltpu.make_async_copy(
                            source.at[piece, pl.ds(first, rows), :],
                            target.at[pl.ds(low, rows), pl.ds(column, D)],
                            sem,
                        )

    for core in (0, 1):

        @pl.when(place_ref[0] == core)
        def _(core=core):
            started = []
            for (mine, other), parts in wanted:
                started += list(copies(mine, core, parts)) + list(copies(other, 1 - core, parts))
            for copy in started:
                copy.start()
            for copy in started:
                copy.wait()


def attn_parts(one, two, rows):
    parts = [(0, 0, rows, rows, 0, 0, one), (1, 0, rows, rows, 0, 0, two)]
    return [part for part in parts if part[-1] is not None]


def up_parts(target, rows):
    return [(j // 2, (j % 2) * rows, rows, rows, 0, j * D, target) for j in range(FF // D)]


def down_parts(target, rows):
    return [(core, 0, rows // 2, rows, core * (rows // 2), 0, target) for core in (0, 1)]


def attn_forward(
    place_ref, one, two, starts_ref, frames_ref, vec_ref,
    q_ref, k_ref, v_ref, o_ref, lse_ref, n1_ref, rstd_ref,
    wq_ref, wk_ref, wv_ref, wo_ref, sem, *, rows,
):
    @pl.when(pl.program_id(0) == 0)
    def _():
        fetch(
            place_ref, sem,
            (one, attn_parts(wq_ref, wk_ref, rows)), (two, attn_parts(wv_ref, wo_ref, rows)),
        )

    bq, bv, bo = vec_ref[0:1, :], vec_ref[1:2, :], vec_ref[2:3, :]
    x0 = jnp.where(masked_frames(starts_ref), vec_ref[5:6, :], frames_ref[...].astype(F32))
    h = x0.astype(BF16)
    scale = HEAD_DIM ** (-0.5)
    q_ref[...] = ((dot_nn(h, wq_ref[0:D, :]) + bq).astype(BF16).astype(F32) * scale).astype(BF16)
    k_ref[...] = dot_nn(h, wk_ref[0:D, :]).astype(BF16)
    v_ref[...] = (dot_nn(h, wv_ref[0:D, :]) + bv).astype(BF16)
    low_lanes = lax.broadcasted_iota(jnp.int32, (FRAMES, PAIR), 1) < HEAD_DIM
    lanes = lax.broadcasted_iota(jnp.int32, (FRAMES, 128), 1)
    lse = jnp.zeros((FRAMES, 128), F32)
    for pair in range(HEADS // 2):
        cols = slice(pair * PAIR, (pair + 1) * PAIR)
        qp, kp, vp = q_ref[:, cols], k_ref[:, cols], v_ref[:, cols]
        parts = []
        for half in range(2):
            keep = low_lanes if half == 0 else jnp.logical_not(low_lanes)
            qh = jnp.where(keep, qp.astype(F32), 0.0).astype(BF16)
            scores = dot_nt(qh, kp)
            top = jnp.max(scores, axis=-1, keepdims=True)
            expo = jnp.exp(scores - top)
            total = jnp.sum(expo, axis=-1, keepdims=True)
            parts.append(dot_nn(expo.astype(BF16), vp) * (1.0 / total))
            lse = jnp.where(lanes == 2 * pair + half, top + jnp.log(total), lse)
        o_ref[:, cols] = jnp.where(low_lanes, parts[0], parts[1]).astype(BF16)
    lse_ref[0] = jnp.transpose(lse)[0:16, :]
    r1 = x0 + (dot_nn(o_ref[...], wo_ref[0:D, :]) + bo)
    center = r1 - mean_last(r1)
    rstd = lax.rsqrt(mean_last(center * center) + EPS)
    n1_ref[...] = center * rstd
    rstd_ref[...] = rstd


def gelu_parts(u):
    bell = jnp.exp(u * u * -0.5)
    t = 1.0 / (1.0 + (0.3275911 * 0.7071067811865476) * jnp.abs(u))
    poly = t * (
        0.5 * 0.254829592
        + t * (0.5 * -0.284496736 + t * (0.5 * 1.421413741 + t * (0.5 * -1.453152027 + t * (0.5 * 1.061405429))))
    )
    tail = poly * bell
    phi = jnp.where(u >= 0, 1.0 - tail, tail)
    return u * phi, phi + u * bell * 0.3989422804014327


def ffn_up(place_ref, up, n1_ref, vec_ref, b1_ref, hidden_ref, slope_ref, w1_ref, sem, *, rows):
    @pl.when(pl.program_id(0) == 0)
    def _():
        fetch(place_ref, sem, (up, up_parts(w1_ref, rows)))

    y1b = (vec_ref[3:4, :] * n1_ref[...] + vec_ref[4:5, :]).astype(BF16)
    for c in range(FF // HID):
        cols = slice(c * HID, (c + 1) * HID)
        u = dot_nn(y1b, w1_ref[0:D, cols]) + b1_ref[0:1, cols]
        act, slope = gelu_parts(u)
        hidden_ref[:, cols] = act.astype(BF16)
        slope_ref[:, cols] = slope.astype(BF16)


def ffn_down(
    place_ref, down, n1_ref, hidden_ref, cot_ref, vec_ref,
    out_ref, dz_ref, dr2_ref, small_ref, *rest, rows, halves,
):
    grads_refs, (acc, w2_ref, sem) = rest[:-3], rest[-3:]
    step = pl.program_id(0)

    @pl.when(step == 0)
    def _():
        small_ref[...] = jnp.zeros_like(small_ref)
        acc[...] = jnp.zeros_like(acc)
        fetch(place_ref, sem, (down, down_parts(w2_ref, rows)))

    g1, s1, g2, s2, b2 = (vec_ref[i : i + 1, :] for i in (3, 4, 6, 7, 8))
    y1 = g1 * n1_ref[...] + s1
    r2 = y1 + (dot_nn(hidden_ref[...], w2_ref[0:FF, :]) + b2)
    center = r2 - mean_last(r2)
    rstd = lax.rsqrt(mean_last(center * center) + EPS)
    n2 = center * rstd
    out_ref[...] = (n2 * g2 + s2).astype(BF16)
    dy = cot_ref[...].astype(F32)
    e = dy * g2
    dr2 = (e - mean_last(e) - n2 * mean_last(e * n2)) * rstd
    dz = dr2.astype(BF16)
    dr2_ref[...] = dr2
    dz_ref[...] = dz
    small_ref[0:1, :] += rows_sum(dz.astype(F32))
    small_ref[1:2, :] += rows_sum(dy * n2)
    small_ref[2:3, :] += rows_sum(dy)
    acc[0:FF, :] += dot_tn(hidden_ref[...], dz)

    @pl.when(step == pl.num_programs(0) - 1)
    def _():
        deliver(place_ref, grads_refs, [(acc, 0, rows)], halves)


def deliver(place_ref, refs, sources, halves):
    if not halves:
        for ref, (acc, column, _) in zip(refs, sources):
            ref[...] = acc[:, column : column + ref.shape[1]].astype(BF16)
        return
    for ref, core in zip(refs, (place_ref[0], 1 - place_ref[0])):
        owners, parts, _, width = ref.shape
        for owner in range(owners):
            for part in range(parts):
                pieces = []
                for acc, column, rows in sources:
                    size = rows // 4
                    low = pl.multiple_of(owner * rows + (2 * core + part) * size, 8)
                    pieces.append(acc[pl.ds(low, size), column : column + width])
                ref[owner, part] = jnp.concatenate(pieces, axis=0).astype(BF16)


def ffn_backward(
    place_ref, two, up, down, n1_ref, rstd_ref, dz_ref, dr2_ref, slope_ref, o_ref, vec_ref,
    dr1_ref, do_ref, small_ref, db1_ref, *rest, rows, halves,
):
    grads_refs = rest[:-7]
    grad_pre, acc1, acco, w1_ref, w2_ref, wo_ref, sem = rest[-7:]
    step = pl.program_id(0)

    @pl.when(step == 0)
    def _():
        small_ref[...] = jnp.zeros_like(small_ref)
        db1_ref[...] = jnp.zeros_like(db1_ref)
        acc1[...] = jnp.zeros_like(acc1)
        acco[...] = jnp.zeros_like(acco)
        fetch(
            place_ref, sem,
            (two, attn_parts(None, wo_ref, rows[0])), (up, up_parts(w1_ref, rows[0])), (down, down_parts(w2_ref, rows[1])),
        )

    g1, s1 = vec_ref[3:4, :], vec_ref[4:5, :]
    n1 = n1_ref[...]
    y1b = (g1 * n1 + s1).astype(BF16)
    dz = dz_ref[...]
    for c in range(FF // HID):
        cols = slice(c * HID, (c + 1) * HID)
        du = (dot_nt(dz, w2_ref[cols, :]) * slope_ref[:, cols].astype(F32)).astype(BF16)
        grad_pre[:, cols] = du
        db1_ref[0:1, cols] += rows_sum(du.astype(F32))
    acc1[0:D, :] += dot_tn(y1b, grad_pre[...])
    dy1 = dot_nt(grad_pre[...], w1_ref[0:D, :]) + dr2_ref[...]
    e = dy1 * g1
    dr1 = (e - mean_last(e) - n1 * mean_last(e * n1)) * rstd_ref[...]
    dr1_ref[...] = dr1
    da = dr1.astype(BF16)
    small_ref[0:1, :] += rows_sum(da.astype(F32))
    small_ref[1:2, :] += rows_sum(dy1 * n1)
    small_ref[2:3, :] += rows_sum(dy1)
    acco[0:D, :] += dot_tn(o_ref[...], da)
    do_ref[...] = dot_nt(da, wo_ref[0:D, :]).astype(BF16)

    @pl.when(step == pl.num_programs(0) - 1)
    def _():
        sources = [(acc1, j * D, rows[0]) for j in range(FF // D)] + [(acco, 0, rows[0])]
        deliver(place_ref, grads_refs, sources, halves)


def attn_backward(
    place_ref, starts_ref, frames_ref, vec_ref, q_ref, k_ref, v_ref, do_ref, lse_ref,
    dq_ref, dk_ref, dv_ref, small_ref, *rest, first, rows, halves,
):
    grads_refs, (accq, acck, accv) = rest[:-3], rest[-3:]
    step = pl.program_id(0)

    @pl.when(step == 0)
    def _():
        small_ref[...] = jnp.zeros_like(small_ref)
        accq[...] = jnp.zeros_like(accq)
        acck[...] = jnp.zeros_like(acck)
        accv[...] = jnp.zeros_like(accv)

    scale = HEAD_DIM ** (-0.5)
    low_lanes = lax.broadcasted_iota(jnp.int32, (FRAMES, PAIR), 1) < HEAD_DIM
    for pair in range(dq_ref.shape[1] // PAIR):
        source = slice((first + pair) * PAIR, (first + pair + 1) * PAIR)
        cols = slice(pair * PAIR, (pair + 1) * PAIR)
        qp, kp, vp, dop = q_ref[:, source], k_ref[:, source], v_ref[:, source], do_ref[:, source]
        parts = []
        for half in range(2):
            keep = low_lanes if half == 0 else jnp.logical_not(low_lanes)
            kh = jnp.where(keep, kp.astype(F32), 0.0).astype(BF16)
            vh = jnp.where(keep, vp.astype(F32), 0.0).astype(BF16)
            head = 2 * (first + pair) + half
            prob = jnp.exp(dot_nt(kh, qp) - lse_ref[0, head : head + 1, :])
            dprob = dot_nt(vh, dop)
            inner = jnp.sum(prob * dprob, axis=0, keepdims=True)
            dscore = (prob * (dprob - inner)).astype(BF16)
            parts.append((dot_nn(prob.astype(BF16), dop), dot_nn(dscore, qp), dot_tn(dscore, kp) * scale))
        for ref, one, two in zip((dv_ref, dk_ref, dq_ref), *parts):
            ref[:, cols] = jnp.where(low_lanes, one, two).astype(BF16)
    x0 = jnp.where(masked_frames(starts_ref), vec_ref[5:6, :], frames_ref[...].astype(F32))
    h = x0.astype(BF16)
    accq[0:D, :] += dot_tn(h, dq_ref[...])
    acck[0:D, :] += dot_tn(h, dk_ref[...])
    accv[0:D, :] += dot_tn(h, dv_ref[...])
    small_ref[0:1, :] += rows_sum(dq_ref[...].astype(F32))
    small_ref[1:2, :] += rows_sum(dv_ref[...].astype(F32))

    @pl.when(step == pl.num_programs(0) - 1)
    def _():
        deliver(place_ref, grads_refs, [(acc, 0, rows) for acc in (accq, acck, accv)], halves)


def input_backward(
    place_ref, one, two, starts_ref, dr1_ref, *rest, rows,
):
    parts, (grad_ref, small_ref, wq_ref, wk_ref, wv_ref, sem) = rest[:-6], rest[-6:]

    @pl.when(pl.program_id(0) == 0)
    def _():
        small_ref[...] = jnp.zeros_like(small_ref)
        fetch(
            place_ref, sem,
            (one, attn_parts(wq_ref, wk_ref, rows)), (two, attn_parts(wv_ref, None, rows)),
        )

    masked = masked_frames(starts_ref)
    dx0 = dr1_ref[...]
    column = 0
    for group in range(0, len(parts), 3):
        width = parts[group].shape[1]
        for grad, weight in zip(parts[group : group + 3], (wq_ref, wk_ref, wv_ref)):
            dx0 += dot_nt(grad[...], weight[0:D, column : column + width])
        column += width
    grad_ref[...] = jnp.where(masked, 0.0, dx0).astype(BF16)
    small_ref[0:1, :] += rows_sum(jnp.where(masked, dx0, 0.0))


def row_blocks(width):
    return pl.BlockSpec((FRAMES, width), lambda i, *_: (i, 0))


def kept(rows, cols):
    return pl.BlockSpec((rows, cols), lambda i, *_: (0, 0), pipeline_mode=pl.Buffered(1))


def held(*sizes):
    return pl.BlockSpec(sizes, lambda i, *_: (0,) * len(sizes))


def shape(*sizes, dtype=BF16):
    return jax.ShapeDtypeStruct(sizes, dtype)


SCALARS = pl.BlockSpec(memory_space=pltpu.SMEM)
WHOLE = pl.BlockSpec(memory_space=pl.ANY)
COPIES = pltpu.SemaphoreType.DMA(())


def call(body, steps, place, units, operands, in_specs, outputs, scratch=(), after=(), flops=0, moved=0):
    flat = [array for unit in units for arrays in unit for array in arrays]

    def kernel(place_ref, *refs):
        refs = refs[len(after) :]
        given = []
        for mine, other in units:
            given.append((refs[: len(mine)], refs[len(mine) : len(mine) + len(other)]))
            refs = refs[len(mine) + len(other) :]
        body(place_ref, *given, *refs)

    return pl.pallas_call(
        kernel,
        grid=(steps,),
        in_specs=[SCALARS] + [WHOLE] * (len(after) + len(flat)) + in_specs,
        out_specs=[spec for spec, _ in outputs],
        out_shape=[out for _, out in outputs],
        scratch_shapes=list(scratch),
        compiler_params=pltpu.CompilerParams(
            dimension_semantics=("arbitrary",), vmem_limit_bytes=VMEM_LIMIT
        ),
        cost_estimate=pl.CostEstimate(flops=int(flops), bytes_accessed=int(moved), transcendentals=0),
    )(place, *after, *flat, *operands)


def starts_spec(starts):
    return pl.BlockSpec((1, 1, starts.shape[-1]), lambda i: (i, 0, 0))


def lse_spec():
    return pl.BlockSpec((1, 16, FRAMES), lambda i: (i, 0, 0))


def weights(*sizes):
    return [pltpu.VMEM(size, BF16) for size in sizes] + [COPIES]


def by_rows(rows, width, dtype=BF16):
    return (row_blocks(width), shape(rows, width, dtype=dtype))


def summed(rows, width):
    return (held(rows, width), shape(rows, width, dtype=F32))


def grads_out(halves, sources):
    if not halves:
        return [(held(rows, width), shape(rows, width)) for rows, width, _ in sources]
    rows, width, count = sources[0]
    sizes = (rows // count, 2, sum(part[2] for part in sources) // 4, width)
    return [(held(*sizes), shape(*sizes))] * 2


class Layer:
    def __init__(self, place, starts, frames, vec, b1, d_rows, ff_rows, d_max, ff_max, halves):
        self.place, self.starts, self.frames, self.vec, self.b1 = place, starts, frames, vec, b1
        self.d_rows, self.ff_rows, self.d_max, self.ff_max, self.halves = d_rows, ff_rows, d_max, ff_max, halves
        self.rows = frames.shape[0]
        self.steps = self.rows // FRAMES

    def attn_forward(self, one, two, after=()):
        rows = self.rows
        return call(
            functools.partial(attn_forward, rows=self.d_rows), self.steps, self.place, (one, two),
            (self.starts, self.frames, self.vec), [starts_spec(self.starts), row_blocks(D), kept(16, D)],
            [by_rows(rows, D)] * 4
            + [(lse_spec(), shape(self.steps, 16, FRAMES, dtype=F32)), by_rows(rows, D, F32), by_rows(rows, 1, F32)],
            weights(*[(self.d_max, D)] * 4), after,
            flops=rows * D * D * 8 + rows * FRAMES * D * 16, moved=rows * D * 14,
        )

    def ffn_up(self, up, n1, after=()):
        rows = self.rows
        return call(
            functools.partial(ffn_up, rows=self.d_rows), self.steps, self.place, (up,),
            (n1, self.vec, self.b1), [row_blocks(D), kept(16, D), kept(8, FF)],
            [by_rows(rows, FF)] * 2, weights((self.d_max, FF)), after,
            flops=rows * D * FF * 4, moved=rows * FF * 6,
        )

    def ffn_down(self, down, n1, hidden, cotangent, halves, after=()):
        rows = self.rows
        return call(
            functools.partial(ffn_down, rows=self.ff_rows, halves=halves), self.steps, self.place, (down,),
            (n1, hidden, cotangent, self.vec), [row_blocks(D), row_blocks(FF), row_blocks(D), kept(16, D)],
            [by_rows(rows, D), by_rows(rows, D), by_rows(rows, D, F32), summed(8, D)]
            + grads_out(halves, [(self.ff_max, D, self.ff_rows)]),
            [pltpu.VMEM((self.ff_max, D), F32)] + weights((self.ff_max, D)), after,
            flops=rows * D * FF * 6, moved=rows * FF * 8,
        )

    def ffn_backward(self, two, up, down, n1, rstd, dz, dr2, slope, o, after=()):
        rows = self.rows
        return call(
            functools.partial(ffn_backward, rows=(self.d_rows, self.ff_rows), halves=self.halves),
            self.steps, self.place, (two, up, down), (n1, rstd, dz, dr2, slope, o, self.vec),
            [row_blocks(w) for w in (D, 1, D, D, FF, D)] + [kept(16, D)],
            [by_rows(rows, D, F32), by_rows(rows, D), summed(8, D), summed(8, FF)]
            + grads_out(
                self.halves,
                [(self.d_max, D, self.d_rows)] * 5,
            ),
            [pltpu.VMEM((FRAMES, FF), BF16), pltpu.VMEM((self.d_max, FF), F32), pltpu.VMEM((self.d_max, D), F32)]
            + weights((self.d_max, FF), (self.ff_max, D), (self.d_max, D)), after,
            flops=rows * D * FF * 8 + rows * D * D * 4, moved=rows * FF * 8,
        )

    def attn_backward(self, first, pairs, q, k, v, do, lse, after=()):
        rows, width = self.rows, pairs * PAIR
        return call(
            functools.partial(attn_backward, first=first, rows=self.d_rows, halves=self.halves),
            self.steps, self.place, (), (self.starts, self.frames, self.vec, q, k, v, do, lse),
            [starts_spec(self.starts), row_blocks(D), kept(16, D)] + [row_blocks(D)] * 4 + [lse_spec()],
            [by_rows(rows, width)] * 3 + [summed(8, width)]
            + grads_out(self.halves, [(self.d_max, width, self.d_rows)] * 3),
            [pltpu.VMEM((self.d_max, width), F32)] * 3, after,
            flops=rows * D * width * 6 + rows * FRAMES * width * 40, moved=rows * D * 10,
        )

    def input_backward(self, one, two, dr1, parts, after=()):
        rows = self.rows
        return call(
            functools.partial(input_backward, rows=self.d_rows), self.steps, self.place, (one, two),
            (self.starts, dr1, *parts),
            [starts_spec(self.starts), row_blocks(D)] + [row_blocks(part.shape[1]) for part in parts],
            [by_rows(rows, D), summed(8, D)], weights(*[(self.d_max, D)] * 3), after,
            flops=rows * D * D * 8, moved=rows * D * 12,
        )


def local(kernel, outputs, place, operands, scratch=(), cost=0):
    count = len(operands)

    def body(place_ref, *refs):
        sources, outs = refs[:count], refs[count : count + len(outputs)]
        held_refs, sems = refs[count + len(outputs) : -1], refs[-1]
        copies = [
            pltpu.make_async_copy(source, target, sems.at[i])
            for i, (source, target) in enumerate(zip(sources, held_refs))
        ]
        for copy in copies:
            copy.start()
        for copy in copies:
            copy.wait()
        kernel(place_ref, held_refs, outs)

    vmem = pl.BlockSpec(memory_space=pltpu.VMEM)
    return pl.pallas_call(
        body,
        in_specs=[SCALARS] + [WHOLE] * count,
        out_specs=[vmem] * len(outputs),
        out_shape=outputs,
        scratch_shapes=[pltpu.VMEM(array.shape, array.dtype) for array in operands]
        + [pltpu.SemaphoreType.DMA((count,))],
        compiler_params=pltpu.CompilerParams(vmem_limit_bytes=VMEM_LIMIT),
        cost_estimate=pl.CostEstimate(flops=1000, bytes_accessed=4 * sum(a.size for a in operands), transcendentals=0),
    )(place, *operands)


def first_sums(place, kept_half, received):
    owners, _, rows, width = kept_half.shape

    def kernel(place_ref, refs, outs):
        for j in range(4):
            for z in range(owners // 2):
                owner, part = 2 * z + ((place_ref[1] % 2) ^ (j // 2)), place_ref[2] ^ (j % 2)
                outs[j][z] = (refs[0][owner, part].astype(F32) + refs[1][owner, part].astype(F32)).astype(BF16)

    return local(kernel, [shape(owners // 2, rows, width)] * 4, place, [kept_half, received])


def next_sums(place, parts, split):
    rows, width = parts[0].shape[-2:]

    def kernel(place_ref, refs, outs):
        for j, out in enumerate(outs):
            pick = (lambda ref, j=j: ref[(place_ref[1] // 2) ^ j]) if split else (lambda ref: ref[...])
            total = pick(refs[0]).astype(F32)
            for ref in refs[1:]:
                total = total + pick(ref).astype(F32)
            out[...] = total.astype(BF16)

    return local(kernel, [shape(rows, width)] * (4 if split else 1), place, parts)


def finish(place, groups, outputs):
    def kernel(place_ref, refs, outs):
        for ref in outs:
            ref[:, D:] = jnp.zeros((ref.shape[0], ref.shape[1] - D), F32)
        for index in range(len(groups)):
            for j in range(4):
                value = refs[4 * index + j][...].astype(F32)
                quarter = 2 * (place_ref[0] ^ (j // 2)) + (place_ref[2] ^ (j % 2))
                for ref, (rows, _, sources) in zip(outs, outputs):
                    size = rows // 4
                    for source, weight, column in sources:
                        if source == index:
                            ref[pl.ds(pl.multiple_of(quarter * size, 8), size), column : column + value.shape[1]] = (
                                value[weight * size : (weight + 1) * size]
                            )

    return local(
        kernel, [shape(rows, cols, dtype=F32) for rows, cols, _ in outputs], place,
        [array for group in groups for array in group],
    )


def unpack(place, stacks, first, count, wide, names):
    owners = 2 * stacks[0].shape[0]

    def kernel(place_ref, refs, outs):
        vec_ref, wide_ref = outs
        lanes = lax.broadcasted_iota(jnp.int32, (16, owners * count), 1)
        total = jnp.zeros((16, owners * count), F32)
        for code in range(owners):
            owner = place_ref[1] ^ code
            rows = refs[code % 2][code // 2, first : first + 16, :].astype(F32)
            row = jnp.pad(rows[:, :count], ((0, 0), (0, (owners - 1) * count)))
            total = total + pltpu.roll(row, owner * count, 1)
            wide_ref[:, pl.ds(pl.multiple_of(owner * wide, 128), wide)] = jnp.broadcast_to(
                rows[names : names + 1, :wide], (8, wide)
            )
        vec_ref[...] = total[:, :D]

    return local(
        kernel, [shape(16, D, dtype=F32), shape(8, owners * wide, dtype=F32)], place, stacks
    )


def small_total(place, attn_a, attn_b, one, mask, two, wide):
    def kernel(place_ref, refs, outs):
        a, b, first, masked, second, broad = (ref[...] for ref in refs)
        rows = [jnp.concatenate([a[0:2], b[0:2]], axis=1), first[0:3], masked[0:1], second[1:3], second[0:1]]
        rows += [broad[0:1, j * D : (j + 1) * D] for j in range(FF // D)]
        rows.append(jnp.zeros((16 - len(VECTORS) - FF // D, D), F32))
        row = 0
        for part in rows:
            outs[0][row : row + part.shape[0], :] = part
            row += part.shape[0]

    return local(kernel, [shape(16, D, dtype=F32)], place, [attn_a, attn_b, one, mask, two, wide])[0]


def tie(value, *before):
    return lax.optimization_barrier((value, *before))[0]


def in_order(value, order):
    return jnp.concatenate([lax.dynamic_slice_in_dim(value, order[i], 1) for i in range(value.shape[0])])


class Grid:
    def __init__(self, dp, fsdp):
        self.dp, self.fsdp = dp, fsdp
        self.dp_bits = [1 << i for i in range(dp.bit_length() - 1)]
        self.fsdp_bits = [1 << i for i in range(fsdp.bit_length() - 1)]

    def bit(self, axis, bit):
        return (lax.axis_index(axis) // bit) % 2

    def swap(self, value, dp_mask, fsdp_mask):
        if not dp_mask:
            return lax.ppermute(value, "fsdp", [(i, i ^ fsdp_mask) for i in range(self.fsdp)])
        if not fsdp_mask:
            return lax.ppermute(value, "dp", [(i, i ^ dp_mask) for i in range(self.dp)])
        pairs = [
            (i * self.fsdp + j, (i ^ dp_mask) * self.fsdp + (j ^ fsdp_mask))
            for i in range(self.dp)
            for j in range(self.fsdp)
        ]
        return lax.ppermute(value, ("dp", "fsdp"), pairs)

    def gather(self, piece):
        gathered = piece[None]
        for bit in self.fsdp_bits:
            gathered = jnp.concatenate([gathered, self.swap(gathered, 0, bit)])
        return gathered

    def from_far(self, piece):
        return [piece] + [self.swap(piece, 0, 2 * code) for code in range(1, self.fsdp // 2)]

    def stages(self):
        dp_left, fsdp_left = self.dp_bits[1:], list(self.fsdp_bits)
        order = [[("dp", 1)]]
        while dp_left and fsdp_left:
            order.append([("dp", dp_left.pop(0)), ("fsdp", fsdp_left.pop(0))])
        order += [[("dp", bit)] for bit in dp_left]
        while fsdp_left:
            order.append([("fsdp", bit) for bit in fsdp_left[:2]])
            fsdp_left = fsdp_left[2:]
        return order

    def reduce(self, grads):
        rows, width = grads.shape[1:]
        left = list(reversed(self.fsdp_bits))
        value = grads.reshape((2,) * len(left) + (rows, width))
        halved = []
        for stage in self.stages():
            for axis, bit in stage:
                if axis == "dp":
                    value = value.reshape(value.shape[:-2] + (2, value.shape[-2] // 2, width))
                    halved.append(bit)
            spots = {}
            extra = len(left)
            for axis, bit in stage:
                if axis == "dp":
                    spots[(axis, bit)] = extra
                    extra += 1
                else:
                    spots[(axis, bit)] = left.index(bit)
            total = None
            for code in range(1 << len(stage)):
                starts = [0] * value.ndim
                sizes = list(value.shape)
                masks = {"dp": 0, "fsdp": 0}
                for place, (axis, bit) in enumerate(stage):
                    other = (code >> place) & 1
                    starts[spots[(axis, bit)]] = self.bit(axis, bit) ^ other
                    sizes[spots[(axis, bit)]] = 1
                    masks[axis] += bit * other
                part = lax.dynamic_slice(value, starts, sizes)
                if code:
                    part = self.swap(part, masks["dp"], masks["fsdp"])
                part = part.astype(F32)
                total = part if total is None else total + part
            total = jnp.squeeze(total, tuple(spots.values()))
            left = [bit for bit in left if ("fsdp", bit) not in spots]
            value = total.astype(BF16)
        for bit in reversed(halved):
            other = self.swap(value, bit, 0)
            first = self.bit("dp", bit) == 0
            value = jnp.concatenate([jnp.where(first, value, other), jnp.where(first, other, value)])
        return value.astype(F32)

    def total(self, value):
        for bit in self.dp_bits:
            value = value + self.swap(value, bit, 0)
        for bit in self.fsdp_bits:
            value = value + self.swap(value, 0, bit)
        return value


def packed_vectors(rows, count, wide, names):
    owners = rows.shape[0]
    vec = rows[:, : names * count].reshape(owners, names, count)
    vec = jnp.swapaxes(vec, 0, 1).reshape(names, owners * count)[:, :D].astype(F32)
    b1 = rows[:, names * count : names * count + wide].reshape(1, -1)[:, :FF].astype(F32)
    return jnp.pad(vec, ((0, 16 - names), (0, 0))), jnp.broadcast_to(b1, (8, FF))


VECTORS = ("qb", "vb", "ob", "g1", "s1", "m", "g2", "s2", "b2")


def vector_grads(small, count, wide, d_max, ff_max):
    me = lax.axis_index("fsdp")
    rows = jnp.pad(small[: len(VECTORS)], ((0, 0), (0, d_max - D)))
    rows = lax.dynamic_slice(rows, (0, me * count), (len(VECTORS), count))
    grads = {name: rows[i] for i, name in enumerate(VECTORS)}
    b1 = jnp.pad(small[len(VECTORS) : len(VECTORS) + FF // D].reshape(-1), (0, ff_max - FF))
    grads["b1"] = lax.dynamic_slice(b1, (me * wide,), (wide,))
    return grads


def small_rows(attn, one, mask, two, wide):
    return jnp.concatenate(
        [attn[0:2], one[0:3], mask[0:1], two[1:3], two[0:1], wide[0].reshape(FF // D, D), jnp.zeros((3, D), F32)]
    )


def in_columns(weight):
    return [weight[:, j * D : (j + 1) * D] for j in range(FF // D)]


def any_grid(grid, frames, cotangent, span_starts, matrices, vectors, up_bias):
    query, key, value, out, up, down = matrices
    count, wide = query.shape[0], down.shape[0]
    owners = grid.fsdp
    d_max, ff_max = count * owners, wide * owners
    me, core = lax.axis_index("fsdp"), lax.axis_index("dp") % 2
    codes = me ^ jnp.arange(owners, dtype=jnp.int32)

    def gathered(pieces):
        stack = in_order(grid.gather(jnp.concatenate(pieces)), codes)
        stack = stack.reshape(owners, len(pieces), -1, D)
        return [stack[:, i].reshape(-1, D) for i in range(len(pieces))]

    packed = jnp.concatenate(vectors + [up_bias]).reshape(1, -1)
    packed = in_order(grid.gather(packed)[:, 0], codes)
    vec, b1 = packed_vectors(packed, count, wide, len(vectors))
    wq, wk, wv, wo = gathered([piece[:, :D] for piece in (query, key, value, out)])
    up_blocks = gathered(in_columns(up))
    (w2,) = gathered([down[:, :D]])

    def unit(role_zero, role_one):
        first = core == 0
        return ([jnp.where(first, role_zero, role_one)[None]], [jnp.where(first, role_one, role_zero)[None]])

    one, two = unit(wq, wk), unit(wv, wo)
    up_unit = unit(jnp.concatenate(up_blocks[:2]), jnp.concatenate(up_blocks[2:]))
    down_unit = unit(w2[: ff_max // 2], w2[ff_max // 2 :])
    place = jnp.stack([core, jnp.zeros_like(core), jnp.zeros_like(core)])
    layer = Layer(place, span_starts[:, None, :], frames, vec, b1, d_max, ff_max, d_max, ff_max, False)
    q, k, v, o, lse, n1, rstd = layer.attn_forward(one, two)
    hidden, slope = layer.ffn_up(up_unit, n1)
    output, dz, dr2, small2, down_grad = layer.ffn_down(down_unit, n1, hidden, cotangent, False)
    dr1, do, small1, wide_small, *up_out = layer.ffn_backward(
        two, up_unit, down_unit, n1, rstd, dz, dr2, slope, o
    )
    dq, dk, dv, small_a, *qkv = layer.attn_backward(0, HEADS // 2, q, k, v, do, lse)
    frames_grad, small_m = layer.input_backward(one, two, dr1, (dq, dk, dv))
    small = grid.total(small_rows(small_a, small1, small_m, small2, wide_small))

    def reduced(grads):
        total = grid.reduce(jnp.concatenate([grad.reshape(owners, -1, D) for grad in grads], axis=1))
        return [part for part in total.reshape(len(grads), -1, D)]

    def wide_rows(grad):
        return jnp.pad(grad, ((0, 0), (0, d_max - D)))

    sums = [wide_rows(grad) for grad in reduced(qkv)]
    up_out = reduced(up_out)
    sums.append(wide_rows(up_out[-1]))
    zeros = jnp.zeros((count, up.shape[1] - FF), F32)
    sums.append(jnp.concatenate(up_out[:-1] + [zeros], axis=1))
    sums.append(wide_rows(reduced([down_grad])[0]))
    return output, frames_grad, sums, vector_grads(small, count, wide, d_max, ff_max)


def four_by_eight(grid, frames, cotangent, span_starts, matrices, vectors, up_bias):
    query, key, value, out, up, down = matrices
    count, wide = query.shape[0], down.shape[0]
    owners = grid.fsdp
    d_max, ff_max = count * owners, wide * owners
    me, dp_at = lax.axis_index("fsdp"), lax.axis_index("dp")
    core = dp_at % 2
    first = core == 0
    place = jnp.stack([core, me, dp_at // 2])

    packed = jnp.pad(jnp.stack(vectors), ((0, 0), (0, D - count)))
    packed = jnp.concatenate([packed, jnp.pad(up_bias, (0, D - wide))[None]])
    packed = jnp.pad(packed, ((0, 16 - packed.shape[0]), (0, 0)))
    half = wide // 2
    blocks = in_columns(up)
    pieces = (
        jnp.where(first, query[:, :D], key[:, :D]),
        jnp.concatenate([jnp.where(first, value[:, :D], out[:, :D]), packed]),
        jnp.where(first, jnp.concatenate(blocks[:2]), jnp.concatenate(blocks[2:])),
        jnp.where(first, down[:half, :D], down[half:, :D]),
    )
    far, near = [], []
    for piece in pieces[:3]:
        far.append(jnp.stack(grid.from_far(tie(piece, far[-1]) if far else piece)))
    for stack in far:
        near.append(grid.swap(tie(stack, near[-1]) if near else stack, 0, 1))
    last = grid.from_far(tie(pieces[3], far[-1]))

    def other_core(stacks, *before):
        return stacks, [grid.swap(tie(stack, *before) if before else stack, 1, 0) for stack in stacks]

    stacks = list(zip(far, near))
    one, two = other_core(stacks[0]), other_core(stacks[1])
    vec, b1 = unpack(place, stacks[1], count, count, wide, len(vectors))

    layer = Layer(place, span_starts[:, None, :], frames, vec, b1, count, wide, d_max, ff_max, True)
    q, k, v, o, lse, n1, rstd = layer.attn_forward(one, two, after=(far[2],))
    last = jnp.stack([last[0]] + [tie(piece, n1) for piece in last[1:]])
    up_unit = other_core(stacks[2], n1, last)
    hidden, slope = layer.ffn_up(up_unit, n1)
    down_unit = other_core((last, grid.swap(tie(last, near[2]), 0, 1)), hidden)
    output, dz, dr2, small2, down_grad = layer.ffn_down(down_unit, n1, hidden, cotangent, False)
    down_sum = lax.psum_scatter(down_grad.reshape(owners, wide, D), "fsdp", scatter_dimension=0)
    dr1, do, small1, wide_small, *up_out = layer.ffn_backward(
        two, up_unit, down_unit, n1, rstd, dz, dr2, slope, o
    )

    def spread(kept_half, sent_half, *before):
        parts = first_sums(place, kept_half, grid.swap(tie(sent_half, *before), 1, 0))
        return parts[0], [grid.swap(parts[j], 2 * (j % 2), j // 2) for j in range(1, 4)]

    def spread_far(own, received):
        parts = next_sums(place, [own] + received, True)
        return parts[0], [grid.swap(parts[j], 0, 2 * j) for j in range(1, 4)]

    def closing(own, received):
        total = next_sums(place, [own] + received, False)[0]
        along = grid.swap(total, 2, 0)
        return total, along, grid.swap(total, 1, 0), grid.swap(along, 1, 0)

    own_u, got_u = spread(*up_out)
    split = FIRST_PAIRS
    dqa, dka, dva, small_a, *qkv_a = layer.attn_backward(0, split, q, k, v, do, lse, after=(own_u,))
    far_u, got_far_u = spread_far(own_u, got_u)
    own_a, got_a = spread(*qkv_a, far_u)
    for bit in grid.dp_bits:
        low = down_sum.astype(BF16)
        down_sum = low.astype(F32) + grid.swap(low, bit, 0).astype(F32)
    dqb, dkb, dvb, small_b, *qkv_b = layer.attn_backward(
        split, HEADS // 2 - split, q, k, v, do, lse, after=(far_u, own_a)
    )
    own_b, got_b = spread(*qkv_b, *got_a, *got_far_u[:2])
    far_a, got_far_a = spread_far(tie(own_a, own_b), got_a)
    frames_grad, small_m = layer.input_backward(
        one, two, dr1, (dqa, dka, dva, dqb, dkb, dvb), after=(far_a,)
    )
    far_b, got_far_b = spread_far(own_b, got_b)
    small = grid.total(tie(small_total(place, small_a, small_b, small1, small_m, small2, wide_small), far_b))
    all_u = closing(tie(far_u, far_b), got_far_u)
    all_a = closing(tie(far_a, far_b), got_far_a)
    all_b = closing(far_b, got_far_b)
    up_sum, out_sum = finish(
        place, [all_u],
        [(count, up.shape[1], [(0, j, j * D) for j in range(FF // D)]), (count, d_max, [(0, FF // D, 0)])],
    )
    qkv_sums = finish(
        place, [all_a, all_b],
        [(count, d_max, [(0, j, 0), (1, j, split * PAIR)]) for j in range(3)],
    )
    sums = list(qkv_sums) + [out_sum, up_sum, jnp.pad(down_sum, ((0, 0), (0, d_max - D)))]
    return output, frames_grad, sums, vector_grads(small, count, wide, d_max, ff_max)


def on_device(
    sizes, frames, cotangent, span_starts, query_weight, key_weight, value_weight, out_weight,
    query_bias, value_bias, out_bias, first_gain, first_shift, up_weight, up_bias, down_weight,
    down_bias, second_gain, second_shift, mask_vector,
):
    grid = Grid(*sizes)
    matrices = (query_weight, key_weight, value_weight, out_weight, up_weight, down_weight)
    vectors = [query_bias, value_bias, out_bias, first_gain, first_shift, mask_vector,
               second_gain, second_shift, down_bias]
    placed = sizes == (4, 8) and query_weight.shape[0] % 32 == 0
    program = four_by_eight if placed else any_grid
    output, frames_grad, sums, small = program(
        grid, frames, cotangent, span_starts, matrices, vectors, up_bias
    )
    return (
        output, frames_grad, *sums[:4], small["qb"], small["vb"], small["ob"], small["g1"], small["s1"],
        sums[4], small["b1"], sums[5], small["b2"], small["g2"], small["s2"], small["m"],
    )


def solution(mesh):
    sizes = (mesh.shape["dp"], mesh.shape["fsdp"])
    tokens = P(("dp", "fsdp"), None)
    matrix, vector = P("fsdp", None), P("fsdp")
    return jax.shard_map(
        functools.partial(on_device, sizes),
        mesh=mesh,
        in_specs=(tokens,) * 3 + (matrix,) * 4 + (vector,) * 5 + (matrix, vector, matrix) + (vector,) * 4,
        out_specs=(tokens,) * 2 + (matrix,) * 4 + (vector,) * 5 + (matrix, vector, matrix) + (vector,) * 4,
        check_vma=False,
    )
```

```python
import functools
import jax
import jax.numpy as jnp
from jax import lax
from jax.experimental import pallas as pl
from jax.experimental.pallas import tpu as pltpu
from jax.sharding import PartitionSpec as P

HEADS = 10
HEAD_DIM = 64
FF = 2560
D = 640
FRAMES = 400
SPAN = 10
PAIR = 2 * HEAD_DIM
EPS = 1e-05
F32 = jnp.float32
BF16 = jnp.bfloat16
VMEM_LIMIT = 60 * 1024 * 1024
HID = 256


def dot_nn(a, b):
    return lax.dot_general(a, b, (((1,), (0,)), ((), ())), preferred_element_type=F32)


def dot_nt(a, b):
    return lax.dot_general(a, b, (((1,), (1,)), ((), ())), preferred_element_type=F32)


def dot_tn(a, b):
    return lax.dot_general(a, b, (((0,), (0,)), ((), ())), preferred_element_type=F32)


def mean_last(a):
    return jnp.mean(a, axis=-1, keepdims=True)


def rows_sum(a):
    return jnp.sum(a, axis=0, keepdims=True)


def masked_frames(starts_ref):
    places = lax.broadcasted_iota(jnp.int32, (FRAMES, starts_ref.shape[-1]), 0)
    ahead = places - starts_ref[0]
    inside = jnp.where((ahead >= 0) & (ahead < SPAN), 1.0, 0.0)
    return jnp.max(inside, axis=1, keepdims=True) > 0.5


def far_codes(pieces):
    codes = [0]
    for bit in reversed(range(pieces.bit_length() - 1)):
        codes += [code | 1 << bit for code in codes]
    return codes


def fetch(place_ref, sem, *wanted):
    def copies(unit, parts, role):
        flips = (0, 1) if len(unit) == 2 else (0, 2, 1, 3)
        for arrays, flip in zip(unit, flips):
            for group, source in enumerate(arrays):
                for piece, code in enumerate(far_codes(source.shape[0])):
                    owner = place_ref[1] ^ (code * len(arrays) + group)
                    for share, first, rows, stride, row, column, target in parts:
                        if share == (role % len(unit)) ^ flip:
                            low = pl.multiple_of(owner * stride + row, 16)
                            yield pltpu.make_async_copy(
                                source.at[piece, pl.ds(first, rows), :],
                                target.at[pl.ds(low, rows), pl.ds(column, D)],
                                sem,
                            )

    for role in range(max(len(unit) for unit, _ in wanted)):
        here = place_ref[0] == role % 2
        if any(len(unit) > 2 for unit, _ in wanted):
            here = here & (place_ref[2] == role // 2)

        @pl.when(here)
        def _(role=role):
            started = [copy for unit, parts in wanted for copy in copies(unit, parts, role)]
            for copy in started:
                copy.start()
            for copy in started:
                copy.wait()


def attn_parts(rows, *targets):
    return [(share, 0, rows, rows, 0, 0, target) for share, target in enumerate(targets) if target is not None]


def up_parts(target, rows):
    return [(j // 2, (j % 2) * rows, rows, rows, 0, j * D, target) for j in range(FF // D)]


def down_parts(target, rows):
    return [(core, 0, rows // 2, rows, core * (rows // 2), 0, target) for core in (0, 1)]


def attn_forward(
    place_ref, attn, starts_ref, frames_ref, vec_ref,
    q_ref, k_ref, v_ref, o_ref, lse_ref, n1_ref, rstd_ref,
    wq_ref, wk_ref, wv_ref, wo_ref, sem, *, rows,
):
    @pl.when(pl.program_id(0) == 0)
    def _():
        fetch(place_ref, sem, (attn, attn_parts(rows, wq_ref, wk_ref, wv_ref, wo_ref)))

    bq, bv, bo = vec_ref[0:1, :], vec_ref[1:2, :], vec_ref[2:3, :]
    x0 = jnp.where(masked_frames(starts_ref), vec_ref[5:6, :], frames_ref[...].astype(F32))
    h = x0.astype(BF16)
    scale = HEAD_DIM ** (-0.5)
    q_ref[...] = ((dot_nn(h, wq_ref[0:D, :]) + bq).astype(BF16).astype(F32) * scale).astype(BF16)
    k_ref[...] = dot_nn(h, wk_ref[0:D, :]).astype(BF16)
    v_ref[...] = (dot_nn(h, wv_ref[0:D, :]) + bv).astype(BF16)
    low_lanes = lax.broadcasted_iota(jnp.int32, (FRAMES, PAIR), 1) < HEAD_DIM
    lanes = lax.broadcasted_iota(jnp.int32, (FRAMES, 128), 1)
    lse = jnp.zeros((FRAMES, 128), F32)
    for pair in range(HEADS // 2):
        cols = slice(pair * PAIR, (pair + 1) * PAIR)
        qp, kp, vp = q_ref[:, cols], k_ref[:, cols], v_ref[:, cols]
        parts = []
        for half in range(2):
            keep = low_lanes if half == 0 else jnp.logical_not(low_lanes)
            qh = jnp.where(keep, qp.astype(F32), 0.0).astype(BF16)
            scores = dot_nt(qh, kp)
            top = jnp.max(scores, axis=-1, keepdims=True)
            expo = jnp.exp(scores - top)
            total = jnp.sum(expo, axis=-1, keepdims=True)
            parts.append(dot_nn(expo.astype(BF16), vp) * (1.0 / total))
            lse = jnp.where(lanes == 2 * pair + half, top + jnp.log(total), lse)
        o_ref[:, cols] = jnp.where(low_lanes, parts[0], parts[1]).astype(BF16)
    lse_ref[0] = jnp.transpose(lse)[0:16, :]
    r1 = x0 + (dot_nn(o_ref[...], wo_ref[0:D, :]) + bo)
    center = r1 - mean_last(r1)
    rstd = lax.rsqrt(mean_last(center * center) + EPS)
    n1_ref[...] = center * rstd
    rstd_ref[...] = rstd


def gelu_parts(u):
    phi = 0.5 + 0.5 * lax.erf(u * 0.7071067811865476)
    return u * phi, phi + u * jnp.exp(u * u * -0.5) * 0.3989422804014327


def ffn_up(place_ref, up, n1_ref, vec_ref, b1_ref, hidden_ref, slope_ref, w1_ref, sem, *, rows):
    @pl.when(pl.program_id(0) == 0)
    def _():
        fetch(place_ref, sem, (up, up_parts(w1_ref, rows)))

    y1b = (vec_ref[3:4, :] * n1_ref[...] + vec_ref[4:5, :]).astype(BF16)
    for c in range(FF // HID):
        cols = slice(c * HID, (c + 1) * HID)
        u = dot_nn(y1b, w1_ref[0:D, cols]) + b1_ref[0:1, cols]
        act, slope = gelu_parts(u)
        hidden_ref[:, cols] = act.astype(BF16)
        slope_ref[:, cols] = slope.astype(BF16)


def ffn_down(
    place_ref, down, n1_ref, hidden_ref, cot_ref, vec_ref,
    out_ref, dz_ref, dr2_ref, small_ref, *rest, rows, halves,
):
    grads_refs, (acc, w2_ref, sem) = rest[:-3], rest[-3:]
    step = pl.program_id(0)

    @pl.when(step == 0)
    def _():
        small_ref[...] = jnp.zeros_like(small_ref)
        acc[...] = jnp.zeros_like(acc)
        fetch(place_ref, sem, (down, down_parts(w2_ref, rows)))

    g1, s1, g2, s2, b2 = (vec_ref[i : i + 1, :] for i in (3, 4, 6, 7, 8))
    y1 = g1 * n1_ref[...] + s1
    r2 = y1 + (dot_nn(hidden_ref[...], w2_ref[0:FF, :]) + b2)
    center = r2 - mean_last(r2)
    rstd = lax.rsqrt(mean_last(center * center) + EPS)
    n2 = center * rstd
    out_ref[...] = (n2 * g2 + s2).astype(BF16)
    dy = cot_ref[...].astype(F32)
    e = dy * g2
    dr2 = (e - mean_last(e) - n2 * mean_last(e * n2)) * rstd
    dz = dr2.astype(BF16)
    dr2_ref[...] = dr2
    dz_ref[...] = dz
    small_ref[0:1, :] += rows_sum(dz.astype(F32))
    small_ref[1:2, :] += rows_sum(dy * n2)
    small_ref[2:3, :] += rows_sum(dy)
    acc[0:FF, :] += dot_tn(hidden_ref[...], dz)

    @pl.when(step == pl.num_programs(0) - 1)
    def _():
        deliver(place_ref, grads_refs, [(acc, 0, rows)], halves)


def deliver(place_ref, refs, sources, halves):
    if not halves:
        for ref, (acc, column, _) in zip(refs, sources):
            ref[...] = acc[:, column : column + ref.shape[1]].astype(BF16)
        return
    for ref, core in zip(refs, (place_ref[0], 1 - place_ref[0])):
        owners, parts, _, width = ref.shape
        for owner in range(owners):
            for part in range(parts):
                pieces = []
                for acc, column, rows in sources:
                    size = rows // 4
                    low = pl.multiple_of(owner * rows + (2 * core + part) * size, 8)
                    pieces.append(acc[pl.ds(low, size), column : column + width])
                ref[owner, part] = jnp.concatenate(pieces, axis=0).astype(BF16)


def ffn_backward(
    place_ref, attn, up, down, starts_ref, n1_ref, rstd_ref, dz_ref, dr2_ref, slope_ref, o_ref, vec_ref,
    dr1_ref, do_ref, small_ref, db1_ref, *rest, rows, halves,
):
    grads_refs = rest[:-7]
    grad_pre, acc1, acco, w1_ref, w2_ref, wo_ref, sem = rest[-7:]
    step = pl.program_id(0)

    @pl.when(step == 0)
    def _():
        small_ref[...] = jnp.zeros_like(small_ref)
        db1_ref[...] = jnp.zeros_like(db1_ref)
        acc1[...] = jnp.zeros_like(acc1)
        acco[...] = jnp.zeros_like(acco)
        fetch(
            place_ref, sem,
            (attn, attn_parts(rows[0], None, None, None, wo_ref)), (up, up_parts(w1_ref, rows[0])), (down, down_parts(w2_ref, rows[1])),
        )

    g1, s1 = vec_ref[3:4, :], vec_ref[4:5, :]
    n1 = n1_ref[...]
    y1b = (g1 * n1 + s1).astype(BF16)
    dz = dz_ref[...]
    for c in range(FF // HID):
        cols = slice(c * HID, (c + 1) * HID)
        du = (dot_nt(dz, w2_ref[cols, :]) * slope_ref[:, cols].astype(F32)).astype(BF16)
        grad_pre[:, cols] = du
        db1_ref[0:1, cols] += rows_sum(du.astype(F32))
    acc1[0:D, :] += dot_tn(y1b, grad_pre[...])
    dy1 = dot_nt(grad_pre[...], w1_ref[0:D, :]) + dr2_ref[...]
    e = dy1 * g1
    dr1 = (e - mean_last(e) - n1 * mean_last(e * n1)) * rstd_ref[...]
    dr1_ref[...] = dr1
    da = dr1.astype(BF16)
    small_ref[0:1, :] += rows_sum(da.astype(F32))
    small_ref[1:2, :] += rows_sum(dy1 * n1)
    small_ref[2:3, :] += rows_sum(dy1)
    small_ref[3:4, :] += rows_sum(jnp.where(masked_frames(starts_ref), dr1, 0.0))
    acco[0:D, :] += dot_tn(o_ref[...], da)
    do_ref[...] = dot_nt(da, wo_ref[0:D, :]).astype(BF16)

    @pl.when(step == pl.num_programs(0) - 1)
    def _():
        sources = [(acc1, j * D, rows[0]) for j in range(FF // D)] + [(acco, 0, rows[0])]
        deliver(place_ref, grads_refs, sources, halves)


def attn_backward(
    place_ref, starts_ref, frames_ref, vec_ref, q_ref, k_ref, v_ref, do_ref, lse_ref,
    dq_ref, dk_ref, dv_ref, small_ref, *rest, rows, halves,
):
    grads_refs, (accq, acck, accv) = rest[:-3], rest[-3:]
    step = pl.program_id(0)

    @pl.when(step == 0)
    def _():
        small_ref[...] = jnp.zeros_like(small_ref)
        accq[...] = jnp.zeros_like(accq)
        acck[...] = jnp.zeros_like(acck)
        accv[...] = jnp.zeros_like(accv)

    scale = HEAD_DIM ** (-0.5)
    low_lanes = lax.broadcasted_iota(jnp.int32, (FRAMES, PAIR), 1) < HEAD_DIM
    for pair in range(HEADS // 2):
        cols = slice(pair * PAIR, (pair + 1) * PAIR)
        qp, kp, vp, dop = q_ref[:, cols], k_ref[:, cols], v_ref[:, cols], do_ref[:, cols]
        parts = []
        for half in range(2):
            keep = low_lanes if half == 0 else jnp.logical_not(low_lanes)
            kh = jnp.where(keep, kp.astype(F32), 0.0).astype(BF16)
            vh = jnp.where(keep, vp.astype(F32), 0.0).astype(BF16)
            head = 2 * pair + half
            prob = jnp.exp(dot_nt(kh, qp) - lse_ref[0, head : head + 1, :])
            dprob = dot_nt(vh, dop)
            inner = jnp.sum(prob * dprob, axis=0, keepdims=True)
            dscore = (prob * (dprob - inner)).astype(BF16)
            parts.append((dot_nn(prob.astype(BF16), dop), dot_nn(dscore, qp), dot_tn(dscore, kp) * scale))
        for ref, one, two in zip((dv_ref, dk_ref, dq_ref), *parts):
            ref[:, cols] = jnp.where(low_lanes, one, two).astype(BF16)
    masked = masked_frames(starts_ref)
    h = jnp.where(masked, vec_ref[5:6, :], frames_ref[...].astype(F32)).astype(BF16)
    accq[0:D, :] += dot_tn(h, dq_ref[...])
    acck[0:D, :] += dot_tn(h, dk_ref[...])
    accv[0:D, :] += dot_tn(h, dv_ref[...])
    small_ref[0:1, :] += rows_sum(dq_ref[...].astype(F32))
    small_ref[1:2, :] += rows_sum(dv_ref[...].astype(F32))
    for row, ref in enumerate((dq_ref, dk_ref, dv_ref), 2):
        small_ref[row : row + 1, :] += rows_sum(jnp.where(masked, ref[...].astype(F32), 0.0))

    @pl.when(step == pl.num_programs(0) - 1)
    def _():
        deliver(place_ref, grads_refs, [(acc, 0, rows) for acc in (accq, acck, accv)], halves)


def input_backward(
    place_ref, attn, starts_ref, dr1_ref, *rest, rows,
):
    parts, (grad_ref, wq_ref, wk_ref, wv_ref, sem) = rest[:-5], rest[-5:]

    @pl.when(pl.program_id(0) == 0)
    def _():
        fetch(place_ref, sem, (attn, attn_parts(rows, wq_ref, wk_ref, wv_ref)))

    masked = masked_frames(starts_ref)
    dx0 = dr1_ref[...]
    for grad, weight in zip(parts, (wq_ref, wk_ref, wv_ref)):
        dx0 += dot_nt(grad[...], weight[0:D, :])
    grad_ref[...] = jnp.where(masked, 0.0, dx0).astype(BF16)


def row_blocks(width):
    return pl.BlockSpec((FRAMES, width), lambda i, *_: (i, 0))


def kept(rows, cols):
    return pl.BlockSpec((rows, cols), lambda i, *_: (0, 0), pipeline_mode=pl.Buffered(1))


def held(*sizes):
    return pl.BlockSpec(sizes, lambda i, *_: (0,) * len(sizes))


def shape(*sizes, dtype=BF16):
    return jax.ShapeDtypeStruct(sizes, dtype)


SCALARS = pl.BlockSpec(memory_space=pltpu.SMEM)
WHOLE = pl.BlockSpec(memory_space=pl.ANY)
COPIES = pltpu.SemaphoreType.DMA(())


def call(
    body, steps, place, units, operands, in_specs, outputs, scratch=(), after=(), flops=0, moved=0,
):
    flat = [array for unit in units for arrays in unit for array in arrays]

    def kernel(place_ref, *refs):
        refs = refs[len(after) :]
        given = []
        for unit in units:
            given.append([])
            for arrays in unit:
                given[-1].append(refs[: len(arrays)])
                refs = refs[len(arrays) :]
        body(place_ref, *given, *refs)

    return pl.pallas_call(
        kernel,
        grid=(steps,),
        in_specs=[SCALARS] + [WHOLE] * (len(after) + len(flat)) + in_specs,
        out_specs=[spec for spec, _ in outputs],
        out_shape=[out for _, out in outputs],
        scratch_shapes=list(scratch),
        compiler_params=pltpu.CompilerParams(
            dimension_semantics=("arbitrary",), vmem_limit_bytes=VMEM_LIMIT
        ),
        cost_estimate=pl.CostEstimate(flops=int(flops), bytes_accessed=int(moved), transcendentals=0),
    )(place, *after, *flat, *operands)


def starts_spec(starts):
    return pl.BlockSpec((1, 1, starts.shape[-1]), lambda i: (i, 0, 0))


def lse_spec():
    return pl.BlockSpec((1, 16, FRAMES), lambda i: (i, 0, 0))


def weights(*sizes):
    return [pltpu.VMEM(size, BF16) for size in sizes] + [COPIES]


def by_rows(rows, width, dtype=BF16):
    return (row_blocks(width), shape(rows, width, dtype=dtype))


def summed(rows, width):
    return (held(rows, width), shape(rows, width, dtype=F32))


def grads_out(halves, sources):
    if not halves:
        return [(held(rows, width), shape(rows, width)) for rows, width, _ in sources]
    rows, width, count = sources[0]
    sizes = (rows // count, 2, sum(part[2] for part in sources) // 4, width)
    return [(held(*sizes), shape(*sizes))] * 2


class Layer:
    def __init__(self, place, starts, frames, vec, b1, d_rows, ff_rows, d_max, ff_max, halves):
        self.place, self.starts, self.frames, self.vec, self.b1 = place, starts, frames, vec, b1
        self.d_rows, self.ff_rows, self.d_max, self.ff_max, self.halves = d_rows, ff_rows, d_max, ff_max, halves
        self.rows = frames.shape[0]
        self.steps = self.rows // FRAMES

    def attn_forward(self, attn, after=()):
        rows = self.rows
        return call(
            functools.partial(attn_forward, rows=self.d_rows), self.steps, self.place, (attn,),
            (self.starts, self.frames, self.vec), [starts_spec(self.starts), row_blocks(D), kept(16, D)],
            [by_rows(rows, D)] * 4
            + [(lse_spec(), shape(self.steps, 16, FRAMES, dtype=F32)), by_rows(rows, D, F32), by_rows(rows, 1, F32)],
            weights(*[(self.d_max, D)] * 4), after,
            flops=rows * D * D * 8 + rows * FRAMES * D * 16, moved=rows * D * 14,
        )

    def ffn_up(self, up, n1, after=()):
        rows = self.rows
        return call(
            functools.partial(ffn_up, rows=self.d_rows), self.steps, self.place, (up,),
            (n1, self.vec, self.b1), [row_blocks(D), kept(16, D), kept(8, FF)],
            [by_rows(rows, FF)] * 2, weights((self.d_max, FF)), after,
            flops=rows * D * FF * 4, moved=rows * FF * 6,
        )

    def ffn_down(self, down, n1, hidden, cotangent, halves, after=()):
        rows = self.rows
        return call(
            functools.partial(ffn_down, rows=self.ff_rows, halves=halves), self.steps, self.place, (down,),
            (n1, hidden, cotangent, self.vec), [row_blocks(D), row_blocks(FF), row_blocks(D), kept(16, D)],
            [by_rows(rows, D), by_rows(rows, D), by_rows(rows, D, F32), summed(8, D)]
            + grads_out(halves, [(self.ff_max, D, self.ff_rows)]),
            [pltpu.VMEM((self.ff_max, D), F32)] + weights((self.ff_max, D)), after,
            flops=rows * D * FF * 6, moved=rows * FF * 8,
        )

    def ffn_backward(self, attn, up, down, n1, rstd, dz, dr2, slope, o, after=()):
        rows = self.rows
        return call(
            functools.partial(ffn_backward, rows=(self.d_rows, self.ff_rows), halves=self.halves),
            self.steps, self.place, (attn, up, down),
            (self.starts, n1, rstd, dz, dr2, slope, o, self.vec),
            [starts_spec(self.starts)] + [row_blocks(w) for w in (D, 1, D, D, FF, D)] + [kept(16, D)],
            [by_rows(rows, D, F32), by_rows(rows, D), summed(8, D), summed(8, FF)]
            + grads_out(
                self.halves,
                [(self.d_max, D, self.d_rows)] * 5,
            ),
            [pltpu.VMEM((FRAMES, FF), BF16), pltpu.VMEM((self.d_max, FF), F32), pltpu.VMEM((self.d_max, D), F32)]
            + weights((self.d_max, FF), (self.ff_max, D), (self.d_max, D)), after,
            flops=rows * D * FF * 8 + rows * D * D * 4, moved=rows * FF * 8,
        )

    def attn_backward(self, q, k, v, do, lse, after=()):
        rows = self.rows
        return call(
            functools.partial(attn_backward, rows=self.d_rows, halves=self.halves),
            self.steps, self.place, (), (self.starts, self.frames, self.vec, q, k, v, do, lse),
            [starts_spec(self.starts), row_blocks(D), kept(16, D)] + [row_blocks(D)] * 4 + [lse_spec()],
            [by_rows(rows, D)] * 3 + [summed(8, D)] + grads_out(self.halves, [(self.d_max, D, self.d_rows)] * 3),
            [pltpu.VMEM((self.d_max, D), F32)] * 3, after,
            flops=rows * D * D * 6 + rows * FRAMES * D * 40, moved=rows * D * 14,
        )

    def input_backward(self, attn, dr1, parts, after=()):
        rows = self.rows
        return call(
            functools.partial(input_backward, rows=self.d_rows), self.steps, self.place, (attn,),
            (self.starts, dr1, *parts),
            [starts_spec(self.starts), row_blocks(D)] + [row_blocks(part.shape[1]) for part in parts],
            [by_rows(rows, D)], weights(*[(self.d_max, D)] * 3), after,
            flops=rows * D * D * 8, moved=rows * D * 12,
        )


def local(kernel, outputs, place, operands, scratch=(), cost=0):
    count = len(operands)

    def body(place_ref, *refs):
        sources, outs = refs[:count], refs[count : count + len(outputs)]
        held_refs, sems = refs[count + len(outputs) : -1], refs[-1]
        copies = [
            pltpu.make_async_copy(source, target, sems.at[i])
            for i, (source, target) in enumerate(zip(sources, held_refs))
        ]
        for copy in copies:
            copy.start()
        for copy in copies:
            copy.wait()
        kernel(place_ref, held_refs, outs)

    vmem = pl.BlockSpec(memory_space=pltpu.VMEM)
    return pl.pallas_call(
        body,
        in_specs=[SCALARS] + [WHOLE] * count,
        out_specs=[vmem] * len(outputs),
        out_shape=outputs,
        scratch_shapes=[pltpu.VMEM(array.shape, array.dtype) for array in operands]
        + [pltpu.SemaphoreType.DMA((count,))],
        compiler_params=pltpu.CompilerParams(vmem_limit_bytes=VMEM_LIMIT),
        cost_estimate=pl.CostEstimate(flops=1000, bytes_accessed=4 * sum(a.size for a in operands), transcendentals=0),
    )(place, *operands)


def first_sums(place, kept_half, received):
    owners, _, rows, width = kept_half.shape

    def kernel(place_ref, refs, outs):
        for j in range(4):
            for z in range(owners // 2):
                owner, part = 2 * z + ((place_ref[1] % 2) ^ (j // 2)), place_ref[2] ^ (j % 2)
                outs[j][z] = (refs[0][owner, part].astype(F32) + refs[1][owner, part].astype(F32)).astype(BF16)

    return local(kernel, [shape(owners // 2, rows, width)] * 4, place, [kept_half, received])


def next_sums(place, *groups):
    rows = groups[0][0].shape[1]
    widths = [group[0].shape[2] for group in groups]

    def kernel(place_ref, refs, outs):
        for j, out in enumerate(outs):
            piece = (place_ref[1] // 2) ^ j
            for index, width in enumerate(widths):
                total = refs[4 * index][piece].astype(F32)
                for ref in refs[4 * index + 1 : 4 * index + 4]:
                    total = total + ref[piece].astype(F32)
                column = sum(widths[:index])
                out[:, column : column + width] = total.astype(BF16)

    return local(kernel, [shape(rows, sum(widths))] * 4, place, [array for group in groups for array in group])


def finish(place, groups, outputs):
    flat = [array for group in groups for array in group]
    outs_shape = [shape(rows, cols, dtype=F32) for rows, cols, _ in outputs]

    def kernel(place_ref, refs, outs):
        for ref, (rows, cols, sources) in zip(outs, outputs):
            filled = len(sources) * D
            ref[:, filled:] = jnp.zeros((rows, cols - filled), F32)
            size = rows // 4
            for group, row, column in sources:
                for j in range(4):
                    quarter = 2 * (place_ref[0] ^ (j // 2)) + (place_ref[2] ^ (j % 2))
                    value = refs[4 * group + j][...].astype(F32)
                    low = pl.multiple_of(quarter * size, 8)
                    ref[pl.ds(low, size), column : column + D] = value[row : row + size]

    return local(kernel, outs_shape, place, flat)


def unpack(place, stacks, first, count, wide, names):
    owners = 2 * stacks[0].shape[0]

    def kernel(place_ref, refs, outs):
        vec_ref, wide_ref = outs
        lanes = lax.broadcasted_iota(jnp.int32, (16, owners * count), 1)
        total = jnp.zeros((16, owners * count), F32)
        codes = far_codes(owners // 2)
        for code in range(owners):
            owner = place_ref[1] ^ code
            rows = refs[code % 2][codes.index(code // 2), first : first + 16, :].astype(F32)
            row = jnp.pad(rows[:, :count], ((0, 0), (0, (owners - 1) * count)))
            total = total + pltpu.roll(row, owner * count, 1)
            wide_ref[:, pl.ds(pl.multiple_of(owner * wide, 128), wide)] = jnp.broadcast_to(
                rows[names : names + 1, :wide], (8, wide)
            )
        vec_ref[...] = total[:, :D]

    return local(
        kernel, [shape(16, D, dtype=F32), shape(8, owners * wide, dtype=F32)], place, stacks
    )


def small_total(place, attn, one, two, wide):
    def kernel(place_ref, refs, outs):
        both, first, second, broad = (ref[...] for ref in refs)
        rows = [both[0:2], first[0:3], second[1:3], second[0:1]]
        rows += [broad[0:1, j * D : (j + 1) * D] for j in range(FF // D)]
        rows += [both[2:5], first[3:4]]
        row = 0
        for part in rows:
            outs[0][row : row + part.shape[0], :] = part
            row += part.shape[0]

    return local(kernel, [shape(16, D, dtype=F32)], place, [attn, one, two, wide])[0]


def last_sums(parts):
    return sum(part.astype(F32) for part in parts).astype(BF16)


def tie(value, *before):
    return lax.optimization_barrier((value, *before))[0]


def in_order(value, order):
    return jnp.concatenate([lax.dynamic_slice_in_dim(value, order[i], 1) for i in range(value.shape[0])])


class Grid:
    def __init__(self, dp, fsdp):
        self.dp, self.fsdp = dp, fsdp
        self.dp_bits = [1 << i for i in range(dp.bit_length() - 1)]
        self.fsdp_bits = [1 << i for i in range(fsdp.bit_length() - 1)]

    def bit(self, axis, bit):
        return (lax.axis_index(axis) // bit) % 2

    def swap(self, value, dp_mask, fsdp_mask):
        if not dp_mask:
            return lax.ppermute(value, "fsdp", [(i, i ^ fsdp_mask) for i in range(self.fsdp)])
        if not fsdp_mask:
            return lax.ppermute(value, "dp", [(i, i ^ dp_mask) for i in range(self.dp)])
        pairs = [
            (i * self.fsdp + j, (i ^ dp_mask) * self.fsdp + (j ^ fsdp_mask))
            for i in range(self.dp)
            for j in range(self.fsdp)
        ]
        return lax.ppermute(value, ("dp", "fsdp"), pairs)

    def gather(self, piece):
        gathered = piece[None]
        for bit in self.fsdp_bits:
            gathered = jnp.concatenate([gathered, self.swap(gathered, 0, bit)])
        return gathered

    def joined(self, stack, bit, *before):
        other = self.swap(stack, 0, bit)
        return jnp.concatenate([stack, tie(other, *before) if before else other])

    def stages(self):
        dp_left, fsdp_left = self.dp_bits[1:], list(self.fsdp_bits)
        order = [[("dp", 1)]]
        while dp_left and fsdp_left:
            order.append([("dp", dp_left.pop(0)), ("fsdp", fsdp_left.pop(0))])
        order += [[("dp", bit)] for bit in dp_left]
        while fsdp_left:
            order.append([("fsdp", bit) for bit in fsdp_left[:2]])
            fsdp_left = fsdp_left[2:]
        return order

    def reduce(self, grads):
        rows, width = grads.shape[1:]
        left = list(reversed(self.fsdp_bits))
        value = grads.reshape((2,) * len(left) + (rows, width))
        halved = []
        for stage in self.stages():
            for axis, bit in stage:
                if axis == "dp":
                    value = value.reshape(value.shape[:-2] + (2, value.shape[-2] // 2, width))
                    halved.append(bit)
            spots = {}
            extra = len(left)
            for axis, bit in stage:
                if axis == "dp":
                    spots[(axis, bit)] = extra
                    extra += 1
                else:
                    spots[(axis, bit)] = left.index(bit)
            total = None
            for code in range(1 << len(stage)):
                starts = [0] * value.ndim
                sizes = list(value.shape)
                masks = {"dp": 0, "fsdp": 0}
                for place, (axis, bit) in enumerate(stage):
                    other = (code >> place) & 1
                    starts[spots[(axis, bit)]] = self.bit(axis, bit) ^ other
                    sizes[spots[(axis, bit)]] = 1
                    masks[axis] += bit * other
                part = lax.dynamic_slice(value, starts, sizes)
                if code:
                    part = self.swap(part, masks["dp"], masks["fsdp"])
                part = part.astype(F32)
                total = part if total is None else total + part
            total = jnp.squeeze(total, tuple(spots.values()))
            left = [bit for bit in left if ("fsdp", bit) not in spots]
            value = total.astype(BF16)
        for bit in reversed(halved):
            other = self.swap(value, bit, 0)
            first = self.bit("dp", bit) == 0
            value = jnp.concatenate([jnp.where(first, value, other), jnp.where(first, other, value)])
        return value.astype(F32)

    def total(self, value, holds=()):
        masks = [(bit | 1, 0) for bit in reversed(self.dp_bits)] + [(1, bit) for bit in reversed(self.fsdp_bits)]
        for step, (dp_mask, fsdp_mask) in enumerate(masks):
            received = self.swap(value, dp_mask, fsdp_mask)
            value = value + (tie(received, *holds[step]) if step < len(holds) else received)
        return value


def packed_vectors(rows, count, wide, names):
    owners = rows.shape[0]
    vec = rows[:, : names * count].reshape(owners, names, count)
    vec = jnp.swapaxes(vec, 0, 1).reshape(names, owners * count)[:, :D].astype(F32)
    b1 = rows[:, names * count : names * count + wide].reshape(1, -1)[:, :FF].astype(F32)
    return jnp.pad(vec, ((0, 16 - names), (0, 0))), jnp.broadcast_to(b1, (8, FF))


VECTORS = ("qb", "vb", "ob", "g1", "s1", "g2", "s2", "b2")


def vector_grads(small, weights, count, wide, d_max, ff_max):
    me = lax.axis_index("fsdp")
    rows = jnp.pad(small, ((0, 0), (0, d_max - D)))
    rows = lax.dynamic_slice(rows, (0, me * count), (small.shape[0], count))
    grads = {name: rows[i] for i, name in enumerate(VECTORS)}
    wide_at = len(VECTORS)
    b1 = jnp.pad(small[wide_at : wide_at + FF // D].reshape(-1), (0, ff_max - FF))
    grads["b1"] = lax.dynamic_slice(b1, (me * wide,), (wide,))
    sums = small[wide_at + FF // D :]
    total = sum(weight[:, :D].astype(F32) * sums[i : i + 1] for i, weight in enumerate(weights))
    within = me * count + jnp.arange(count, dtype=jnp.int32) < D
    grads["m"] = jnp.where(within, jnp.sum(total, axis=1), 0.0) + rows[-1]
    return grads


def in_columns(weight):
    return [weight[:, j * D : (j + 1) * D] for j in range(FF // D)]


def any_grid(grid, frames, cotangent, span_starts, matrices, vectors, up_bias):
    query, key, value, out, up, down = matrices
    count, wide = query.shape[0], down.shape[0]
    owners = grid.fsdp
    d_max, ff_max = count * owners, wide * owners
    me, core = lax.axis_index("fsdp"), lax.axis_index("dp") % 2
    codes = me ^ jnp.arange(owners, dtype=jnp.int32)

    def gathered(pieces):
        stack = in_order(grid.gather(jnp.concatenate(pieces)), codes)
        stack = stack.reshape(owners, len(pieces), -1, D)
        return [stack[:, i].reshape(-1, D) for i in range(len(pieces))]

    packed = jnp.concatenate(vectors + [up_bias]).reshape(1, -1)
    packed = in_order(grid.gather(packed)[:, 0], codes)
    vec, b1 = packed_vectors(packed, count, wide, len(vectors))
    wq, wk, wv, wo = gathered([piece[:, :D] for piece in (query, key, value, out)])
    up_blocks = gathered(in_columns(up))
    (w2,) = gathered([down[:, :D]])

    def unit(role_zero, role_one):
        first = core == 0
        return ([jnp.where(first, role_zero, role_one)[None]], [jnp.where(first, role_one, role_zero)[None]])

    quarter = lax.axis_index("dp") % 4
    stacked = jnp.stack([wq, wk, wv, wo])
    attn = [[lax.dynamic_slice_in_dim(stacked, quarter ^ flip, 1)] for flip in (0, 2, 1, 3)]
    up_unit = unit(jnp.concatenate(up_blocks[:2]), jnp.concatenate(up_blocks[2:]))
    down_unit = unit(w2[: ff_max // 2], w2[ff_max // 2 :])
    place = jnp.stack([core, jnp.zeros_like(core), quarter // 2])
    layer = Layer(place, span_starts[:, None, :], frames, vec, b1, d_max, ff_max, d_max, ff_max, False)
    q, k, v, o, lse, n1, rstd = layer.attn_forward(attn)
    hidden, slope = layer.ffn_up(up_unit, n1)
    output, dz, dr2, small2, down_grad = layer.ffn_down(down_unit, n1, hidden, cotangent, False)
    dr1, do, small1, wide_small, *up_out = layer.ffn_backward(
        attn, up_unit, down_unit, n1, rstd, dz, dr2, slope, o
    )
    dq, dk, dv, small_a, *qkv = layer.attn_backward(q, k, v, do, lse)
    frames_grad = layer.input_backward(attn, dr1, (dq, dk, dv))[0]
    small = grid.total(small_total(place, small_a, small1, small2, wide_small))

    def reduced(grads):
        total = grid.reduce(jnp.concatenate([grad.reshape(owners, -1, D) for grad in grads], axis=1))
        return [part for part in total.reshape(len(grads), -1, D)]

    def wide_rows(grad):
        return jnp.pad(grad, ((0, 0), (0, d_max - D)))

    sums = [wide_rows(grad) for grad in reduced(qkv)]
    up_out = reduced(up_out)
    sums.append(wide_rows(up_out[-1]))
    zeros = jnp.zeros((count, up.shape[1] - FF), F32)
    sums.append(jnp.concatenate(up_out[:-1] + [zeros], axis=1))
    sums.append(wide_rows(reduced([down_grad])[0]))
    return output, frames_grad, sums, vector_grads(small, matrices[:3], count, wide, d_max, ff_max)


def four_by_eight(grid, frames, cotangent, span_starts, matrices, vectors, up_bias):
    query, key, value, out, up, down = matrices
    count, wide = query.shape[0], down.shape[0]
    owners = grid.fsdp
    d_max, ff_max = count * owners, wide * owners
    me, dp_at = lax.axis_index("fsdp"), lax.axis_index("dp")
    core = dp_at % 2
    first = core == 0
    place = jnp.stack([core, me, dp_at // 2])

    packed = jnp.pad(jnp.stack(vectors), ((0, 0), (0, D - count)))
    packed = jnp.concatenate([packed, jnp.pad(up_bias, (0, D - wide))[None]])
    packed = jnp.pad(packed, ((0, 16 - packed.shape[0]), (0, 0)))
    half = wide // 2
    blocks = in_columns(up)
    stacked = jnp.stack([query[:, :D], key[:, :D], value[:, :D], out[:, :D]])
    attn_piece = jnp.concatenate([lax.dynamic_index_in_dim(stacked, dp_at, keepdims=False), packed])
    up_piece = jnp.where(first, jnp.concatenate(blocks[:2]), jnp.concatenate(blocks[2:]))
    down_piece = jnp.where(first, down[:half, :D], down[half:, :D])

    def other_core(value):
        return grid.swap(value, 1, 0)

    high, low = 4, 2
    far = grid.joined(grid.joined(attn_piece[None], high), low)
    far_along = grid.swap(far, 2, 0)
    near = grid.swap(far, 0, 1)
    up_far = grid.joined(tie(up_piece, far)[None], high)
    near_along = grid.swap(tie(near, far_along, up_far), 2, 0)
    attn = [[far, near], [far_along, near_along]]
    attn += [[other_core(value) for value in arrays] for arrays in attn]
    vec, b1 = unpack(place, [far, near], count, count, wide, len(vectors))
    down_far = grid.joined(tie(down_piece, up_far)[None], high)
    up_far = grid.joined(up_far, low)
    up_near = grid.swap(tie(up_far, near), 0, 1)

    layer = Layer(place, span_starts[:, None, :], frames, vec, b1, count, wide, d_max, ff_max, True)
    q, k, v, o, lse, n1, rstd = layer.attn_forward(attn, after=(up_far, down_far))
    down_far = grid.joined(tie(down_far, up_far), low, n1)
    down_near = grid.swap(tie(down_far, up_near), 0, 1)
    up_unit = [[up_far, up_near], [other_core(up_far), other_core(tie(up_near, down_far))]]
    hidden, slope = layer.ffn_up(up_unit, n1)
    down_unit = [[down_far, down_near], [other_core(down_far), other_core(tie(down_near, hidden))]]
    output, dz, dr2, small2, down_grad = layer.ffn_down(down_unit, n1, hidden, cotangent, False)
    down_sum = lax.psum_scatter(down_grad.reshape(owners, wide, D), "fsdp", scatter_dimension=0)
    dr1, do, small1, wide_small, *up_out = layer.ffn_backward(
        attn, up_unit, down_unit, n1, rstd, dz, dr2, slope, o
    )

    def spread(kept_half, sent_half, *before):
        parts = first_sums(place, kept_half, grid.swap(tie(sent_half, *before), 1, 0))
        return parts[0], [grid.swap(parts[j], 2 * (j % 2), j // 2) for j in range(1, 4)]

    def spread_far(*groups):
        parts = next_sums(place, *groups)
        return [parts[0]] + [grid.swap(parts[j], 0, 2 * j) for j in range(1, 4)]

    def quarters(total):
        along = grid.swap(total, 2, 0)
        return total, along, grid.swap(total, 1, 0), grid.swap(along, 1, 0)

    own_u, got_u = spread(*up_out)
    dq, dk, dv, small_q, *qkv = layer.attn_backward(q, k, v, do, lse, after=(own_u,))
    own_q, got_q = spread(*qkv, *got_u)
    far_u = spread_far([tie(own_u, own_q)] + got_u)
    small = small_total(place, tie(small_q, own_q), small1, small2, wide_small)
    frames_grad = layer.input_backward(attn, dr1, (dq, dk, dv), after=(far_u[0], small))[0]
    far_q = spread_far([tie(own_q, frames_grad)] + got_q)
    sum_u = last_sums([tie(far_u[0], far_q[0])] + far_u[1:])
    down_part = tie(down_sum, sum_u)
    for axis, mask in ((0, 1), (1, 2)):
        size = down_part.shape[-2] // 2
        mine = (dp_at // mask) % 2
        kept_part, sent = (
            lax.dynamic_slice_in_dim(down_part, at * size, size, down_part.ndim - 2) for at in (mine, 1 - mine)
        )
        down_part = (kept_part.astype(F32) + grid.swap(sent, mask, 0).astype(F32)).astype(BF16)
    total_u = quarters(jnp.concatenate([sum_u, down_part.reshape(-1, D)]))
    sum_q = last_sums([far_q[0]] + [tie(part, total_u[0]) for part in far_q[1:]])
    small = grid.total(small, ((frames_grad,), far_q[1:], (sum_q,)))
    quarter = count // 4
    blocks_up = FF // D
    up_sum, out_sum, down_out = finish(
        place, [total_u],
        [
            (count, up.shape[1], [(0, j * quarter, j * D) for j in range(blocks_up)]),
            (count, d_max, [(0, blocks_up * quarter, 0)]),
            (wide, d_max, [(0, (blocks_up + 1) * quarter, 0)]),
        ],
    )
    along_q = grid.swap(sum_q, 2, 0)
    total_q = [sum_q, along_q, other_core(sum_q), other_core(tie(along_q, up_sum))]
    qkv_sums = finish(place, [total_q], [(count, d_max, [(0, j * quarter, 0)]) for j in range(3)])
    sums = list(qkv_sums) + [out_sum, up_sum, down_out]
    return output, frames_grad, sums, vector_grads(small, matrices[:3], count, wide, d_max, ff_max)


def on_device(
    sizes, frames, cotangent, span_starts, query_weight, key_weight, value_weight, out_weight,
    query_bias, value_bias, out_bias, first_gain, first_shift, up_weight, up_bias, down_weight,
    down_bias, second_gain, second_shift, mask_vector,
):
    grid = Grid(*sizes)
    matrices = (query_weight, key_weight, value_weight, out_weight, up_weight, down_weight)
    vectors = [query_bias, value_bias, out_bias, first_gain, first_shift, mask_vector,
               second_gain, second_shift, down_bias]
    placed = sizes == (4, 8) and query_weight.shape[0] % 32 == 0
    program = four_by_eight if placed else any_grid
    output, frames_grad, sums, small = program(
        grid, frames, cotangent, span_starts, matrices, vectors, up_bias
    )
    return (
        output, frames_grad, *sums[:4], small["qb"], small["vb"], small["ob"], small["g1"], small["s1"],
        sums[4], small["b1"], sums[5], small["b2"], small["g2"], small["s2"], small["m"],
    )


def solution(mesh):
    sizes = (mesh.shape["dp"], mesh.shape["fsdp"])
    tokens = P(("dp", "fsdp"), None)
    matrix, vector = P("fsdp", None), P("fsdp")
    return jax.shard_map(
        functools.partial(on_device, sizes),
        mesh=mesh,
        in_specs=(tokens,) * 3 + (matrix,) * 4 + (vector,) * 5 + (matrix, vector, matrix) + (vector,) * 4,
        out_specs=(tokens,) * 2 + (matrix,) * 4 + (vector,) * 5 + (matrix, vector, matrix) + (vector,) * 4,
        check_vma=False,
    )
```

```python
import functools
import jax
import jax.numpy as jnp
from jax import lax
from jax.experimental import pallas as pl
from jax.experimental.pallas import tpu as pltpu
from jax.sharding import PartitionSpec as P

HEADS = 10
HEAD_DIM = 64
FF = 2560
D = 640
FRAMES = 400
SPAN = 10
PAIR = 2 * HEAD_DIM
EPS = 1e-05
F32 = jnp.float32
BF16 = jnp.bfloat16
VMEM_LIMIT = 60 * 1024 * 1024
HID = 256


def dot_nn(a, b):
    return lax.dot_general(a, b, (((1,), (0,)), ((), ())), preferred_element_type=F32)


def dot_nt(a, b):
    return lax.dot_general(a, b, (((1,), (1,)), ((), ())), preferred_element_type=F32)


def dot_tn(a, b):
    return lax.dot_general(a, b, (((0,), (0,)), ((), ())), preferred_element_type=F32)


def mean_last(a):
    return jnp.mean(a, axis=-1, keepdims=True)


def rows_sum(a):
    return jnp.sum(a, axis=0, keepdims=True)


def masked_frames(starts_ref):
    places = lax.broadcasted_iota(jnp.int32, (FRAMES, starts_ref.shape[-1]), 0)
    ahead = places - starts_ref[0]
    inside = jnp.where((ahead >= 0) & (ahead < SPAN), 1.0, 0.0)
    return jnp.max(inside, axis=1, keepdims=True) > 0.5


def far_codes(pieces):
    codes = [0]
    for bit in reversed(range(pieces.bit_length() - 1)):
        codes += [code | 1 << bit for code in codes]
    return codes


def fetch(place_ref, sem, *wanted):
    def copies(unit, parts, role):
        flips = (0, 1) if len(unit) == 2 else (0, 2, 1, 3)
        for arrays, flip in zip(unit, flips):
            for group, source in enumerate(arrays):
                for piece, code in enumerate(far_codes(source.shape[0])):
                    owner = place_ref[1] ^ (code * len(arrays) + group)
                    for share, first, rows, stride, row, column, target in parts:
                        if share == (role % len(unit)) ^ flip:
                            low = pl.multiple_of(owner * stride + row, 16)
                            yield pltpu.make_async_copy(
                                source.at[piece, pl.ds(first, rows), :],
                                target.at[pl.ds(low, rows), pl.ds(column, D)],
                                sem,
                            )

    for role in range(max(len(unit) for unit, _ in wanted)):
        here = place_ref[0] == role % 2
        if any(len(unit) > 2 for unit, _ in wanted):
            here = here & (place_ref[2] == role // 2)

        @pl.when(here)
        def _(role=role):
            started = [copy for unit, parts in wanted for copy in copies(unit, parts, role)]
            for copy in started:
                copy.start()
            for copy in started:
                copy.wait()


def attn_parts(rows, *targets):
    return [(share, 0, rows, rows, 0, 0, target) for share, target in enumerate(targets) if target is not None]


def up_parts(target, rows):
    return [(j // 2, (j % 2) * rows, rows, rows, 0, j * D, target) for j in range(FF // D)]


def down_parts(target, rows):
    return [(core, 0, rows // 2, rows, core * (rows // 2), 0, target) for core in (0, 1)]


def attn_forward(
    place_ref, attn, starts_ref, frames_ref, vec_ref,
    q_ref, k_ref, v_ref, o_ref, lse_ref, n1_ref, rstd_ref,
    wq_ref, wk_ref, wv_ref, wo_ref, sem, *, rows,
):
    @pl.when(pl.program_id(0) == 0)
    def _():
        fetch(place_ref, sem, (attn, attn_parts(rows, wq_ref, wk_ref, wv_ref, wo_ref)))

    bq, bv, bo = vec_ref[0:1, :], vec_ref[1:2, :], vec_ref[2:3, :]
    x0 = jnp.where(masked_frames(starts_ref), vec_ref[5:6, :], frames_ref[...].astype(F32))
    h = x0.astype(BF16)
    scale = HEAD_DIM ** (-0.5)
    q_ref[...] = ((dot_nn(h, wq_ref[0:D, :]) + bq).astype(BF16).astype(F32) * scale).astype(BF16)
    k_ref[...] = dot_nn(h, wk_ref[0:D, :]).astype(BF16)
    v_ref[...] = (dot_nn(h, wv_ref[0:D, :]) + bv).astype(BF16)
    low_lanes = lax.broadcasted_iota(jnp.int32, (FRAMES, PAIR), 1) < HEAD_DIM
    lanes = lax.broadcasted_iota(jnp.int32, (FRAMES, 128), 1)
    lse = jnp.zeros((FRAMES, 128), F32)
    for pair in range(HEADS // 2):
        cols = slice(pair * PAIR, (pair + 1) * PAIR)
        qp, kp, vp = q_ref[:, cols], k_ref[:, cols], v_ref[:, cols]
        parts = []
        for half in range(2):
            keep = low_lanes if half == 0 else jnp.logical_not(low_lanes)
            qh = jnp.where(keep, qp.astype(F32), 0.0).astype(BF16)
            scores = dot_nt(qh, kp)
            top = jnp.max(scores, axis=-1, keepdims=True)
            expo = jnp.exp(scores - top)
            total = jnp.sum(expo, axis=-1, keepdims=True)
            parts.append(dot_nn(expo.astype(BF16), vp) * (1.0 / total))
            lse = jnp.where(lanes == 2 * pair + half, top + jnp.log(total), lse)
        o_ref[:, cols] = jnp.where(low_lanes, parts[0], parts[1]).astype(BF16)
    lse_ref[0] = jnp.transpose(lse)[0:16, :]
    r1 = x0 + (dot_nn(o_ref[...], wo_ref[0:D, :]) + bo)
    center = r1 - mean_last(r1)
    rstd = lax.rsqrt(mean_last(center * center) + EPS)
    n1_ref[...] = center * rstd
    rstd_ref[...] = rstd


def gelu_parts(u):
    phi = 0.5 + 0.5 * lax.erf(u * 0.7071067811865476)
    return u * phi, phi + u * jnp.exp(u * u * -0.5) * 0.3989422804014327


def ffn_up(place_ref, up, n1_ref, vec_ref, b1_ref, hidden_ref, slope_ref, w1_ref, sem, *, rows):
    @pl.when(pl.program_id(0) == 0)
    def _():
        fetch(place_ref, sem, (up, up_parts(w1_ref, rows)))

    y1b = (vec_ref[3:4, :] * n1_ref[...] + vec_ref[4:5, :]).astype(BF16)
    for c in range(FF // HID):
        cols = slice(c * HID, (c + 1) * HID)
        u = dot_nn(y1b, w1_ref[0:D, cols]) + b1_ref[0:1, cols]
        act, slope = gelu_parts(u)
        hidden_ref[:, cols] = act.astype(BF16)
        slope_ref[:, cols] = slope.astype(BF16)


def ffn_down(
    place_ref, down, n1_ref, hidden_ref, cot_ref, vec_ref,
    out_ref, dz_ref, dr2_ref, small_ref, *rest, rows, halves,
):
    grads_refs, (acc, w2_ref, sem) = rest[:-3], rest[-3:]
    step = pl.program_id(0)

    @pl.when(step == 0)
    def _():
        small_ref[...] = jnp.zeros_like(small_ref)
        acc[...] = jnp.zeros_like(acc)
        fetch(place_ref, sem, (down, down_parts(w2_ref, rows)))

    g1, s1, g2, s2, b2 = (vec_ref[i : i + 1, :] for i in (3, 4, 6, 7, 8))
    y1 = g1 * n1_ref[...] + s1
    r2 = y1 + (dot_nn(hidden_ref[...], w2_ref[0:FF, :]) + b2)
    center = r2 - mean_last(r2)
    rstd = lax.rsqrt(mean_last(center * center) + EPS)
    n2 = center * rstd
    out_ref[...] = (n2 * g2 + s2).astype(BF16)
    dy = cot_ref[...].astype(F32)
    e = dy * g2
    dr2 = (e - mean_last(e) - n2 * mean_last(e * n2)) * rstd
    dz = dr2.astype(BF16)
    dr2_ref[...] = dr2
    dz_ref[...] = dz
    small_ref[0:1, :] += rows_sum(dz.astype(F32))
    small_ref[1:2, :] += rows_sum(dy * n2)
    small_ref[2:3, :] += rows_sum(dy)
    acc[0:FF, :] += dot_tn(hidden_ref[...], dz)

    @pl.when(step == pl.num_programs(0) - 1)
    def _():
        deliver(place_ref, grads_refs, [(acc, 0, rows)], halves)


def deliver(place_ref, refs, sources, halves, extra=None):
    if not halves:
        for ref, (acc, column, _) in zip(refs, sources):
            ref[...] = acc[:, column : column + ref.shape[1]].astype(BF16)
        return
    for ref, core in zip(refs, (place_ref[0], 1 - place_ref[0])):
        owners, parts, _, width = ref.shape
        for owner in range(owners):
            for part in range(parts):
                pieces = []
                for acc, column, rows in sources:
                    size = rows // 4
                    low = pl.multiple_of(owner * rows + (2 * core + part) * size, 8)
                    pieces.append(acc[pl.ds(low, size), column : column + width])
                if extra:
                    pieces.append(jnp.where(core == 0, extra(owner, part), 0.0))
                ref[owner, part] = jnp.concatenate(pieces, axis=0).astype(BF16)


def ffn_backward(
    place_ref, attn, up, down, starts_ref, n1_ref, rstd_ref, dz_ref, dr2_ref, slope_ref, o_ref, vec_ref,
    dr1_ref, do_ref, small_ref, db1_ref, *rest, rows, halves,
):
    grads_refs = rest[:-7]
    grad_pre, acc1, acco, w1_ref, w2_ref, wo_ref, sem = rest[-7:]
    step = pl.program_id(0)

    @pl.when(step == 0)
    def _():
        small_ref[...] = jnp.zeros_like(small_ref)
        db1_ref[...] = jnp.zeros_like(db1_ref)
        acc1[...] = jnp.zeros_like(acc1)
        acco[...] = jnp.zeros_like(acco)
        fetch(
            place_ref, sem,
            (attn, attn_parts(rows[0], None, None, None, wo_ref)), (up, up_parts(w1_ref, rows[0])), (down, down_parts(w2_ref, rows[1])),
        )

    g1, s1 = vec_ref[3:4, :], vec_ref[4:5, :]
    n1 = n1_ref[...]
    y1b = (g1 * n1 + s1).astype(BF16)
    dz = dz_ref[...]
    for c in range(FF // HID):
        cols = slice(c * HID, (c + 1) * HID)
        du = (dot_nt(dz, w2_ref[cols, :]) * slope_ref[:, cols].astype(F32)).astype(BF16)
        grad_pre[:, cols] = du
        db1_ref[0:1, cols] += rows_sum(du.astype(F32))
    acc1[0:D, :] += dot_tn(y1b, grad_pre[...])
    dy1 = dot_nt(grad_pre[...], w1_ref[0:D, :]) + dr2_ref[...]
    e = dy1 * g1
    dr1 = (e - mean_last(e) - n1 * mean_last(e * n1)) * rstd_ref[...]
    dr1_ref[...] = dr1
    da = dr1.astype(BF16)
    small_ref[0:1, :] += rows_sum(da.astype(F32))
    small_ref[1:2, :] += rows_sum(dy1 * n1)
    small_ref[2:3, :] += rows_sum(dy1)
    small_ref[3:4, :] += rows_sum(jnp.where(masked_frames(starts_ref), dr1, 0.0))
    acco[0:D, :] += dot_tn(o_ref[...], da)
    do_ref[...] = dot_nt(da, wo_ref[0:D, :]).astype(BF16)

    @pl.when(step == pl.num_programs(0) - 1)
    def _():
        sources = [(acc1, j * D, rows[0]) for j in range(FF // D)] + [(acco, 0, rows[0])]
        deliver(place_ref, grads_refs, sources, halves)


def attn_backward(
    place_ref, *rest, rows, halves,
):
    if halves:
        attn, (one_ref, two_ref, wide_ref), rest = rest[0], rest[1:4], rest[4:]
        rest, (wq_ref, wk_ref, wv_ref, sem) = rest[:-4], rest[-4:]
    starts_ref, frames_ref, vec_ref, q_ref, k_ref, v_ref, do_ref, lse_ref, *rest = rest
    dq_ref, dk_ref, dv_ref, small_ref, *rest = rest
    grads_refs, (accq, acck, accv) = rest[:-3], rest[-3:]
    step = pl.program_id(0)

    @pl.when(step == 0)
    def _():
        small_ref[...] = jnp.zeros_like(small_ref)
        accq[...] = jnp.zeros_like(accq)
        acck[...] = jnp.zeros_like(acck)
        accv[...] = jnp.zeros_like(accv)
        if halves:
            fetch(place_ref, sem, (attn, attn_parts(rows, wq_ref, wk_ref, wv_ref)))

    scale = HEAD_DIM ** (-0.5)
    low_lanes = lax.broadcasted_iota(jnp.int32, (FRAMES, PAIR), 1) < HEAD_DIM
    for pair in range(HEADS // 2):
        cols = slice(pair * PAIR, (pair + 1) * PAIR)
        qp, kp, vp, dop = q_ref[:, cols], k_ref[:, cols], v_ref[:, cols], do_ref[:, cols]
        parts = []
        for half in range(2):
            keep = low_lanes if half == 0 else jnp.logical_not(low_lanes)
            kh = jnp.where(keep, kp.astype(F32), 0.0).astype(BF16)
            vh = jnp.where(keep, vp.astype(F32), 0.0).astype(BF16)
            head = 2 * pair + half
            prob = jnp.exp(dot_nt(kh, qp) - lse_ref[0, head : head + 1, :])
            dprob = dot_nt(vh, dop)
            inner = jnp.sum(prob * dprob, axis=0, keepdims=True)
            dscore = (prob * (dprob - inner)).astype(BF16)
            parts.append((dot_nn(prob.astype(BF16), dop), dot_nn(dscore, qp), dot_tn(dscore, kp) * scale))
        for ref, one, two in zip((dv_ref, dk_ref, dq_ref), *parts):
            ref[:, cols] = jnp.where(low_lanes, one, two).astype(BF16)
    masked = masked_frames(starts_ref)
    h = jnp.where(masked, vec_ref[5:6, :], frames_ref[...].astype(F32)).astype(BF16)
    accq[0:D, :] += dot_tn(h, dq_ref[...])
    acck[0:D, :] += dot_tn(h, dk_ref[...])
    accv[0:D, :] += dot_tn(h, dv_ref[...])
    small_ref[0:1, :] += rows_sum(dq_ref[...].astype(F32))
    small_ref[1:2, :] += rows_sum(dv_ref[...].astype(F32))
    for row, ref in enumerate((dq_ref, dk_ref, dv_ref), 2):
        small_ref[row : row + 1, :] += rows_sum(jnp.where(masked, ref[...].astype(F32), 0.0))

    @pl.when(step == pl.num_programs(0) - 1)
    def _():
        extra = None
        if halves:
            first, second, wide = one_ref[...], two_ref[...], wide_ref[0:1, :]
            mask_row = first[3:4]
            for row, weight in enumerate((wq_ref, wk_ref, wv_ref), 2):
                line = jnp.broadcast_to(small_ref[row : row + 1, :], (8, D))
                upper = line.astype(BF16)
                lower = (line - upper.astype(F32)).astype(BF16)
                product = dot_nt(upper, weight[0:D, :]) + dot_nt(lower, weight[0:D, :])
                mask_row = mask_row + product[0:1]
            owners = grads_refs[0].shape[0]
            lines = jnp.concatenate([small_ref[0:2, :], first[0:3], second[1:3], second[0:1]], axis=0)
            lines = jnp.concatenate([lines, jnp.zeros((8, owners * rows - D), F32)], axis=1)
            mask_row = jnp.concatenate([mask_row, jnp.zeros((1, owners * rows - D), F32)], axis=1)
            count = wide_ref.shape[1] // FF * rows * (FF // D)
            wide = jnp.concatenate([wide, jnp.zeros((1, owners * count - FF), F32)], axis=1)

            def filled(line):
                return jnp.concatenate([line, jnp.zeros((line.shape[0], D - line.shape[1]), F32)], axis=1)

            def extra(owner, part):
                if part == 0:
                    return filled(lines[:, owner * rows : (owner + 1) * rows])
                return jnp.concatenate(
                    [
                        filled(mask_row[:, owner * rows : (owner + 1) * rows]),
                        filled(wide[:, owner * count : (owner + 1) * count]),
                        jnp.zeros((6, D), F32),
                    ],
                    axis=0,
                )

        deliver(place_ref, grads_refs, [(acc, 0, rows) for acc in (accq, acck, accv)], halves, extra)


def input_backward(
    place_ref, attn, starts_ref, dr1_ref, *rest, rows,
):
    parts, (grad_ref, wq_ref, wk_ref, wv_ref, sem) = rest[:-5], rest[-5:]

    @pl.when(pl.program_id(0) == 0)
    def _():
        fetch(place_ref, sem, (attn, attn_parts(rows, wq_ref, wk_ref, wv_ref)))

    masked = masked_frames(starts_ref)
    dx0 = dr1_ref[...]
    for grad, weight in zip(parts, (wq_ref, wk_ref, wv_ref)):
        dx0 += dot_nt(grad[...], weight[0:D, :])
    grad_ref[...] = jnp.where(masked, 0.0, dx0).astype(BF16)


def row_blocks(width):
    return pl.BlockSpec((FRAMES, width), lambda i, *_: (i, 0))


def kept(rows, cols):
    return pl.BlockSpec((rows, cols), lambda i, *_: (0, 0), pipeline_mode=pl.Buffered(1))


def held(*sizes):
    return pl.BlockSpec(sizes, lambda i, *_: (0,) * len(sizes))


def shape(*sizes, dtype=BF16):
    return jax.ShapeDtypeStruct(sizes, dtype)


SCALARS = pl.BlockSpec(memory_space=pltpu.SMEM)
WHOLE = pl.BlockSpec(memory_space=pl.ANY)
COPIES = pltpu.SemaphoreType.DMA(())


def call(
    body, steps, place, units, operands, in_specs, outputs, scratch=(), after=(), flops=0, moved=0,
):
    flat = [array for unit in units for arrays in unit for array in arrays]

    def kernel(place_ref, *refs):
        refs = refs[len(after) :]
        given = []
        for unit in units:
            given.append([])
            for arrays in unit:
                given[-1].append(refs[: len(arrays)])
                refs = refs[len(arrays) :]
        body(place_ref, *given, *refs)

    return pl.pallas_call(
        kernel,
        grid=(steps,),
        in_specs=[SCALARS] + [WHOLE] * (len(after) + len(flat)) + in_specs,
        out_specs=[spec for spec, _ in outputs],
        out_shape=[out for _, out in outputs],
        scratch_shapes=list(scratch),
        compiler_params=pltpu.CompilerParams(
            dimension_semantics=("arbitrary",), vmem_limit_bytes=VMEM_LIMIT
        ),
        cost_estimate=pl.CostEstimate(flops=int(flops), bytes_accessed=int(moved), transcendentals=0),
    )(place, *after, *flat, *operands)


def starts_spec(starts):
    return pl.BlockSpec((1, 1, starts.shape[-1]), lambda i: (i, 0, 0))


def lse_spec():
    return pl.BlockSpec((1, 16, FRAMES), lambda i: (i, 0, 0))


def weights(*sizes):
    return [pltpu.VMEM(size, BF16) for size in sizes] + [COPIES]


def by_rows(rows, width, dtype=BF16):
    return (row_blocks(width), shape(rows, width, dtype=dtype))


def summed(rows, width):
    return (held(rows, width), shape(rows, width, dtype=F32))


def grads_out(halves, sources, extra=0):
    if not halves:
        return [(held(rows, width), shape(rows, width)) for rows, width, _ in sources]
    rows, width, count = sources[0]
    sizes = (rows // count, 2, sum(part[2] for part in sources) // 4 + extra, width)
    return [(held(*sizes), shape(*sizes))] * 2


class Layer:
    def __init__(self, place, starts, frames, vec, b1, d_rows, ff_rows, d_max, ff_max, halves):
        self.place, self.starts, self.frames, self.vec, self.b1 = place, starts, frames, vec, b1
        self.d_rows, self.ff_rows, self.d_max, self.ff_max, self.halves = d_rows, ff_rows, d_max, ff_max, halves
        self.rows = frames.shape[0]
        self.steps = self.rows // FRAMES

    def attn_forward(self, attn, after=()):
        rows = self.rows
        return call(
            functools.partial(attn_forward, rows=self.d_rows), self.steps, self.place, (attn,),
            (self.starts, self.frames, self.vec), [starts_spec(self.starts), row_blocks(D), kept(16, D)],
            [by_rows(rows, D)] * 4
            + [(lse_spec(), shape(self.steps, 16, FRAMES, dtype=F32)), by_rows(rows, D, F32), by_rows(rows, 1, F32)],
            weights(*[(self.d_max, D)] * 4), after,
            flops=rows * D * D * 8 + rows * FRAMES * D * 16, moved=rows * D * 14,
        )

    def ffn_up(self, up, n1, after=()):
        rows = self.rows
        return call(
            functools.partial(ffn_up, rows=self.d_rows), self.steps, self.place, (up,),
            (n1, self.vec, self.b1), [row_blocks(D), kept(16, D), kept(8, FF)],
            [by_rows(rows, FF)] * 2, weights((self.d_max, FF)), after,
            flops=rows * D * FF * 4, moved=rows * FF * 6,
        )

    def ffn_down(self, down, n1, hidden, cotangent, halves, after=()):
        rows = self.rows
        return call(
            functools.partial(ffn_down, rows=self.ff_rows, halves=halves), self.steps, self.place, (down,),
            (n1, hidden, cotangent, self.vec), [row_blocks(D), row_blocks(FF), row_blocks(D), kept(16, D)],
            [by_rows(rows, D), by_rows(rows, D), by_rows(rows, D, F32), summed(8, D)]
            + grads_out(halves, [(self.ff_max, D, self.ff_rows)]),
            [pltpu.VMEM((self.ff_max, D), F32)] + weights((self.ff_max, D)), after,
            flops=rows * D * FF * 6, moved=rows * FF * 8,
        )

    def ffn_backward(self, attn, up, down, n1, rstd, dz, dr2, slope, o, after=()):
        rows = self.rows
        return call(
            functools.partial(ffn_backward, rows=(self.d_rows, self.ff_rows), halves=self.halves),
            self.steps, self.place, (attn, up, down),
            (self.starts, n1, rstd, dz, dr2, slope, o, self.vec),
            [starts_spec(self.starts)] + [row_blocks(w) for w in (D, 1, D, D, FF, D)] + [kept(16, D)],
            [by_rows(rows, D, F32), by_rows(rows, D), summed(8, D), summed(8, FF)]
            + grads_out(
                self.halves,
                [(self.d_max, D, self.d_rows)] * 5,
            ),
            [pltpu.VMEM((FRAMES, FF), BF16), pltpu.VMEM((self.d_max, FF), F32), pltpu.VMEM((self.d_max, D), F32)]
            + weights((self.d_max, FF), (self.ff_max, D), (self.d_max, D)), after,
            flops=rows * D * FF * 8 + rows * D * D * 4, moved=rows * FF * 8,
        )

    def attn_backward(self, q, k, v, do, lse, attn=None, vectors=(), after=()):
        rows = self.rows
        own = [row_blocks(D)] * 4
        return call(
            functools.partial(attn_backward, rows=self.d_rows, halves=self.halves),
            self.steps, self.place, (attn,) if attn else (),
            (*vectors, self.starts, self.frames, self.vec, q, k, v, do, lse),
            [kept(*vector.shape) for vector in vectors]
            + [starts_spec(self.starts), row_blocks(D), kept(16, D)] + own + [lse_spec()],
            [by_rows(rows, D)] * 3 + [summed(8, D)]
            + grads_out(self.halves, [(self.d_max, D, self.d_rows)] * 3, 8),
            [pltpu.VMEM((self.d_max, D), F32)] * 3 + (weights(*[(self.d_max, D)] * 3) if attn else []), after,
            flops=rows * D * D * 6 + rows * FRAMES * D * 40, moved=rows * D * 14,
        )

    def input_backward(self, attn, dr1, parts, after=()):
        rows = self.rows
        return call(
            functools.partial(input_backward, rows=self.d_rows), self.steps, self.place, (attn,),
            (self.starts, dr1, *parts),
            [starts_spec(self.starts), row_blocks(D)] + [row_blocks(part.shape[1]) for part in parts],
            [by_rows(rows, D)], weights(*[(self.d_max, D)] * 3), after,
            flops=rows * D * D * 8, moved=rows * D * 12,
        )


def local(kernel, outputs, place, operands, scratch=(), cost=0):
    count = len(operands)

    def body(place_ref, *refs):
        sources, outs = refs[:count], refs[count : count + len(outputs)]
        held_refs, sems = refs[count + len(outputs) : -1], refs[-1]
        copies = [
            pltpu.make_async_copy(source, target, sems.at[i])
            for i, (source, target) in enumerate(zip(sources, held_refs))
        ]
        for copy in copies:
            copy.start()
        for copy in copies:
            copy.wait()
        kernel(place_ref, held_refs, outs)

    vmem = pl.BlockSpec(memory_space=pltpu.VMEM)
    return pl.pallas_call(
        body,
        in_specs=[SCALARS] + [WHOLE] * count,
        out_specs=[vmem] * len(outputs),
        out_shape=outputs,
        scratch_shapes=[pltpu.VMEM(array.shape, array.dtype) for array in operands]
        + [pltpu.SemaphoreType.DMA((count,))],
        compiler_params=pltpu.CompilerParams(
            vmem_limit_bytes=4 * 2**20 + sum(4 * a.size for a in operands) + sum(4 * a.size for a in outputs)
        ),
        cost_estimate=pl.CostEstimate(flops=1000, bytes_accessed=4 * sum(a.size for a in operands), transcendentals=0),
    )(place, *operands)


def first_sums(place, kept_half, received):
    owners, _, rows, width = kept_half.shape

    def kernel(place_ref, refs, outs):
        for j in range(4):
            for z in range(owners // 2):
                owner, part = 2 * z + ((place_ref[1] % 2) ^ (j // 2)), place_ref[2] ^ (j % 2)
                outs[j][z] = (refs[0][owner, part].astype(F32) + refs[1][owner, part].astype(F32)).astype(BF16)

    return local(kernel, [shape(owners // 2, rows, width)] * 4, place, [kept_half, received])


def next_sums(place, parts, arrays):
    def kernel(place_ref, refs, outs):
        for j in range(4):
            piece = (place_ref[1] // 2) ^ j
            total = refs[0][piece].astype(F32)
            for ref in refs[1:]:
                total = total + ref[piece].astype(F32)
            outs[j * arrays // 4][j % (4 // arrays)] = total.astype(BF16)

    return local(kernel, [shape(4 // arrays, *parts[0].shape[1:])] * arrays, place, parts)


def finish(place, groups, outputs):
    flat = [array for group in groups for array in group]
    outs_shape = [shape(rows, cols, dtype=F32) for rows, cols, _ in outputs]

    def kernel(place_ref, refs, outs):
        for ref, (rows, cols, sources) in zip(outs, outputs):
            filled = len(sources) * D
            if cols > filled:
                ref[:, filled:] = jnp.zeros((rows, cols - filled), F32)
            size = rows // 4
            for group, row, column in sources:
                for j in range(4):
                    quarter = 2 * (place_ref[0] ^ (j // 2)) + (place_ref[2] ^ (j % 2))
                    value = refs[4 * group + j][...].astype(F32)
                    low = pl.multiple_of(quarter * size, 8)
                    ref[pl.ds(low, size), column : column + D] = value[row : row + size]

    return local(kernel, outs_shape, place, flat)


def unpack(place, stacks, first, count, wide, names):
    owners = 2 * stacks[0].shape[0]

    def kernel(place_ref, refs, outs):
        vec_ref, wide_ref = outs
        lanes = lax.broadcasted_iota(jnp.int32, (16, owners * count), 1)
        total = jnp.zeros((16, owners * count), F32)
        codes = far_codes(owners // 2)
        for code in range(owners):
            owner = place_ref[1] ^ code
            rows = refs[code % 2][codes.index(code // 2), first : first + 16, :].astype(F32)
            row = jnp.pad(rows[:, :count], ((0, 0), (0, (owners - 1) * count)))
            total = total + pltpu.roll(row, owner * count, 1)
            wide_ref[:, pl.ds(pl.multiple_of(owner * wide, 128), wide)] = jnp.broadcast_to(
                rows[names : names + 1, :wide], (8, wide)
            )
        vec_ref[...] = total[:, :D]

    return local(
        kernel, [shape(16, D, dtype=F32), shape(8, owners * wide, dtype=F32)], place, stacks
    )


def small_total(place, attn, one, two, wide):
    def kernel(place_ref, refs, outs):
        both, first, second, broad = (ref[...] for ref in refs)
        rows = [both[0:2], first[0:3], second[1:3], second[0:1]]
        rows += [broad[0:1, j * D : (j + 1) * D] for j in range(FF // D)]
        rows += [both[2:5], first[3:4]]
        row = 0
        for part in rows:
            outs[0][row : row + part.shape[0], :] = part
            row += part.shape[0]

    return local(kernel, [shape(16, D, dtype=F32)], place, [attn, one, two, wide])[0]


def last_sums(parts):
    return sum(part.astype(F32) for part in parts).astype(BF16)


def tie(value, *before):
    return lax.optimization_barrier((value, *before))[0]


def in_order(value, order):
    return jnp.concatenate([lax.dynamic_slice_in_dim(value, order[i], 1) for i in range(value.shape[0])])


class Grid:
    def __init__(self, dp, fsdp):
        self.dp, self.fsdp = dp, fsdp
        self.dp_bits = [1 << i for i in range(dp.bit_length() - 1)]
        self.fsdp_bits = [1 << i for i in range(fsdp.bit_length() - 1)]

    def bit(self, axis, bit):
        return (lax.axis_index(axis) // bit) % 2

    def swap(self, value, dp_mask, fsdp_mask):
        if not dp_mask:
            return lax.ppermute(value, "fsdp", [(i, i ^ fsdp_mask) for i in range(self.fsdp)])
        if not fsdp_mask:
            return lax.ppermute(value, "dp", [(i, i ^ dp_mask) for i in range(self.dp)])
        pairs = [
            (i * self.fsdp + j, (i ^ dp_mask) * self.fsdp + (j ^ fsdp_mask))
            for i in range(self.dp)
            for j in range(self.fsdp)
        ]
        return lax.ppermute(value, ("dp", "fsdp"), pairs)

    def gather(self, piece):
        gathered = piece[None]
        for bit in self.fsdp_bits:
            gathered = jnp.concatenate([gathered, self.swap(gathered, 0, bit)])
        return gathered

    def joined(self, stack, bit, *before):
        other = self.swap(stack, 0, bit)
        return jnp.concatenate([stack, tie(other, *before) if before else other])

    def stages(self):
        dp_left, fsdp_left = self.dp_bits[1:], list(self.fsdp_bits)
        order = [[("dp", 1)]]
        while dp_left and fsdp_left:
            order.append([("dp", dp_left.pop(0)), ("fsdp", fsdp_left.pop(0))])
        order += [[("dp", bit)] for bit in dp_left]
        while fsdp_left:
            order.append([("fsdp", bit) for bit in fsdp_left[:2]])
            fsdp_left = fsdp_left[2:]
        return order

    def reduce(self, grads):
        rows, width = grads.shape[1:]
        left = list(reversed(self.fsdp_bits))
        value = grads.reshape((2,) * len(left) + (rows, width))
        halved = []
        for stage in self.stages():
            for axis, bit in stage:
                if axis == "dp":
                    value = value.reshape(value.shape[:-2] + (2, value.shape[-2] // 2, width))
                    halved.append(bit)
            spots = {}
            extra = len(left)
            for axis, bit in stage:
                if axis == "dp":
                    spots[(axis, bit)] = extra
                    extra += 1
                else:
                    spots[(axis, bit)] = left.index(bit)
            total = None
            for code in range(1 << len(stage)):
                starts = [0] * value.ndim
                sizes = list(value.shape)
                masks = {"dp": 0, "fsdp": 0}
                for place, (axis, bit) in enumerate(stage):
                    other = (code >> place) & 1
                    starts[spots[(axis, bit)]] = self.bit(axis, bit) ^ other
                    sizes[spots[(axis, bit)]] = 1
                    masks[axis] += bit * other
                part = lax.dynamic_slice(value, starts, sizes)
                if code:
                    part = self.swap(part, masks["dp"], masks["fsdp"])
                part = part.astype(F32)
                total = part if total is None else total + part
            total = jnp.squeeze(total, tuple(spots.values()))
            left = [bit for bit in left if ("fsdp", bit) not in spots]
            value = total.astype(BF16)
        for bit in reversed(halved):
            other = self.swap(value, bit, 0)
            first = self.bit("dp", bit) == 0
            value = jnp.concatenate([jnp.where(first, value, other), jnp.where(first, other, value)])
        return value.astype(F32)

    def total(self, value):
        masks = [(bit | 1, 0) for bit in reversed(self.dp_bits)] + [(1, bit) for bit in reversed(self.fsdp_bits)]
        for dp_mask, fsdp_mask in masks:
            value = value + self.swap(value, dp_mask, fsdp_mask)
        return value


def packed_vectors(rows, count, wide, names):
    owners = rows.shape[0]
    vec = rows[:, : names * count].reshape(owners, names, count)
    vec = jnp.swapaxes(vec, 0, 1).reshape(names, owners * count)[:, :D].astype(F32)
    b1 = rows[:, names * count : names * count + wide].reshape(1, -1)[:, :FF].astype(F32)
    return jnp.pad(vec, ((0, 16 - names), (0, 0))), jnp.broadcast_to(b1, (8, FF))


VECTORS = ("qb", "vb", "ob", "g1", "s1", "g2", "s2", "b2")


def vector_grads(small, weights, count, wide, d_max, ff_max):
    me = lax.axis_index("fsdp")
    rows = jnp.pad(small, ((0, 0), (0, d_max - D)))
    rows = lax.dynamic_slice(rows, (0, me * count), (small.shape[0], count))
    grads = {name: rows[i] for i, name in enumerate(VECTORS)}
    wide_at = len(VECTORS)
    b1 = jnp.pad(small[wide_at : wide_at + FF // D].reshape(-1), (0, ff_max - FF))
    grads["b1"] = lax.dynamic_slice(b1, (me * wide,), (wide,))
    sums = small[wide_at + FF // D :]
    total = sum(weight[:, :D].astype(F32) * sums[i : i + 1] for i, weight in enumerate(weights))
    within = me * count + jnp.arange(count, dtype=jnp.int32) < D
    grads["m"] = jnp.where(within, jnp.sum(total, axis=1), 0.0) + rows[-1]
    return grads


def in_columns(weight):
    return [weight[:, j * D : (j + 1) * D] for j in range(FF // D)]


def any_grid(grid, frames, cotangent, span_starts, matrices, vectors, up_bias):
    query, key, value, out, up, down = matrices
    count, wide = query.shape[0], down.shape[0]
    owners = grid.fsdp
    d_max, ff_max = count * owners, wide * owners
    me, core = lax.axis_index("fsdp"), lax.axis_index("dp") % 2
    codes = me ^ jnp.arange(owners, dtype=jnp.int32)

    def gathered(pieces):
        stack = in_order(grid.gather(jnp.concatenate(pieces)), codes)
        stack = stack.reshape(owners, len(pieces), -1, D)
        return [stack[:, i].reshape(-1, D) for i in range(len(pieces))]

    packed = jnp.concatenate(vectors + [up_bias]).reshape(1, -1)
    packed = in_order(grid.gather(packed)[:, 0], codes)
    vec, b1 = packed_vectors(packed, count, wide, len(vectors))
    wq, wk, wv, wo = gathered([piece[:, :D] for piece in (query, key, value, out)])
    up_blocks = gathered(in_columns(up))
    (w2,) = gathered([down[:, :D]])

    def unit(role_zero, role_one):
        first = core == 0
        return ([jnp.where(first, role_zero, role_one)[None]], [jnp.where(first, role_one, role_zero)[None]])

    quarter = lax.axis_index("dp") % 4
    stacked = jnp.stack([wq, wk, wv, wo])
    attn = [[lax.dynamic_slice_in_dim(stacked, quarter ^ flip, 1)] for flip in (0, 2, 1, 3)]
    up_unit = unit(jnp.concatenate(up_blocks[:2]), jnp.concatenate(up_blocks[2:]))
    down_unit = unit(w2[: ff_max // 2], w2[ff_max // 2 :])
    place = jnp.stack([core, jnp.zeros_like(core), quarter // 2])
    layer = Layer(place, span_starts[:, None, :], frames, vec, b1, d_max, ff_max, d_max, ff_max, False)
    q, k, v, o, lse, n1, rstd = layer.attn_forward(attn)
    hidden, slope = layer.ffn_up(up_unit, n1)
    output, dz, dr2, small2, down_grad = layer.ffn_down(down_unit, n1, hidden, cotangent, False)
    dr1, do, small1, wide_small, *up_out = layer.ffn_backward(
        attn, up_unit, down_unit, n1, rstd, dz, dr2, slope, o
    )
    dq, dk, dv, small_a, *qkv = layer.attn_backward(q, k, v, do, lse)
    frames_grad = layer.input_backward(attn, dr1, (dq, dk, dv))[0]
    small = grid.total(small_total(place, small_a, small1, small2, wide_small))

    def reduced(grads):
        total = grid.reduce(jnp.concatenate([grad.reshape(owners, -1, D) for grad in grads], axis=1))
        return [part for part in total.reshape(len(grads), -1, D)]

    def wide_rows(grad):
        return jnp.pad(grad, ((0, 0), (0, d_max - D)))

    sums = [wide_rows(grad) for grad in reduced(qkv)]
    up_out = reduced(up_out)
    sums.append(wide_rows(up_out[-1]))
    zeros = jnp.zeros((count, up.shape[1] - FF), F32)
    sums.append(jnp.concatenate(up_out[:-1] + [zeros], axis=1))
    sums.append(wide_rows(reduced([down_grad])[0]))
    return output, frames_grad, sums, vector_grads(small, matrices[:3], count, wide, d_max, ff_max)


def four_by_eight(grid, frames, cotangent, span_starts, matrices, vectors, up_bias):
    query, key, value, out, up, down = matrices
    count, wide = query.shape[0], down.shape[0]
    owners = grid.fsdp
    d_max, ff_max = count * owners, wide * owners
    me, dp_at = lax.axis_index("fsdp"), lax.axis_index("dp")
    core = dp_at % 2
    first = core == 0
    place = jnp.stack([core, me, dp_at // 2])

    packed = jnp.pad(jnp.stack(vectors), ((0, 0), (0, D - count)))
    packed = jnp.concatenate([packed, jnp.pad(up_bias, (0, D - wide))[None]])
    packed = jnp.pad(packed, ((0, 16 - packed.shape[0]), (0, 0)))
    half = wide // 2
    blocks = in_columns(up)
    attn_piece = jnp.where(
        dp_at < 2, jnp.where(first, query[:, :D], key[:, :D]), jnp.where(first, value[:, :D], out[:, :D])
    )
    up_piece = jnp.where(first, jnp.concatenate(blocks[:2]), jnp.concatenate(blocks[2:]))
    down_piece = jnp.where(first, down[:half, :D], down[half:, :D])

    def other_core(value):
        return grid.swap(value, 1, 0)

    high, low = 4, 2
    attn_pairs = grid.joined(attn_piece[None], high)
    attn_pairs = jnp.concatenate([attn_pairs, grid.joined(packed[None], high)], axis=1)
    far = grid.joined(attn_pairs, low)
    up_far = grid.joined(tie(up_piece, attn_pairs)[None], high)
    far = tie(far, up_far)
    far_along = grid.swap(far, 2, 0)
    near = grid.swap(far, 0, 1)
    near_along = grid.swap(tie(near, far_along), 2, 0)
    attn = [[far, near], [far_along, near_along]]
    attn += [[other_core(value) for value in arrays] for arrays in attn]
    vec, b1 = unpack(place, [far, near], count, count, wide, len(vectors))
    down_far = grid.joined(tie(down_piece, up_far)[None], high)
    up_far = grid.joined(tie(up_far, far), low)
    up_near = grid.swap(tie(up_far, near), 0, 1)

    layer = Layer(place, span_starts[:, None, :], frames, vec, b1, count, wide, d_max, ff_max, True)
    q, k, v, o, lse, n1, rstd = layer.attn_forward(attn, after=(up_far, down_far))
    down_far = grid.joined(tie(down_far, up_far), low, n1)
    down_near = grid.swap(tie(down_far, up_near), 0, 1)
    up_unit = [[up_far, up_near], [other_core(up_far), other_core(tie(up_near, down_far))]]
    hidden, slope = layer.ffn_up(up_unit, n1)
    down_unit = [[down_far, down_near], [other_core(down_far), other_core(tie(down_near, hidden))]]
    output, dz, dr2, small2, down_grad = layer.ffn_down(down_unit, n1, hidden, cotangent, False)
    down_sum = lax.psum_scatter(down_grad.reshape(owners, wide, D), "fsdp", scatter_dimension=0)
    dr1, do, small1, wide_small, *up_out = layer.ffn_backward(
        attn, up_unit, down_unit, n1, rstd, dz, dr2, slope, o
    )

    def spread(kept_half, sent_half, *before):
        parts = first_sums(place, kept_half, grid.swap(tie(sent_half, *before), 1, 0))
        return parts[0], [grid.swap(parts[j], 2 * (j % 2), j // 2) for j in range(1, 4)]

    def spread_far(parts):
        pieces = next_sums(place, parts, 4)
        return [pieces[0]] + [grid.swap(pieces[j], 0, 2 * j) for j in range(1, 4)]

    def quarters(total):
        along = grid.swap(total, 2, 0)
        return total, along, grid.swap(total, 1, 0), grid.swap(along, 1, 0)

    own_u, got_u = spread(*up_out)
    dq, dk, dv, _, *qkv = layer.attn_backward(
        q, k, v, do, lse, attn, (small1, small2, wide_small), after=(own_u,)
    )
    own_q, got_q = spread(*qkv, *got_u)
    pair_u, sent_u = next_sums(place, [tie(own_u, own_q)] + got_u, 2)
    got_far_u = grid.swap(sent_u, 0, high)
    def halved(value, mask):
        size = value.shape[0] // 2
        mine = (dp_at // mask) % 2
        return [lax.dynamic_slice_in_dim(value, at * size, size) for at in (mine, 1 - mine)]

    kept_part, sent = halved(tie(down_sum, own_q), 1)
    down_half = last_sums([kept_part, grid.swap(sent, 1, 0)])
    kept_part, sent = halved(down_half, 2)
    got_down = grid.swap(sent, 2, 0)
    frames_grad = layer.input_backward(attn, dr1, (dq, dk, dv), after=(pair_u, down_half))[0]
    far_q = spread_far([tie(own_q, frames_grad)] + got_q)
    pair_u = last_sums([tie(pair_u, far_q[0]), got_far_u])
    sum_u = last_sums([tie(pair_u[0], *far_q[1:]), grid.swap(pair_u[1], 0, low)])
    down_part = last_sums([kept_part, tie(got_down, frames_grad)])
    total_u = quarters(jnp.concatenate([sum_u, down_part]))
    sum_q = last_sums(far_q)[0]
    quarter = count // 4
    blocks_up = FF // D
    up_sum, out_sum, down_out = finish(
        place, [total_u],
        [
            (count, up.shape[1], [(0, j * quarter, j * D) for j in range(blocks_up)]),
            (count, d_max, [(0, blocks_up * quarter, 0)]),
            (wide, d_max, [(0, (blocks_up + 1) * quarter, 0)]),
        ],
    )
    along_q = grid.swap(sum_q, 2, 0)
    total_q = [sum_q, along_q, other_core(sum_q), other_core(tie(along_q, up_sum))]
    *qkv_sums, small = finish(
        place, [total_q],
        [(count, d_max, [(0, j * quarter, 0)]) for j in range(3)] + [(32, D, [(0, 3 * quarter, 0)])],
    )
    vectors_out = {name: small[i, :count] for i, name in enumerate(VECTORS + ("m",))}
    vectors_out["b1"] = small[len(VECTORS) + 1, :wide]
    return output, frames_grad, [*qkv_sums, out_sum, up_sum, down_out], vectors_out


def on_device(
    sizes, frames, cotangent, span_starts, query_weight, key_weight, value_weight, out_weight,
    query_bias, value_bias, out_bias, first_gain, first_shift, up_weight, up_bias, down_weight,
    down_bias, second_gain, second_shift, mask_vector,
):
    grid = Grid(*sizes)
    matrices = (query_weight, key_weight, value_weight, out_weight, up_weight, down_weight)
    vectors = [query_bias, value_bias, out_bias, first_gain, first_shift, mask_vector,
               second_gain, second_shift, down_bias]
    placed = sizes == (4, 8) and query_weight.shape[0] % 32 == 0
    program = four_by_eight if placed else any_grid
    output, frames_grad, sums, small = program(
        grid, frames, cotangent, span_starts, matrices, vectors, up_bias
    )
    return (
        output, frames_grad, *sums[:4], small["qb"], small["vb"], small["ob"], small["g1"], small["s1"],
        sums[4], small["b1"], sums[5], small["b2"], small["g2"], small["s2"], small["m"],
    )


def solution(mesh):
    sizes = (mesh.shape["dp"], mesh.shape["fsdp"])
    tokens = P(("dp", "fsdp"), None)
    matrix, vector = P("fsdp", None), P("fsdp")
    return jax.shard_map(
        functools.partial(on_device, sizes),
        mesh=mesh,
        in_specs=(tokens,) * 3 + (matrix,) * 4 + (vector,) * 5 + (matrix, vector, matrix) + (vector,) * 4,
        out_specs=(tokens,) * 2 + (matrix,) * 4 + (vector,) * 5 + (matrix, vector, matrix) + (vector,) * 4,
        check_vma=False,
    )
```

```python
import functools
import jax
import jax.numpy as jnp
from jax import lax
from jax.experimental import pallas as pl
from jax.experimental.pallas import tpu as pltpu
from jax.sharding import PartitionSpec as P

HEADS = 10
HEAD_DIM = 64
FF = 2560
D = 640
FRAMES = 400
SPAN = 10
PAIR = 2 * HEAD_DIM
EPS = 1e-05
F32 = jnp.float32
BF16 = jnp.bfloat16
VMEM_LIMIT = 60 * 1024 * 1024
HID = 256


def dot_nn(a, b):
    return lax.dot_general(a, b, (((1,), (0,)), ((), ())), preferred_element_type=F32)


def dot_nt(a, b):
    return lax.dot_general(a, b, (((1,), (1,)), ((), ())), preferred_element_type=F32)


def dot_tn(a, b):
    return lax.dot_general(a, b, (((0,), (0,)), ((), ())), preferred_element_type=F32)


def mean_last(a):
    return jnp.mean(a, axis=-1, keepdims=True)


def rows_sum(a):
    return jnp.sum(a, axis=0, keepdims=True)


def masked_frames(starts_ref):
    places = lax.broadcasted_iota(jnp.int32, (FRAMES, starts_ref.shape[-1]), 0)
    ahead = places - starts_ref[0]
    inside = jnp.where((ahead >= 0) & (ahead < SPAN), 1.0, 0.0)
    return jnp.max(inside, axis=1, keepdims=True) > 0.5


def far_codes(pieces):
    codes = [0]
    for bit in reversed(range(pieces.bit_length() - 1)):
        codes += [code | 1 << bit for code in codes]
    return codes


def fetch(place_ref, sem, *wanted):
    def copies(unit, parts, role):
        flips = (0, 1) if len(unit) == 2 else (0, 2, 1, 3)
        for arrays, flip in zip(unit, flips):
            for group, source in enumerate(arrays):
                for piece, code in enumerate(far_codes(source.shape[0])):
                    owner = place_ref[1] ^ (code * len(arrays) + group)
                    for share, first, rows, stride, row, column, target in parts:
                        if share == (role % len(unit)) ^ flip:
                            low = pl.multiple_of(owner * stride + row, 16)
                            yield pltpu.make_async_copy(
                                source.at[piece, pl.ds(first, rows), :],
                                target.at[pl.ds(low, rows), pl.ds(column, D)],
                                sem,
                            )

    for role in range(max(len(unit) for unit, _ in wanted)):
        here = place_ref[0] == role % 2
        if any(len(unit) > 2 for unit, _ in wanted):
            here = here & (place_ref[2] == role // 2)

        @pl.when(here)
        def _(role=role):
            started = [copy for unit, parts in wanted for copy in copies(unit, parts, role)]
            for copy in started:
                copy.start()
            for copy in started:
                copy.wait()


def attn_parts(rows, *targets):
    return [(share, 0, rows, rows, 0, 0, target) for share, target in enumerate(targets) if target is not None]


def up_parts(target, rows):
    return [(j // 2, (j % 2) * rows, rows, rows, 0, j * D, target) for j in range(FF // D)]


def down_parts(target, rows):
    return [(core, 0, rows // 2, rows, core * (rows // 2), 0, target) for core in (0, 1)]


def attn_forward(
    place_ref, attn, starts_ref, frames_ref, vec_ref,
    q_ref, k_ref, v_ref, o_ref, lse_ref, n1_ref, rstd_ref,
    wq_ref, wk_ref, wv_ref, wo_ref, sem, *, rows,
):
    @pl.when(pl.program_id(0) == 0)
    def _():
        fetch(place_ref, sem, (attn, attn_parts(rows, wq_ref, wk_ref, wv_ref, wo_ref)))

    bq, bv, bo = vec_ref[0:1, :], vec_ref[1:2, :], vec_ref[2:3, :]
    x0 = jnp.where(masked_frames(starts_ref), vec_ref[5:6, :], frames_ref[...].astype(F32))
    h = x0.astype(BF16)
    scale = HEAD_DIM ** (-0.5)
    q_ref[...] = ((dot_nn(h, wq_ref[0:D, :]) + bq).astype(BF16).astype(F32) * scale).astype(BF16)
    k_ref[...] = dot_nn(h, wk_ref[0:D, :]).astype(BF16)
    v_ref[...] = (dot_nn(h, wv_ref[0:D, :]) + bv).astype(BF16)
    low_lanes = lax.broadcasted_iota(jnp.int32, (FRAMES, PAIR), 1) < HEAD_DIM
    lanes = lax.broadcasted_iota(jnp.int32, (FRAMES, 128), 1)
    lse = jnp.zeros((FRAMES, 128), F32)

    def scores_of(head):
        cols = slice(head // 2 * PAIR, (head // 2 + 1) * PAIR)
        keep = low_lanes if head % 2 == 0 else jnp.logical_not(low_lanes)
        qh = jnp.where(keep, q_ref[:, cols].astype(F32), 0.0).astype(BF16)
        return dot_nt(qh, k_ref[:, cols])

    ahead = scores_of(0)
    parts = []
    for head in range(HEADS):
        cols = slice(head // 2 * PAIR, (head // 2 + 1) * PAIR)
        scores = ahead
        if head + 1 < HEADS:
            ahead = scores_of(head + 1)
        top = jnp.max(scores, axis=-1, keepdims=True)
        expo = jnp.exp(scores - top)
        total = jnp.sum(expo, axis=-1, keepdims=True)
        parts.append(dot_nn(expo.astype(BF16), v_ref[:, cols]) * (1.0 / total))
        lse = jnp.where(lanes == head, top + jnp.log(total), lse)
        if head % 2:
            o_ref[:, cols] = jnp.where(low_lanes, parts[0], parts[1]).astype(BF16)
            parts = []
    lse_ref[0] = jnp.transpose(lse)[0:16, :]
    r1 = x0 + (dot_nn(o_ref[...], wo_ref[0:D, :]) + bo)
    center = r1 - mean_last(r1)
    rstd = lax.rsqrt(mean_last(center * center) + EPS)
    n1_ref[...] = center * rstd
    rstd_ref[...] = rstd


def gelu_parts(u):
    phi = 0.5 + 0.5 * lax.erf(u * 0.7071067811865476)
    return u * phi, phi + u * jnp.exp(u * u * -0.5) * 0.3989422804014327


def ffn_up(place_ref, up, n1_ref, vec_ref, b1_ref, hidden_ref, slope_ref, w1_ref, sem, *, rows):
    @pl.when(pl.program_id(0) == 0)
    def _():
        fetch(place_ref, sem, (up, up_parts(w1_ref, rows)))

    y1b = (vec_ref[3:4, :] * n1_ref[...] + vec_ref[4:5, :]).astype(BF16)
    for c in range(FF // HID):
        cols = slice(c * HID, (c + 1) * HID)
        u = dot_nn(y1b, w1_ref[0:D, cols]) + b1_ref[0:1, cols]
        act, slope = gelu_parts(u)
        hidden_ref[:, cols] = act.astype(BF16)
        slope_ref[:, cols] = slope.astype(BF16)


def ffn_down(
    place_ref, down, n1_ref, hidden_ref, cot_ref, vec_ref,
    out_ref, dz_ref, dr2_ref, small_ref, *rest, rows, halves,
):
    grads_refs, (acc, w2_ref, sem) = rest[:-3], rest[-3:]
    step = pl.program_id(0)

    @pl.when(step == 0)
    def _():
        small_ref[...] = jnp.zeros_like(small_ref)
        acc[...] = jnp.zeros_like(acc)
        fetch(place_ref, sem, (down, down_parts(w2_ref, rows)))

    g1, s1, g2, s2, b2 = (vec_ref[i : i + 1, :] for i in (3, 4, 6, 7, 8))
    y1 = g1 * n1_ref[...] + s1
    r2 = y1 + (dot_nn(hidden_ref[...], w2_ref[0:FF, :]) + b2)
    center = r2 - mean_last(r2)
    rstd = lax.rsqrt(mean_last(center * center) + EPS)
    n2 = center * rstd
    out_ref[...] = (n2 * g2 + s2).astype(BF16)
    dy = cot_ref[...].astype(F32)
    e = dy * g2
    dr2 = (e - mean_last(e) - n2 * mean_last(e * n2)) * rstd
    dz = dr2.astype(BF16)
    dr2_ref[...] = dr2
    dz_ref[...] = dz
    small_ref[0:1, :] += rows_sum(dz.astype(F32))
    small_ref[1:2, :] += rows_sum(dy * n2)
    small_ref[2:3, :] += rows_sum(dy)
    acc[0:FF, :] += dot_tn(hidden_ref[...], dz)

    @pl.when(step == pl.num_programs(0) - 1)
    def _():
        deliver(place_ref, grads_refs, [(acc, 0, rows)], halves)


def deliver(place_ref, refs, sources, halves, extra=None):
    if not halves:
        for ref, (acc, column, _) in zip(refs, sources):
            ref[...] = acc[:, column : column + ref.shape[1]].astype(BF16)
        return
    for ref, core in zip(refs, (place_ref[0], 1 - place_ref[0])):
        owners, parts, _, width = ref.shape
        for owner in range(owners):
            for part in range(parts):
                pieces = []
                for acc, column, rows in sources:
                    size = rows // 4
                    low = pl.multiple_of(owner * rows + (2 * core + part) * size, 8)
                    pieces.append(acc[pl.ds(low, size), column : column + width])
                if extra:
                    pieces.append(jnp.where(core == 0, extra(owner, part), 0.0))
                ref[owner, part] = jnp.concatenate(pieces, axis=0).astype(BF16)


def ffn_backward(
    place_ref, attn, up, down, starts_ref, n1_ref, rstd_ref, dz_ref, dr2_ref, slope_ref, o_ref, vec_ref,
    dr1_ref, do_ref, small_ref, db1_ref, *rest, rows, halves,
):
    grads_refs = rest[:-7]
    grad_pre, acc1, acco, w1_ref, w2_ref, wo_ref, sem = rest[-7:]
    step = pl.program_id(0)

    @pl.when(step == 0)
    def _():
        small_ref[...] = jnp.zeros_like(small_ref)
        db1_ref[...] = jnp.zeros_like(db1_ref)
        acc1[...] = jnp.zeros_like(acc1)
        acco[...] = jnp.zeros_like(acco)
        fetch(
            place_ref, sem,
            (attn, attn_parts(rows[0], None, None, None, wo_ref)), (up, up_parts(w1_ref, rows[0])), (down, down_parts(w2_ref, rows[1])),
        )

    g1, s1 = vec_ref[3:4, :], vec_ref[4:5, :]
    n1 = n1_ref[...]
    y1b = (g1 * n1 + s1).astype(BF16)
    dz = dz_ref[...]
    for c in range(FF // HID):
        cols = slice(c * HID, (c + 1) * HID)
        du = (dot_nt(dz, w2_ref[cols, :]) * slope_ref[:, cols].astype(F32)).astype(BF16)
        grad_pre[:, cols] = du
        db1_ref[0:1, cols] += rows_sum(du.astype(F32))
    acc1[0:D, :] += dot_tn(y1b, grad_pre[...])
    dy1 = dot_nt(grad_pre[...], w1_ref[0:D, :]) + dr2_ref[...]
    e = dy1 * g1
    dr1 = (e - mean_last(e) - n1 * mean_last(e * n1)) * rstd_ref[...]
    dr1_ref[...] = dr1
    da = dr1.astype(BF16)
    small_ref[0:1, :] += rows_sum(da.astype(F32))
    small_ref[1:2, :] += rows_sum(dy1 * n1)
    small_ref[2:3, :] += rows_sum(dy1)
    small_ref[3:4, :] += rows_sum(jnp.where(masked_frames(starts_ref), dr1, 0.0))
    acco[0:D, :] += dot_tn(o_ref[...], da)
    do_ref[...] = dot_nt(da, wo_ref[0:D, :]).astype(BF16)

    @pl.when(step == pl.num_programs(0) - 1)
    def _():
        sources = [(acc1, j * D, rows[0]) for j in range(FF // D)] + [(acco, 0, rows[0])]
        deliver(place_ref, grads_refs, sources, halves)


def attn_backward(
    place_ref, *rest, rows, halves,
):
    if halves:
        attn, (one_ref, two_ref, wide_ref), rest = rest[0], rest[1:4], rest[4:]
        rest, (wq_ref, wk_ref, wv_ref, sem) = rest[:-4], rest[-4:]
    starts_ref, frames_ref, vec_ref, q_ref, k_ref, v_ref, do_ref, lse_ref, *rest = rest
    dq_ref, dk_ref, dv_ref, small_ref, *rest = rest
    grads_refs, (accq, acck, accv) = rest[:-3], rest[-3:]
    step = pl.program_id(0)

    @pl.when(step == 0)
    def _():
        small_ref[...] = jnp.zeros_like(small_ref)
        accq[...] = jnp.zeros_like(accq)
        acck[...] = jnp.zeros_like(acck)
        accv[...] = jnp.zeros_like(accv)
        if halves:
            fetch(place_ref, sem, (attn, attn_parts(rows, wq_ref, wk_ref, wv_ref)))

    scale = HEAD_DIM ** (-0.5)
    low_lanes = lax.broadcasted_iota(jnp.int32, (FRAMES, PAIR), 1) < HEAD_DIM

    def products(head):
        cols = slice(head // 2 * PAIR, (head // 2 + 1) * PAIR)
        keep = low_lanes if head % 2 == 0 else jnp.logical_not(low_lanes)
        kh = jnp.where(keep, k_ref[:, cols].astype(F32), 0.0).astype(BF16)
        vh = jnp.where(keep, v_ref[:, cols].astype(F32), 0.0).astype(BF16)
        return dot_nt(kh, q_ref[:, cols]), dot_nt(vh, do_ref[:, cols])

    ahead = products(0)
    parts = []
    for head in range(HEADS):
        cols = slice(head // 2 * PAIR, (head // 2 + 1) * PAIR)
        scores, dprob = ahead
        if head + 1 < HEADS:
            ahead = products(head + 1)
        prob = jnp.exp(scores - lse_ref[0, head : head + 1, :])
        inner = jnp.sum(prob * dprob, axis=0, keepdims=True)
        dscore = (prob * (dprob - inner)).astype(BF16)
        parts.append(
            (
                dot_nn(prob.astype(BF16), do_ref[:, cols]),
                dot_nn(dscore, q_ref[:, cols]),
                dot_tn(dscore, k_ref[:, cols]) * scale,
            )
        )
        if head % 2:
            for ref, one, two in zip((dv_ref, dk_ref, dq_ref), *parts):
                ref[:, cols] = jnp.where(low_lanes, one, two).astype(BF16)
            parts = []
    masked = masked_frames(starts_ref)
    h = jnp.where(masked, vec_ref[5:6, :], frames_ref[...].astype(F32)).astype(BF16)
    accq[0:D, :] += dot_tn(h, dq_ref[...])
    acck[0:D, :] += dot_tn(h, dk_ref[...])
    accv[0:D, :] += dot_tn(h, dv_ref[...])
    small_ref[0:1, :] += rows_sum(dq_ref[...].astype(F32))
    small_ref[1:2, :] += rows_sum(dv_ref[...].astype(F32))
    for row, ref in enumerate((dq_ref, dk_ref, dv_ref), 2):
        small_ref[row : row + 1, :] += rows_sum(jnp.where(masked, ref[...].astype(F32), 0.0))

    @pl.when(step == pl.num_programs(0) - 1)
    def _():
        extra = None
        if halves:
            first, second, wide = one_ref[...], two_ref[...], wide_ref[0:1, :]
            mask_row = first[3:4]
            for row, weight in enumerate((wq_ref, wk_ref, wv_ref), 2):
                line = jnp.broadcast_to(small_ref[row : row + 1, :], (8, D))
                upper = line.astype(BF16)
                lower = (line - upper.astype(F32)).astype(BF16)
                product = dot_nt(upper, weight[0:D, :]) + dot_nt(lower, weight[0:D, :])
                mask_row = mask_row + product[0:1]
            owners = grads_refs[0].shape[0]
            lines = jnp.concatenate([small_ref[0:2, :], first[0:3], second[1:3], second[0:1]], axis=0)
            lines = jnp.concatenate([lines, jnp.zeros((8, owners * rows - D), F32)], axis=1)
            mask_row = jnp.concatenate([mask_row, jnp.zeros((1, owners * rows - D), F32)], axis=1)
            count = wide_ref.shape[1] // FF * rows * (FF // D)
            wide = jnp.concatenate([wide, jnp.zeros((1, owners * count - FF), F32)], axis=1)

            def filled(line):
                return jnp.concatenate([line, jnp.zeros((line.shape[0], D - line.shape[1]), F32)], axis=1)

            def extra(owner, part):
                if part == 0:
                    return filled(lines[:, owner * rows : (owner + 1) * rows])
                return jnp.concatenate(
                    [
                        filled(mask_row[:, owner * rows : (owner + 1) * rows]),
                        filled(wide[:, owner * count : (owner + 1) * count]),
                        jnp.zeros((6, D), F32),
                    ],
                    axis=0,
                )

        deliver(place_ref, grads_refs, [(acc, 0, rows) for acc in (accq, acck, accv)], halves, extra)


def input_backward(
    place_ref, attn, starts_ref, dr1_ref, *rest, rows,
):
    parts, (grad_ref, wq_ref, wk_ref, wv_ref, sem) = rest[:-5], rest[-5:]

    @pl.when(pl.program_id(0) == 0)
    def _():
        fetch(place_ref, sem, (attn, attn_parts(rows, wq_ref, wk_ref, wv_ref)))

    masked = masked_frames(starts_ref)
    dx0 = dr1_ref[...]
    for grad, weight in zip(parts, (wq_ref, wk_ref, wv_ref)):
        dx0 += dot_nt(grad[...], weight[0:D, :])
    grad_ref[...] = jnp.where(masked, 0.0, dx0).astype(BF16)


def row_blocks(width):
    return pl.BlockSpec((FRAMES, width), lambda i, *_: (i, 0))


def kept(rows, cols):
    return pl.BlockSpec((rows, cols), lambda i, *_: (0, 0), pipeline_mode=pl.Buffered(1))


def held(*sizes):
    return pl.BlockSpec(sizes, lambda i, *_: (0,) * len(sizes))


def shape(*sizes, dtype=BF16):
    return jax.ShapeDtypeStruct(sizes, dtype)


SCALARS = pl.BlockSpec(memory_space=pltpu.SMEM)
WHOLE = pl.BlockSpec(memory_space=pl.ANY)
COPIES = pltpu.SemaphoreType.DMA(())


def call(
    body, steps, place, units, operands, in_specs, outputs, scratch=(), after=(), flops=0, moved=0,
):
    flat = [array for unit in units for arrays in unit for array in arrays]

    def kernel(place_ref, *refs):
        refs = refs[len(after) :]
        given = []
        for unit in units:
            given.append([])
            for arrays in unit:
                given[-1].append(refs[: len(arrays)])
                refs = refs[len(arrays) :]
        body(place_ref, *given, *refs)

    return pl.pallas_call(
        kernel,
        grid=(steps,),
        in_specs=[SCALARS] + [WHOLE] * (len(after) + len(flat)) + in_specs,
        out_specs=[spec for spec, _ in outputs],
        out_shape=[out for _, out in outputs],
        scratch_shapes=list(scratch),
        compiler_params=pltpu.CompilerParams(
            dimension_semantics=("arbitrary",), vmem_limit_bytes=VMEM_LIMIT
        ),
        cost_estimate=pl.CostEstimate(flops=int(flops), bytes_accessed=int(moved), transcendentals=0),
    )(place, *after, *flat, *operands)


def starts_spec(starts):
    return pl.BlockSpec((1, 1, starts.shape[-1]), lambda i: (i, 0, 0))


def lse_spec():
    return pl.BlockSpec((1, 16, FRAMES), lambda i: (i, 0, 0))


def weights(*sizes):
    return [pltpu.VMEM(size, BF16) for size in sizes] + [COPIES]


def by_rows(rows, width, dtype=BF16):
    return (row_blocks(width), shape(rows, width, dtype=dtype))


def summed(rows, width):
    return (held(rows, width), shape(rows, width, dtype=F32))


def grads_out(halves, sources, extra=0):
    if not halves:
        return [(held(rows, width), shape(rows, width)) for rows, width, _ in sources]
    rows, width, count = sources[0]
    sizes = (rows // count, 2, sum(part[2] for part in sources) // 4 + extra, width)
    return [(held(*sizes), shape(*sizes))] * 2


class Layer:
    def __init__(self, place, starts, frames, vec, b1, d_rows, ff_rows, d_max, ff_max, halves):
        self.place, self.starts, self.frames, self.vec, self.b1 = place, starts, frames, vec, b1
        self.d_rows, self.ff_rows, self.d_max, self.ff_max, self.halves = d_rows, ff_rows, d_max, ff_max, halves
        self.rows = frames.shape[0]
        self.steps = self.rows // FRAMES

    def attn_forward(self, attn, after=()):
        rows = self.rows
        return call(
            functools.partial(attn_forward, rows=self.d_rows), self.steps, self.place, (attn,),
            (self.starts, self.frames, self.vec), [starts_spec(self.starts), row_blocks(D), kept(16, D)],
            [by_rows(rows, D)] * 4
            + [(lse_spec(), shape(self.steps, 16, FRAMES, dtype=F32)), by_rows(rows, D, F32), by_rows(rows, 1, F32)],
            weights(*[(self.d_max, D)] * 4), after,
            flops=rows * D * D * 8 + rows * FRAMES * D * 16, moved=rows * D * 14,
        )

    def ffn_up(self, up, n1, after=()):
        rows = self.rows
        return call(
            functools.partial(ffn_up, rows=self.d_rows), self.steps, self.place, (up,),
            (n1, self.vec, self.b1), [row_blocks(D), kept(16, D), kept(8, FF)],
            [by_rows(rows, FF)] * 2, weights((self.d_max, FF)), after,
            flops=rows * D * FF * 4, moved=rows * FF * 6,
        )

    def ffn_down(self, down, n1, hidden, cotangent, halves, after=()):
        rows = self.rows
        return call(
            functools.partial(ffn_down, rows=self.ff_rows, halves=halves), self.steps, self.place, (down,),
            (n1, hidden, cotangent, self.vec), [row_blocks(D), row_blocks(FF), row_blocks(D), kept(16, D)],
            [by_rows(rows, D), by_rows(rows, D), by_rows(rows, D, F32), summed(8, D)]
            + grads_out(halves, [(self.ff_max, D, self.ff_rows)]),
            [pltpu.VMEM((self.ff_max, D), F32)] + weights((self.ff_max, D)), after,
            flops=rows * D * FF * 6, moved=rows * FF * 8,
        )

    def ffn_backward(self, attn, up, down, n1, rstd, dz, dr2, slope, o, after=()):
        rows = self.rows
        return call(
            functools.partial(ffn_backward, rows=(self.d_rows, self.ff_rows), halves=self.halves),
            self.steps, self.place, (attn, up, down),
            (self.starts, n1, rstd, dz, dr2, slope, o, self.vec),
            [starts_spec(self.starts)] + [row_blocks(w) for w in (D, 1, D, D, FF, D)] + [kept(16, D)],
            [by_rows(rows, D, F32), by_rows(rows, D), summed(8, D), summed(8, FF)]
            + grads_out(
                self.halves,
                [(self.d_max, D, self.d_rows)] * 5,
            ),
            [pltpu.VMEM((FRAMES, FF), BF16), pltpu.VMEM((self.d_max, FF), F32), pltpu.VMEM((self.d_max, D), F32)]
            + weights((self.d_max, FF), (self.ff_max, D), (self.d_max, D)), after,
            flops=rows * D * FF * 8 + rows * D * D * 4, moved=rows * FF * 8,
        )

    def attn_backward(self, q, k, v, do, lse, attn=None, vectors=(), after=()):
        rows = self.rows
        own = [row_blocks(D)] * 4
        return call(
            functools.partial(attn_backward, rows=self.d_rows, halves=self.halves),
            self.steps, self.place, (attn,) if attn else (),
            (*vectors, self.starts, self.frames, self.vec, q, k, v, do, lse),
            [kept(*vector.shape) for vector in vectors]
            + [starts_spec(self.starts), row_blocks(D), kept(16, D)] + own + [lse_spec()],
            [by_rows(rows, D)] * 3 + [summed(8, D)]
            + grads_out(self.halves, [(self.d_max, D, self.d_rows)] * 3, 8),
            [pltpu.VMEM((self.d_max, D), F32)] * 3 + (weights(*[(self.d_max, D)] * 3) if attn else []), after,
            flops=rows * D * D * 6 + rows * FRAMES * D * 40, moved=rows * D * 14,
        )

    def input_backward(self, attn, dr1, parts, after=()):
        rows = self.rows
        return call(
            functools.partial(input_backward, rows=self.d_rows), self.steps, self.place, (attn,),
            (self.starts, dr1, *parts),
            [starts_spec(self.starts), row_blocks(D)] + [row_blocks(part.shape[1]) for part in parts],
            [by_rows(rows, D)], weights(*[(self.d_max, D)] * 3), after,
            flops=rows * D * D * 8, moved=rows * D * 12,
        )


def local(kernel, outputs, place, operands, wide=False):
    count = len(operands)

    def body(place_ref, *refs):
        sources, outs = refs[:count], refs[count : count + len(outputs)]
        held_refs, sems = refs[count + len(outputs) : -1], refs[-1]
        copies = [
            pltpu.make_async_copy(source, target, sems.at[i])
            for i, (source, target) in enumerate(zip(sources, held_refs))
        ]
        for copy in copies:
            copy.start()
        for copy in copies:
            copy.wait()
        kernel(place_ref, held_refs, outs)

    vmem = pl.BlockSpec(memory_space=pltpu.VMEM)
    return pl.pallas_call(
        body,
        in_specs=[SCALARS] + [WHOLE] * count,
        out_specs=[vmem] * len(outputs),
        out_shape=outputs,
        scratch_shapes=[pltpu.VMEM(array.shape, array.dtype) for array in operands]
        + [pltpu.SemaphoreType.DMA((count,))],
        compiler_params=pltpu.CompilerParams(
            vmem_limit_bytes=VMEM_LIMIT if wide else 4 * 2**20 + sum(4 * a.size for a in (*operands, *outputs))
        ),
        cost_estimate=pl.CostEstimate(flops=1000, bytes_accessed=4 * sum(a.size for a in operands), transcendentals=0),
    )(place, *operands)


def first_sums(place, kept_half, received, wide=False):
    owners, _, rows, width = kept_half.shape

    def kernel(place_ref, refs, outs):
        for j in range(4):
            for z in range(owners // 2):
                owner, part = 2 * z + ((place_ref[1] % 2) ^ (j // 2)), place_ref[2] ^ (j % 2)
                outs[j][z] = (refs[0][owner, part].astype(F32) + refs[1][owner, part].astype(F32)).astype(BF16)

    return local(kernel, [shape(owners // 2, rows, width)] * 4, place, [kept_half, received], wide)


def next_sums(place, parts, arrays):
    def kernel(place_ref, refs, outs):
        for j in range(4):
            piece = (place_ref[1] // 2) ^ j
            total = refs[0][piece].astype(F32)
            for ref in refs[1:]:
                total = total + ref[piece].astype(F32)
            outs[j * arrays // 4][j % (4 // arrays)] = total.astype(BF16)

    return local(kernel, [shape(4 // arrays, *parts[0].shape[1:])] * arrays, place, parts)


def finish(place, groups, outputs):
    flat = [array for group in groups for array in group]
    outs_shape = [shape(rows, cols, dtype=F32) for rows, cols, _ in outputs]

    def kernel(place_ref, refs, outs):
        for ref, (rows, cols, sources) in zip(outs, outputs):
            filled = len(sources) * D
            if cols > filled:
                ref[:, filled:] = jnp.zeros((rows, cols - filled), F32)
            size = rows // 4
            for group, row, column in sources:
                for j in range(4):
                    quarter = 2 * (place_ref[0] ^ (j // 2)) + (place_ref[2] ^ (j % 2))
                    value = refs[4 * group + j][...].astype(F32)
                    low = pl.multiple_of(quarter * size, 8)
                    ref[pl.ds(low, size), column : column + D] = value[row : row + size]

    return local(kernel, outs_shape, place, flat)


def unpack(place, stacks, first, count, wide, names):
    owners = 2 * stacks[0].shape[0]

    def kernel(place_ref, refs, outs):
        vec_ref, wide_ref = outs
        lanes = lax.broadcasted_iota(jnp.int32, (16, owners * count), 1)
        total = jnp.zeros((16, owners * count), F32)
        codes = far_codes(owners // 2)
        for code in range(owners):
            owner = place_ref[1] ^ code
            rows = refs[code % 2][codes.index(code // 2), first : first + 16, :].astype(F32)
            row = jnp.pad(rows[:, :count], ((0, 0), (0, (owners - 1) * count)))
            total = total + pltpu.roll(row, owner * count, 1)
            wide_ref[:, pl.ds(pl.multiple_of(owner * wide, 128), wide)] = jnp.broadcast_to(
                rows[names : names + 1, :wide], (8, wide)
            )
        vec_ref[...] = total[:, :D]

    return local(
        kernel, [shape(16, D, dtype=F32), shape(8, owners * wide, dtype=F32)], place, stacks
    )


def small_total(place, attn, one, two, wide):
    def kernel(place_ref, refs, outs):
        both, first, second, broad = (ref[...] for ref in refs)
        rows = [both[0:2], first[0:3], second[1:3], second[0:1]]
        rows += [broad[0:1, j * D : (j + 1) * D] for j in range(FF // D)]
        rows += [both[2:5], first[3:4]]
        row = 0
        for part in rows:
            outs[0][row : row + part.shape[0], :] = part
            row += part.shape[0]

    return local(kernel, [shape(16, D, dtype=F32)], place, [attn, one, two, wide])[0]


def last_sums(parts):
    return sum(part.astype(F32) for part in parts).astype(BF16)


def tie(value, *before):
    return lax.optimization_barrier((value, *before))[0]


def in_order(value, order):
    return jnp.concatenate([lax.dynamic_slice_in_dim(value, order[i], 1) for i in range(value.shape[0])])


class Grid:
    def __init__(self, dp, fsdp):
        self.dp, self.fsdp = dp, fsdp
        self.dp_bits = [1 << i for i in range(dp.bit_length() - 1)]
        self.fsdp_bits = [1 << i for i in range(fsdp.bit_length() - 1)]

    def bit(self, axis, bit):
        return (lax.axis_index(axis) // bit) % 2

    def swap(self, value, dp_mask, fsdp_mask):
        if not dp_mask:
            return lax.ppermute(value, "fsdp", [(i, i ^ fsdp_mask) for i in range(self.fsdp)])
        if not fsdp_mask:
            return lax.ppermute(value, "dp", [(i, i ^ dp_mask) for i in range(self.dp)])
        pairs = [
            (i * self.fsdp + j, (i ^ dp_mask) * self.fsdp + (j ^ fsdp_mask))
            for i in range(self.dp)
            for j in range(self.fsdp)
        ]
        return lax.ppermute(value, ("dp", "fsdp"), pairs)

    def gather(self, piece):
        gathered = piece[None]
        for bit in self.fsdp_bits:
            gathered = jnp.concatenate([gathered, self.swap(gathered, 0, bit)])
        return gathered

    def joined(self, stack, bit, *before):
        other = self.swap(stack, 0, bit)
        return jnp.concatenate([stack, tie(other, *before) if before else other])

    def stages(self):
        dp_left, fsdp_left = self.dp_bits[1:], list(self.fsdp_bits)
        order = [[("dp", 1)]]
        while dp_left and fsdp_left:
            order.append([("dp", dp_left.pop(0)), ("fsdp", fsdp_left.pop(0))])
        order += [[("dp", bit)] for bit in dp_left]
        while fsdp_left:
            order.append([("fsdp", bit) for bit in fsdp_left[:2]])
            fsdp_left = fsdp_left[2:]
        return order

    def reduce(self, grads):
        rows, width = grads.shape[1:]
        left = list(reversed(self.fsdp_bits))
        value = grads.reshape((2,) * len(left) + (rows, width))
        halved = []
        for stage in self.stages():
            for axis, bit in stage:
                if axis == "dp":
                    value = value.reshape(value.shape[:-2] + (2, value.shape[-2] // 2, width))
                    halved.append(bit)
            spots = {}
            extra = len(left)
            for axis, bit in stage:
                if axis == "dp":
                    spots[(axis, bit)] = extra
                    extra += 1
                else:
                    spots[(axis, bit)] = left.index(bit)
            total = None
            for code in range(1 << len(stage)):
                starts = [0] * value.ndim
                sizes = list(value.shape)
                masks = {"dp": 0, "fsdp": 0}
                for place, (axis, bit) in enumerate(stage):
                    other = (code >> place) & 1
                    starts[spots[(axis, bit)]] = self.bit(axis, bit) ^ other
                    sizes[spots[(axis, bit)]] = 1
                    masks[axis] += bit * other
                part = lax.dynamic_slice(value, starts, sizes)
                if code:
                    part = self.swap(part, masks["dp"], masks["fsdp"])
                part = part.astype(F32)
                total = part if total is None else total + part
            total = jnp.squeeze(total, tuple(spots.values()))
            left = [bit for bit in left if ("fsdp", bit) not in spots]
            value = total.astype(BF16)
        for bit in reversed(halved):
            other = self.swap(value, bit, 0)
            first = self.bit("dp", bit) == 0
            value = jnp.concatenate([jnp.where(first, value, other), jnp.where(first, other, value)])
        return value.astype(F32)

    def total(self, value):
        masks = [(bit | 1, 0) for bit in reversed(self.dp_bits)] + [(1, bit) for bit in reversed(self.fsdp_bits)]
        for dp_mask, fsdp_mask in masks:
            value = value + self.swap(value, dp_mask, fsdp_mask)
        return value


def packed_vectors(rows, count, wide, names):
    owners = rows.shape[0]
    vec = rows[:, : names * count].reshape(owners, names, count)
    vec = jnp.swapaxes(vec, 0, 1).reshape(names, owners * count)[:, :D].astype(F32)
    b1 = rows[:, names * count : names * count + wide].reshape(1, -1)[:, :FF].astype(F32)
    return jnp.pad(vec, ((0, 16 - names), (0, 0))), jnp.broadcast_to(b1, (8, FF))


VECTORS = ("qb", "vb", "ob", "g1", "s1", "g2", "s2", "b2")


def vector_grads(small, weights, count, wide, d_max, ff_max):
    me = lax.axis_index("fsdp")
    rows = jnp.pad(small, ((0, 0), (0, d_max - D)))
    rows = lax.dynamic_slice(rows, (0, me * count), (small.shape[0], count))
    grads = {name: rows[i] for i, name in enumerate(VECTORS)}
    wide_at = len(VECTORS)
    b1 = jnp.pad(small[wide_at : wide_at + FF // D].reshape(-1), (0, ff_max - FF))
    grads["b1"] = lax.dynamic_slice(b1, (me * wide,), (wide,))
    sums = small[wide_at + FF // D :]
    total = sum(weight[:, :D].astype(F32) * sums[i : i + 1] for i, weight in enumerate(weights))
    within = me * count + jnp.arange(count, dtype=jnp.int32) < D
    grads["m"] = jnp.where(within, jnp.sum(total, axis=1), 0.0) + rows[-1]
    return grads


def in_columns(weight):
    return [weight[:, j * D : (j + 1) * D] for j in range(FF // D)]


def any_grid(grid, frames, cotangent, span_starts, matrices, vectors, up_bias):
    query, key, value, out, up, down = matrices
    count, wide = query.shape[0], down.shape[0]
    owners = grid.fsdp
    d_max, ff_max = count * owners, wide * owners
    me, core = lax.axis_index("fsdp"), lax.axis_index("dp") % 2
    codes = me ^ jnp.arange(owners, dtype=jnp.int32)

    def gathered(pieces):
        stack = in_order(grid.gather(jnp.concatenate(pieces)), codes)
        stack = stack.reshape(owners, len(pieces), -1, D)
        return [stack[:, i].reshape(-1, D) for i in range(len(pieces))]

    packed = jnp.concatenate(vectors + [up_bias]).reshape(1, -1)
    packed = in_order(grid.gather(packed)[:, 0], codes)
    vec, b1 = packed_vectors(packed, count, wide, len(vectors))
    wq, wk, wv, wo = gathered([piece[:, :D] for piece in (query, key, value, out)])
    up_blocks = gathered(in_columns(up))
    (w2,) = gathered([down[:, :D]])

    def unit(role_zero, role_one):
        first = core == 0
        return ([jnp.where(first, role_zero, role_one)[None]], [jnp.where(first, role_one, role_zero)[None]])

    quarter = lax.axis_index("dp") % 4
    stacked = jnp.stack([wq, wk, wv, wo])
    attn = [[lax.dynamic_slice_in_dim(stacked, quarter ^ flip, 1)] for flip in (0, 2, 1, 3)]
    up_unit = unit(jnp.concatenate(up_blocks[:2]), jnp.concatenate(up_blocks[2:]))
    down_unit = unit(w2[: ff_max // 2], w2[ff_max // 2 :])
    place = jnp.stack([core, jnp.zeros_like(core), quarter // 2])
    layer = Layer(place, span_starts[:, None, :], frames, vec, b1, d_max, ff_max, d_max, ff_max, False)
    q, k, v, o, lse, n1, rstd = layer.attn_forward(attn)
    hidden, slope = layer.ffn_up(up_unit, n1)
    output, dz, dr2, small2, down_grad = layer.ffn_down(down_unit, n1, hidden, cotangent, False)
    dr1, do, small1, wide_small, *up_out = layer.ffn_backward(
        attn, up_unit, down_unit, n1, rstd, dz, dr2, slope, o
    )
    dq, dk, dv, small_a, *qkv = layer.attn_backward(q, k, v, do, lse)
    frames_grad = layer.input_backward(attn, dr1, (dq, dk, dv))[0]
    small = grid.total(small_total(place, small_a, small1, small2, wide_small))

    def reduced(grads):
        total = grid.reduce(jnp.concatenate([grad.reshape(owners, -1, D) for grad in grads], axis=1))
        return [part for part in total.reshape(len(grads), -1, D)]

    def wide_rows(grad):
        return jnp.pad(grad, ((0, 0), (0, d_max - D)))

    sums = [wide_rows(grad) for grad in reduced(qkv)]
    up_out = reduced(up_out)
    sums.append(wide_rows(up_out[-1]))
    zeros = jnp.zeros((count, up.shape[1] - FF), F32)
    sums.append(jnp.concatenate(up_out[:-1] + [zeros], axis=1))
    sums.append(wide_rows(reduced([down_grad])[0]))
    return output, frames_grad, sums, vector_grads(small, matrices[:3], count, wide, d_max, ff_max)


def four_by_eight(grid, frames, cotangent, span_starts, matrices, vectors, up_bias):
    query, key, value, out, up, down = matrices
    count, wide = query.shape[0], down.shape[0]
    owners = grid.fsdp
    d_max, ff_max = count * owners, wide * owners
    me, dp_at = lax.axis_index("fsdp"), lax.axis_index("dp")
    core = dp_at % 2
    first = core == 0
    place = jnp.stack([core, me, dp_at // 2])

    packed = jnp.pad(jnp.stack(vectors), ((0, 0), (0, D - count)))
    packed = jnp.concatenate([packed, jnp.pad(up_bias, (0, D - wide))[None]])
    packed = jnp.pad(packed, ((0, 16 - packed.shape[0]), (0, 0)))
    half = wide // 2
    blocks = in_columns(up)
    attn_piece = jnp.where(
        dp_at < 2, jnp.where(first, query[:, :D], key[:, :D]), jnp.where(first, value[:, :D], out[:, :D])
    )
    up_piece = jnp.where(first, jnp.concatenate(blocks[:2]), jnp.concatenate(blocks[2:]))
    down_piece = jnp.where(first, down[:half, :D], down[half:, :D])

    def other_core(value):
        return grid.swap(value, 1, 0)

    high, low = 4, 2
    attn_pairs = grid.joined(attn_piece[None], high)
    attn_pairs = jnp.concatenate([attn_pairs, grid.joined(packed[None], high)], axis=1)
    far = grid.joined(attn_pairs, low)
    up_far = grid.joined(tie(up_piece, attn_pairs)[None], high)
    far = tie(far, up_far)
    far_along = grid.swap(far, 2, 0)
    near = grid.swap(far, 0, 1)
    near_along = grid.swap(tie(near, far_along), 2, 0)
    attn = [[far, near], [far_along, near_along]]
    attn += [[other_core(value) for value in arrays] for arrays in attn]
    vec, b1 = unpack(place, [far, near], count, count, wide, len(vectors))
    down_far = grid.joined(tie(down_piece, up_far)[None], high)
    up_far = grid.joined(tie(up_far, far), low)
    up_near = grid.swap(tie(up_far, near), 0, 1)

    layer = Layer(place, span_starts[:, None, :], frames, vec, b1, count, wide, d_max, ff_max, True)
    q, k, v, o, lse, n1, rstd = layer.attn_forward(attn, after=(up_far, down_far))
    down_far = grid.joined(tie(down_far, up_far), low, n1)
    down_near = grid.swap(tie(down_far, up_near), 0, 1)
    up_unit = [[up_far, up_near], [other_core(up_far), other_core(tie(up_near, down_far))]]
    hidden, slope = layer.ffn_up(up_unit, n1)
    down_unit = [[down_far, down_near], [other_core(down_far), other_core(tie(down_near, hidden))]]
    output, dz, dr2, small2, down_grad = layer.ffn_down(down_unit, n1, hidden, cotangent, False)
    down_sum = lax.psum_scatter(down_grad.reshape(owners, wide, D), "fsdp", scatter_dimension=0)
    dr1, do, small1, wide_small, *up_out = layer.ffn_backward(
        attn, up_unit, down_unit, n1, rstd, dz, dr2, slope, o
    )

    def spread(kept_half, received, wide=False):
        parts = first_sums(place, kept_half, received, wide)
        return parts[0], [grid.swap(parts[j], 2 * (j % 2), j // 2) for j in range(1, 4)]

    def spread_far(parts):
        pieces = next_sums(place, parts, 4)
        return [pieces[0]] + [grid.swap(pieces[j], 0, 2 * j) for j in range(1, 4)]

    own_u, got_u = spread(up_out[0], other_core(up_out[1]))
    dq, dk, dv, _, *qkv = layer.attn_backward(
        q, k, v, do, lse, attn, (small1, small2, wide_small), after=(own_u,)
    )
    received_q = other_core(tie(qkv[1], *got_u))
    pair_u, sent_u = next_sums(place, [tie(own_u, qkv[1])] + got_u, 2)
    got_far_u = grid.swap(sent_u, 0, high)
    own_q, got_q = spread(tie(qkv[0], pair_u), received_q, True)
    def halved(value, mask):
        size = value.shape[0] // 2
        mine = (dp_at // mask) % 2
        return [lax.dynamic_slice_in_dim(value, at * size, size) for at in (mine, 1 - mine)]

    kept_part, sent = halved(tie(down_sum, own_q), 1)
    down_half = last_sums([kept_part, grid.swap(sent, 1, 0)])
    kept_part, sent = halved(down_half, 2)
    got_down = grid.swap(sent, 2, 0)
    frames_grad = layer.input_backward(attn, dr1, (dq, dk, dv), after=(pair_u, down_half))[0]
    far_q = spread_far([tie(own_q, frames_grad)] + got_q)
    pair_u = last_sums([pair_u, tie(got_far_u, frames_grad)])
    sum_u = last_sums([pair_u[0], tie(grid.swap(pair_u[1], 0, low), far_q[0])])
    down_part = last_sums([kept_part, tie(got_down, frames_grad)])
    sum_u = jnp.concatenate([sum_u, down_part])
    cross_u = grid.swap(sum_u, 3, 0)
    sum_q = last_sums([far_q[0]] + [tie(part, cross_u) for part in far_q[1:]])[0]
    along_q = grid.swap(sum_q, 2, 0)
    total_u = [sum_u, other_core(cross_u), other_core(sum_u), cross_u]
    quarter = count // 4
    blocks_up = FF // D
    up_sum, out_sum, down_out = finish(
        place, [total_u],
        [
            (count, up.shape[1], [(0, j * quarter, j * D) for j in range(blocks_up)]),
            (count, d_max, [(0, blocks_up * quarter, 0)]),
            (wide, d_max, [(0, (blocks_up + 1) * quarter, 0)]),
        ],
    )
    total_q = [sum_q, along_q, other_core(sum_q), other_core(tie(along_q, up_sum))]
    *qkv_sums, small = finish(
        place, [total_q],
        [(count, d_max, [(0, j * quarter, 0)]) for j in range(3)] + [(32, D, [(0, 3 * quarter, 0)])],
    )
    vectors_out = {name: small[i, :count] for i, name in enumerate(VECTORS + ("m",))}
    vectors_out["b1"] = small[len(VECTORS) + 1, :wide]
    return output, frames_grad, [*qkv_sums, out_sum, up_sum, down_out], vectors_out


def on_device(
    sizes, frames, cotangent, span_starts, query_weight, key_weight, value_weight, out_weight,
    query_bias, value_bias, out_bias, first_gain, first_shift, up_weight, up_bias, down_weight,
    down_bias, second_gain, second_shift, mask_vector,
):
    grid = Grid(*sizes)
    matrices = (query_weight, key_weight, value_weight, out_weight, up_weight, down_weight)
    vectors = [query_bias, value_bias, out_bias, first_gain, first_shift, mask_vector,
               second_gain, second_shift, down_bias]
    placed = sizes == (4, 8) and query_weight.shape[0] % 32 == 0
    program = four_by_eight if placed else any_grid
    output, frames_grad, sums, small = program(
        grid, frames, cotangent, span_starts, matrices, vectors, up_bias
    )
    return (
        output, frames_grad, *sums[:4], small["qb"], small["vb"], small["ob"], small["g1"], small["s1"],
        sums[4], small["b1"], sums[5], small["b2"], small["g2"], small["s2"], small["m"],
    )


def solution(mesh):
    sizes = (mesh.shape["dp"], mesh.shape["fsdp"])
    tokens = P(("dp", "fsdp"), None)
    matrix, vector = P("fsdp", None), P("fsdp")
    return jax.shard_map(
        functools.partial(on_device, sizes),
        mesh=mesh,
        in_specs=(tokens,) * 3 + (matrix,) * 4 + (vector,) * 5 + (matrix, vector, matrix) + (vector,) * 4,
        out_specs=(tokens,) * 2 + (matrix,) * 4 + (vector,) * 5 + (matrix, vector, matrix) + (vector,) * 4,
        check_vma=False,
    )
```

```python
import functools
import jax
import jax.numpy as jnp
from jax import lax
from jax.experimental import pallas as pl
from jax.experimental.pallas import tpu as pltpu
from jax.sharding import PartitionSpec as P

HEADS = 10
HEAD_DIM = 64
FF = 2560
D = 640
FRAMES = 400
SPAN = 10
PAIR = 2 * HEAD_DIM
EPS = 1e-05
F32 = jnp.float32
BF16 = jnp.bfloat16
VMEM_LIMIT = 60 * 1024 * 1024
HID = 256


def dot_nn(a, b):
    return lax.dot_general(a, b, (((1,), (0,)), ((), ())), preferred_element_type=F32)


def dot_nt(a, b):
    return lax.dot_general(a, b, (((1,), (1,)), ((), ())), preferred_element_type=F32)


def dot_tn(a, b):
    return lax.dot_general(a, b, (((0,), (0,)), ((), ())), preferred_element_type=F32)


def mean_last(a):
    return jnp.mean(a, axis=-1, keepdims=True)


def rows_sum(a):
    return jnp.sum(a, axis=0, keepdims=True)


def masked_frames(starts_ref):
    places = lax.broadcasted_iota(jnp.int32, (FRAMES, starts_ref.shape[-1]), 0)
    ahead = places - starts_ref[0]
    inside = jnp.where((ahead >= 0) & (ahead < SPAN), 1.0, 0.0)
    return jnp.max(inside, axis=1, keepdims=True) > 0.5


def far_codes(pieces):
    codes = [0]
    for bit in reversed(range(pieces.bit_length() - 1)):
        codes += [code | 1 << bit for code in codes]
    return codes


def fetch(place_ref, sem, *wanted, start=True, wait=True):
    def copies(unit, parts, role):
        flips = (0, 1) if len(unit) == 2 else (0, 2, 1, 3)
        for arrays, flip in zip(unit, flips):
            for group, source in enumerate(arrays):
                for piece, code in enumerate(far_codes(source.shape[0])):
                    owner = place_ref[1] ^ (code * len(arrays) + group)
                    for share, first, rows, stride, row, column, target in parts:
                        if share == (role % len(unit)) ^ flip:
                            low = pl.multiple_of(owner * stride + row, 16)
                            yield pltpu.make_async_copy(
                                source.at[piece, pl.ds(first, rows), :],
                                target.at[pl.ds(low, rows), pl.ds(column, D)],
                                sem,
                            )

    for role in range(max(len(unit) for unit, _ in wanted)):
        here = place_ref[0] == role % 2
        if any(len(unit) > 2 for unit, _ in wanted):
            here = here & (place_ref[2] == role // 2)

        @pl.when(here)
        def _(role=role):
            listed = [copy for unit, parts in wanted for copy in copies(unit, parts, role)]
            if start:
                for copy in listed:
                    copy.start()
            if wait:
                for copy in listed:
                    copy.wait()


def attn_parts(rows, *targets):
    return [(share, 0, rows, rows, 0, 0, target) for share, target in enumerate(targets) if target is not None]


def up_parts(target, rows):
    return [(j // 2, (j % 2) * rows, rows, rows, 0, j * D, target) for j in range(FF // D)]


def down_parts(target, rows):
    return [(core, 0, rows // 2, rows, core * (rows // 2), 0, target) for core in (0, 1)]


def attn_forward(
    place_ref, attn, starts_ref, frames_ref, vec_ref,
    q_ref, k_ref, v_ref, o_ref, lse_ref, n1_ref, rstd_ref,
    wq_ref, wk_ref, wv_ref, wo_ref, sem, *, rows,
):
    @pl.when(pl.program_id(0) == 0)
    def _():
        fetch(place_ref, sem, (attn, attn_parts(rows, wq_ref, wk_ref, wv_ref, wo_ref)))

    bq, bv, bo = vec_ref[0:1, :], vec_ref[1:2, :], vec_ref[2:3, :]
    x0 = jnp.where(masked_frames(starts_ref), vec_ref[5:6, :], frames_ref[...].astype(F32))
    h = x0.astype(BF16)
    scale = HEAD_DIM ** (-0.5)
    q_ref[...] = ((dot_nn(h, wq_ref[0:D, :]) + bq).astype(BF16).astype(F32) * scale).astype(BF16)
    k_ref[...] = dot_nn(h, wk_ref[0:D, :]).astype(BF16)
    v_ref[...] = (dot_nn(h, wv_ref[0:D, :]) + bv).astype(BF16)
    low_lanes = lax.broadcasted_iota(jnp.int32, (FRAMES, PAIR), 1) < HEAD_DIM
    lanes = lax.broadcasted_iota(jnp.int32, (FRAMES, 128), 1)
    lse = jnp.zeros((FRAMES, 128), F32)

    def scores_of(head):
        cols = slice(head // 2 * PAIR, (head // 2 + 1) * PAIR)
        keep = low_lanes if head % 2 == 0 else jnp.logical_not(low_lanes)
        qh = jnp.where(keep, q_ref[:, cols].astype(F32), 0.0).astype(BF16)
        return dot_nt(qh, k_ref[:, cols])

    ahead = scores_of(0)
    parts = []
    for head in range(HEADS):
        cols = slice(head // 2 * PAIR, (head // 2 + 1) * PAIR)
        scores = ahead
        if head + 1 < HEADS:
            ahead = scores_of(head + 1)
        top = jnp.max(scores, axis=-1, keepdims=True)
        expo = jnp.exp(scores - top)
        total = jnp.sum(expo, axis=-1, keepdims=True)
        parts.append(dot_nn(expo.astype(BF16), v_ref[:, cols]) * (1.0 / total))
        lse = jnp.where(lanes == head, top + jnp.log(total), lse)
        if head % 2:
            o_ref[:, cols] = jnp.where(low_lanes, parts[0], parts[1]).astype(BF16)
            parts = []
    lse_ref[0] = jnp.transpose(lse)[0:16, :]
    r1 = x0 + (dot_nn(o_ref[...], wo_ref[0:D, :]) + bo)
    center = r1 - mean_last(r1)
    rstd = lax.rsqrt(mean_last(center * center) + EPS)
    n1_ref[...] = center * rstd
    rstd_ref[...] = rstd


def gelu_parts(u):
    phi = 0.5 + 0.5 * lax.erf(u * 0.7071067811865476)
    return u * phi, phi + u * jnp.exp(u * u * -0.5) * 0.3989422804014327


def ffn_up(place_ref, up, n1_ref, vec_ref, b1_ref, hidden_ref, slope_ref, w1_ref, sem, *, rows):
    @pl.when(pl.program_id(0) == 0)
    def _():
        fetch(place_ref, sem, (up, up_parts(w1_ref, rows)))

    y1b = (vec_ref[3:4, :] * n1_ref[...] + vec_ref[4:5, :]).astype(BF16)
    for c in range(FF // HID):
        cols = slice(c * HID, (c + 1) * HID)
        u = dot_nn(y1b, w1_ref[0:D, cols]) + b1_ref[0:1, cols]
        act, slope = gelu_parts(u)
        hidden_ref[:, cols] = act.astype(BF16)
        slope_ref[:, cols] = slope.astype(BF16)


def ffn_down(
    place_ref, down, n1_ref, hidden_ref, cot_ref, vec_ref,
    out_ref, dz_ref, dr2_ref, small_ref, *rest, rows, halves,
):
    grads_refs, (acc, w2_ref, sem) = rest[:-3], rest[-3:]
    step = pl.program_id(0)

    @pl.when(step == 0)
    def _():
        small_ref[...] = jnp.zeros_like(small_ref)
        acc[...] = jnp.zeros_like(acc)
        fetch(place_ref, sem, (down, down_parts(w2_ref, rows)))

    g1, s1, g2, s2, b2 = (vec_ref[i : i + 1, :] for i in (3, 4, 6, 7, 8))
    y1 = g1 * n1_ref[...] + s1
    r2 = y1 + (dot_nn(hidden_ref[...], w2_ref[0:FF, :]) + b2)
    center = r2 - mean_last(r2)
    rstd = lax.rsqrt(mean_last(center * center) + EPS)
    n2 = center * rstd
    out_ref[...] = (n2 * g2 + s2).astype(BF16)
    dy = cot_ref[...].astype(F32)
    e = dy * g2
    dr2 = (e - mean_last(e) - n2 * mean_last(e * n2)) * rstd
    dz = dr2.astype(BF16)
    dr2_ref[...] = dr2
    dz_ref[...] = dz
    small_ref[0:1, :] += rows_sum(dz.astype(F32))
    small_ref[1:2, :] += rows_sum(dy * n2)
    small_ref[2:3, :] += rows_sum(dy)
    acc[0:FF, :] += dot_tn(hidden_ref[...], dz)

    @pl.when(step == pl.num_programs(0) - 1)
    def _():
        deliver(place_ref, grads_refs, [(acc, 0, rows)], halves)


def deliver(place_ref, refs, sources, halves, extra=None):
    if not halves:
        for ref, (acc, column, _) in zip(refs, sources):
            ref[...] = acc[:, column : column + ref.shape[1]].astype(BF16)
        return
    for ref, core in zip(refs, (place_ref[0], 1 - place_ref[0])):
        owners, parts, _, width = ref.shape
        for owner in range(owners):
            for part in range(parts):
                pieces = []
                for acc, column, rows in sources:
                    size = rows // 4
                    low = pl.multiple_of(owner * rows + (2 * core + part) * size, 8)
                    pieces.append(acc[pl.ds(low, size), column : column + width])
                if extra:
                    pieces.append(jnp.where(core == 0, extra(owner, part), 0.0))
                ref[owner, part] = jnp.concatenate(pieces, axis=0).astype(BF16)


def ffn_backward(
    place_ref, attn, up, down, starts_ref, n1_ref, rstd_ref, dz_ref, dr2_ref, slope_ref, o_ref, vec_ref,
    dr1_ref, do_ref, small_ref, db1_ref, *rest, rows, halves,
):
    grads_refs = rest[:-8]
    grad_pre, acc1, acco, w1_ref, w2_ref, wo_ref, sem, late_sem = rest[-8:]
    late = ((up, up_parts(w1_ref, rows[0])), (attn, attn_parts(rows[0], None, None, None, wo_ref)))
    step = pl.program_id(0)

    @pl.when(step == 0)
    def _():
        small_ref[...] = jnp.zeros_like(small_ref)
        db1_ref[...] = jnp.zeros_like(db1_ref)
        acc1[...] = jnp.zeros_like(acc1)
        acco[...] = jnp.zeros_like(acco)
        fetch(place_ref, sem, (down, down_parts(w2_ref, rows[1])), wait=False)
        fetch(place_ref, late_sem, *late, wait=False)
        fetch(place_ref, sem, (down, down_parts(w2_ref, rows[1])), start=False)

    g1, s1 = vec_ref[3:4, :], vec_ref[4:5, :]
    n1 = n1_ref[...]
    y1b = (g1 * n1 + s1).astype(BF16)
    dz = dz_ref[...]
    for c in range(FF // HID):
        cols = slice(c * HID, (c + 1) * HID)
        du = (dot_nt(dz, w2_ref[cols, :]) * slope_ref[:, cols].astype(F32)).astype(BF16)
        grad_pre[:, cols] = du
        db1_ref[0:1, cols] += rows_sum(du.astype(F32))
    acc1[0:D, :] += dot_tn(y1b, grad_pre[...])

    @pl.when(step == 0)
    def _():
        fetch(place_ref, late_sem, *late, start=False)

    dy1 = dot_nt(grad_pre[...], w1_ref[0:D, :]) + dr2_ref[...]
    e = dy1 * g1
    dr1 = (e - mean_last(e) - n1 * mean_last(e * n1)) * rstd_ref[...]
    dr1_ref[...] = dr1
    da = dr1.astype(BF16)
    small_ref[0:1, :] += rows_sum(da.astype(F32))
    small_ref[1:2, :] += rows_sum(dy1 * n1)
    small_ref[2:3, :] += rows_sum(dy1)
    small_ref[3:4, :] += rows_sum(jnp.where(masked_frames(starts_ref), dr1, 0.0))
    acco[0:D, :] += dot_tn(o_ref[...], da)
    do_ref[...] = dot_nt(da, wo_ref[0:D, :]).astype(BF16)

    @pl.when(step == pl.num_programs(0) - 1)
    def _():
        sources = [(acc1, j * D, rows[0]) for j in range(FF // D)] + [(acco, 0, rows[0])]
        deliver(place_ref, grads_refs, sources, halves)


def attn_backward(
    place_ref, *rest, rows, halves,
):
    if halves:
        attn, (one_ref, two_ref, wide_ref), rest = rest[0], rest[1:4], rest[4:]
        rest, (wq_ref, wk_ref, wv_ref, sem) = rest[:-4], rest[-4:]
    starts_ref, frames_ref, vec_ref, q_ref, k_ref, v_ref, do_ref, lse_ref, *rest = rest
    dq_ref, dk_ref, dv_ref, small_ref, *rest = rest
    grads_refs, (accq, acck, accv) = rest[:-3], rest[-3:]
    step = pl.program_id(0)

    @pl.when(step == 0)
    def _():
        small_ref[...] = jnp.zeros_like(small_ref)
        accq[...] = jnp.zeros_like(accq)
        acck[...] = jnp.zeros_like(acck)
        accv[...] = jnp.zeros_like(accv)
        if halves:
            fetch(place_ref, sem, (attn, attn_parts(rows, wq_ref, wk_ref, wv_ref)), wait=False)

    scale = HEAD_DIM ** (-0.5)
    low_lanes = lax.broadcasted_iota(jnp.int32, (FRAMES, PAIR), 1) < HEAD_DIM

    def products(head):
        cols = slice(head // 2 * PAIR, (head // 2 + 1) * PAIR)
        keep = low_lanes if head % 2 == 0 else jnp.logical_not(low_lanes)
        kh = jnp.where(keep, k_ref[:, cols].astype(F32), 0.0).astype(BF16)
        vh = jnp.where(keep, v_ref[:, cols].astype(F32), 0.0).astype(BF16)
        return dot_nt(kh, q_ref[:, cols]), dot_nt(vh, do_ref[:, cols])

    ahead = products(0)
    parts = []
    for head in range(HEADS):
        cols = slice(head // 2 * PAIR, (head // 2 + 1) * PAIR)
        scores, dprob = ahead
        if head + 1 < HEADS:
            ahead = products(head + 1)
        prob = jnp.exp(scores - lse_ref[0, head : head + 1, :])
        inner = jnp.sum(prob * dprob, axis=0, keepdims=True)
        dscore = (prob * (dprob - inner)).astype(BF16)
        parts.append(
            (
                dot_nn(prob.astype(BF16), do_ref[:, cols]),
                dot_nn(dscore, q_ref[:, cols]),
                dot_tn(dscore, k_ref[:, cols]) * scale,
            )
        )
        if head % 2:
            for ref, one, two in zip((dv_ref, dk_ref, dq_ref), *parts):
                ref[:, cols] = jnp.where(low_lanes, one, two).astype(BF16)
            parts = []
    masked = masked_frames(starts_ref)
    h = jnp.where(masked, vec_ref[5:6, :], frames_ref[...].astype(F32)).astype(BF16)
    accq[0:D, :] += dot_tn(h, dq_ref[...])
    acck[0:D, :] += dot_tn(h, dk_ref[...])
    accv[0:D, :] += dot_tn(h, dv_ref[...])
    small_ref[0:1, :] += rows_sum(dq_ref[...].astype(F32))
    small_ref[1:2, :] += rows_sum(dv_ref[...].astype(F32))
    for row, ref in enumerate((dq_ref, dk_ref, dv_ref), 2):
        small_ref[row : row + 1, :] += rows_sum(jnp.where(masked, ref[...].astype(F32), 0.0))

    @pl.when(step == pl.num_programs(0) - 1)
    def _():
        extra = None
        if halves:
            fetch(place_ref, sem, (attn, attn_parts(rows, wq_ref, wk_ref, wv_ref)), start=False)
            first, second, wide = one_ref[...], two_ref[...], wide_ref[0:1, :]
            mask_row = first[3:4]
            for row, weight in enumerate((wq_ref, wk_ref, wv_ref), 2):
                line = jnp.broadcast_to(small_ref[row : row + 1, :], (8, D))
                upper = line.astype(BF16)
                lower = (line - upper.astype(F32)).astype(BF16)
                product = dot_nt(upper, weight[0:D, :]) + dot_nt(lower, weight[0:D, :])
                mask_row = mask_row + product[0:1]
            owners = grads_refs[0].shape[0]
            lines = jnp.concatenate([small_ref[0:2, :], first[0:3], second[1:3], second[0:1]], axis=0)
            lines = jnp.concatenate([lines, jnp.zeros((8, owners * rows - D), F32)], axis=1)
            mask_row = jnp.concatenate([mask_row, jnp.zeros((1, owners * rows - D), F32)], axis=1)
            count = wide_ref.shape[1] // FF * rows * (FF // D)
            wide = jnp.concatenate([wide, jnp.zeros((1, owners * count - FF), F32)], axis=1)

            def filled(line):
                return jnp.concatenate([line, jnp.zeros((line.shape[0], D - line.shape[1]), F32)], axis=1)

            def extra(owner, part):
                if part == 0:
                    return filled(lines[:, owner * rows : (owner + 1) * rows])
                return jnp.concatenate(
                    [
                        filled(mask_row[:, owner * rows : (owner + 1) * rows]),
                        filled(wide[:, owner * count : (owner + 1) * count]),
                        jnp.zeros((6, D), F32),
                    ],
                    axis=0,
                )

        deliver(place_ref, grads_refs, [(acc, 0, rows) for acc in (accq, acck, accv)], halves, extra)


def input_backward(
    place_ref, attn, starts_ref, dr1_ref, *rest, rows,
):
    parts, (grad_ref, wq_ref, wk_ref, wv_ref, sem) = rest[:-5], rest[-5:]

    @pl.when(pl.program_id(0) == 0)
    def _():
        fetch(place_ref, sem, (attn, attn_parts(rows, wq_ref, wk_ref, wv_ref)))

    masked = masked_frames(starts_ref)
    dx0 = dr1_ref[...]
    for grad, weight in zip(parts, (wq_ref, wk_ref, wv_ref)):
        dx0 += dot_nt(grad[...], weight[0:D, :])
    grad_ref[...] = jnp.where(masked, 0.0, dx0).astype(BF16)


def row_blocks(width):
    return pl.BlockSpec((FRAMES, width), lambda i, *_: (i, 0))


def kept(rows, cols):
    return pl.BlockSpec((rows, cols), lambda i, *_: (0, 0), pipeline_mode=pl.Buffered(1))


def held(*sizes):
    return pl.BlockSpec(sizes, lambda i, *_: (0,) * len(sizes))


def shape(*sizes, dtype=BF16):
    return jax.ShapeDtypeStruct(sizes, dtype)


SCALARS = pl.BlockSpec(memory_space=pltpu.SMEM)
WHOLE = pl.BlockSpec(memory_space=pl.ANY)
COPIES = pltpu.SemaphoreType.DMA(())


def call(
    body, steps, place, units, operands, in_specs, outputs, scratch=(), after=(), flops=0, moved=0,
):
    flat = [array for unit in units for arrays in unit for array in arrays]

    def kernel(place_ref, *refs):
        refs = refs[len(after) :]
        given = []
        for unit in units:
            given.append([])
            for arrays in unit:
                given[-1].append(refs[: len(arrays)])
                refs = refs[len(arrays) :]
        body(place_ref, *given, *refs)

    return pl.pallas_call(
        kernel,
        grid=(steps,),
        in_specs=[SCALARS] + [WHOLE] * (len(after) + len(flat)) + in_specs,
        out_specs=[spec for spec, _ in outputs],
        out_shape=[out for _, out in outputs],
        scratch_shapes=list(scratch),
        compiler_params=pltpu.CompilerParams(
            dimension_semantics=("arbitrary",), vmem_limit_bytes=VMEM_LIMIT
        ),
        cost_estimate=pl.CostEstimate(flops=int(flops), bytes_accessed=int(moved), transcendentals=0),
    )(place, *after, *flat, *operands)


def starts_spec(starts):
    return pl.BlockSpec((1, 1, starts.shape[-1]), lambda i: (i, 0, 0))


def lse_spec():
    return pl.BlockSpec((1, 16, FRAMES), lambda i: (i, 0, 0))


def weights(*sizes):
    return [pltpu.VMEM(size, BF16) for size in sizes] + [COPIES]


def by_rows(rows, width, dtype=BF16):
    return (row_blocks(width), shape(rows, width, dtype=dtype))


def summed(rows, width):
    return (held(rows, width), shape(rows, width, dtype=F32))


def grads_out(halves, sources, extra=0):
    if not halves:
        return [(held(rows, width), shape(rows, width)) for rows, width, _ in sources]
    rows, width, count = sources[0]
    sizes = (rows // count, 2, sum(part[2] for part in sources) // 4 + extra, width)
    return [(held(*sizes), shape(*sizes))] * 2


class Layer:
    def __init__(self, place, starts, frames, vec, b1, d_rows, ff_rows, d_max, ff_max, halves):
        self.place, self.starts, self.frames, self.vec, self.b1 = place, starts, frames, vec, b1
        self.d_rows, self.ff_rows, self.d_max, self.ff_max, self.halves = d_rows, ff_rows, d_max, ff_max, halves
        self.rows = frames.shape[0]
        self.steps = self.rows // FRAMES

    def attn_forward(self, attn, after=()):
        rows = self.rows
        return call(
            functools.partial(attn_forward, rows=self.d_rows), self.steps, self.place, (attn,),
            (self.starts, self.frames, self.vec), [starts_spec(self.starts), row_blocks(D), kept(16, D)],
            [by_rows(rows, D)] * 4
            + [(lse_spec(), shape(self.steps, 16, FRAMES, dtype=F32)), by_rows(rows, D, F32), by_rows(rows, 1, F32)],
            weights(*[(self.d_max, D)] * 4), after,
            flops=rows * D * D * 8 + rows * FRAMES * D * 16, moved=rows * D * 14,
        )

    def ffn_up(self, up, n1, after=()):
        rows = self.rows
        return call(
            functools.partial(ffn_up, rows=self.d_rows), self.steps, self.place, (up,),
            (n1, self.vec, self.b1), [row_blocks(D), kept(16, D), kept(8, FF)],
            [by_rows(rows, FF)] * 2, weights((self.d_max, FF)), after,
            flops=rows * D * FF * 4, moved=rows * FF * 6,
        )

    def ffn_down(self, down, n1, hidden, cotangent, halves, after=()):
        rows = self.rows
        return call(
            functools.partial(ffn_down, rows=self.ff_rows, halves=halves), self.steps, self.place, (down,),
            (n1, hidden, cotangent, self.vec), [row_blocks(D), row_blocks(FF), row_blocks(D), kept(16, D)],
            [by_rows(rows, D), by_rows(rows, D), by_rows(rows, D, F32), summed(8, D)]
            + grads_out(halves, [(self.ff_max, D, self.ff_rows)]),
            [pltpu.VMEM((self.ff_max, D), F32)] + weights((self.ff_max, D)), after,
            flops=rows * D * FF * 6, moved=rows * FF * 8,
        )

    def ffn_backward(self, attn, up, down, n1, rstd, dz, dr2, slope, o, after=()):
        rows = self.rows
        return call(
            functools.partial(ffn_backward, rows=(self.d_rows, self.ff_rows), halves=self.halves),
            self.steps, self.place, (attn, up, down),
            (self.starts, n1, rstd, dz, dr2, slope, o, self.vec),
            [starts_spec(self.starts)] + [row_blocks(w) for w in (D, 1, D, D, FF, D)] + [kept(16, D)],
            [by_rows(rows, D, F32), by_rows(rows, D), summed(8, D), summed(8, FF)]
            + grads_out(
                self.halves,
                [(self.d_max, D, self.d_rows)] * 5,
            ),
            [pltpu.VMEM((FRAMES, FF), BF16), pltpu.VMEM((self.d_max, FF), F32), pltpu.VMEM((self.d_max, D), F32)]
            + weights((self.d_max, FF), (self.ff_max, D), (self.d_max, D)) + [COPIES], after,
            flops=rows * D * FF * 8 + rows * D * D * 4, moved=rows * FF * 8,
        )

    def attn_backward(self, q, k, v, do, lse, attn=None, vectors=(), after=()):
        rows = self.rows
        own = [row_blocks(D)] * 4
        return call(
            functools.partial(attn_backward, rows=self.d_rows, halves=self.halves),
            self.steps, self.place, (attn,) if attn else (),
            (*vectors, self.starts, self.frames, self.vec, q, k, v, do, lse),
            [kept(*vector.shape) for vector in vectors]
            + [starts_spec(self.starts), row_blocks(D), kept(16, D)] + own + [lse_spec()],
            [by_rows(rows, D)] * 3 + [summed(8, D)]
            + grads_out(self.halves, [(self.d_max, D, self.d_rows)] * 3, 8),
            [pltpu.VMEM((self.d_max, D), F32)] * 3 + (weights(*[(self.d_max, D)] * 3) if attn else []), after,
            flops=rows * D * D * 6 + rows * FRAMES * D * 40, moved=rows * D * 14,
        )

    def input_backward(self, attn, dr1, parts, after=()):
        rows = self.rows
        return call(
            functools.partial(input_backward, rows=self.d_rows), self.steps, self.place, (attn,),
            (self.starts, dr1, *parts),
            [starts_spec(self.starts), row_blocks(D)] + [row_blocks(part.shape[1]) for part in parts],
            [by_rows(rows, D)], weights(*[(self.d_max, D)] * 3), after,
            flops=rows * D * D * 8, moved=rows * D * 12,
        )


def local(kernel, outputs, place, operands, wide=False):
    count = len(operands)

    def body(place_ref, *refs):
        sources, outs = refs[:count], refs[count : count + len(outputs)]
        held_refs, sems = refs[count + len(outputs) : -1], refs[-1]
        copies = [
            pltpu.make_async_copy(source, target, sems.at[i])
            for i, (source, target) in enumerate(zip(sources, held_refs))
        ]
        for copy in copies:
            copy.start()
        for copy in copies:
            copy.wait()
        kernel(place_ref, held_refs, outs)

    vmem = pl.BlockSpec(memory_space=pltpu.VMEM)
    return pl.pallas_call(
        body,
        in_specs=[SCALARS] + [WHOLE] * count,
        out_specs=[vmem] * len(outputs),
        out_shape=outputs,
        scratch_shapes=[pltpu.VMEM(array.shape, array.dtype) for array in operands]
        + [pltpu.SemaphoreType.DMA((count,))],
        compiler_params=pltpu.CompilerParams(
            vmem_limit_bytes=VMEM_LIMIT if wide else 4 * 2**20 + sum(4 * a.size for a in (*operands, *outputs))
        ),
        cost_estimate=pl.CostEstimate(flops=1000, bytes_accessed=4 * sum(a.size for a in operands), transcendentals=0),
    )(place, *operands)


def first_sums(place, kept_half, received):
    owners, _, rows, width = kept_half.shape

    def kernel(place_ref, refs, outs):
        for j in range(4):
            for z in range(owners // 2):
                owner, part = 2 * z + ((place_ref[1] % 2) ^ (j // 2)), place_ref[2] ^ (j % 2)
                outs[j][z] = (refs[0][owner, part].astype(F32) + refs[1][owner, part].astype(F32)).astype(BF16)

    return local(kernel, [shape(owners // 2, rows, width)] * 4, place, [kept_half, received])


def first_sums_from_hbm(place, kept_half, received):
    owners, _, rows, width = kept_half.shape
    steps = owners // 2

    def body(place_ref, kept_hbm, received_hbm, *refs):
        outs, (one, two), results, (in_sems, out_sems) = refs[:4], refs[4:6], refs[6:10], refs[10:]
        copies = []
        for z in range(steps):
            part = pl.ds(2 * z, 2)
            copies.append(
                [
                    pltpu.make_async_copy(source.at[part], target.at[part], in_sems.at[z, i])
                    for i, (source, target) in enumerate(((kept_hbm, one), (received_hbm, two)))
                ]
            )
            for copy in copies[-1]:
                copy.start()
        leaving = []
        for z in range(steps):
            for copy in copies[z]:
                copy.wait()
            for j in range(4):
                owner, part = 2 * z + ((place_ref[1] % 2) ^ (j // 2)), place_ref[2] ^ (j % 2)
                results[j][z] = (one[owner, part].astype(F32) + two[owner, part].astype(F32)).astype(BF16)
                leaving.append(pltpu.make_async_copy(results[j].at[z], outs[j].at[z], out_sems.at[z, j]))
                leaving[-1].start()
        for copy in leaving:
            copy.wait()

    out = shape(steps, rows, width)
    return pl.pallas_call(
        body,
        in_specs=[SCALARS, WHOLE, WHOLE],
        out_specs=[WHOLE] * 4,
        out_shape=[out] * 4,
        scratch_shapes=[pltpu.VMEM(kept_half.shape, BF16)] * 2
        + [pltpu.VMEM(out.shape, BF16)] * 4
        + [pltpu.SemaphoreType.DMA((steps, 2)), pltpu.SemaphoreType.DMA((steps, 4))],
        compiler_params=pltpu.CompilerParams(
            vmem_limit_bytes=VMEM_LIMIT
        ),
        cost_estimate=pl.CostEstimate(flops=1000, bytes_accessed=6 * kept_half.size, transcendentals=0),
    )(place, kept_half, received)


def next_sums(place, parts, arrays):
    def kernel(place_ref, refs, outs):
        for j in range(4):
            piece = (place_ref[1] // 2) ^ j
            total = refs[0][piece].astype(F32)
            for ref in refs[1:]:
                total = total + ref[piece].astype(F32)
            outs[j * arrays // 4][j % (4 // arrays)] = total.astype(BF16)

    return local(kernel, [shape(4 // arrays, *parts[0].shape[1:])] * arrays, place, parts)


def finish(place, groups, outputs):
    flat = [array for group in groups for array in group]
    outs_shape = [shape(rows, cols, dtype=F32) for rows, cols, _ in outputs]

    def kernel(place_ref, refs, outs):
        for ref, (rows, cols, sources) in zip(outs, outputs):
            filled = len(sources) * D
            if cols > filled:
                ref[:, filled:] = jnp.zeros((rows, cols - filled), F32)
            size = rows // 4
            for group, row, column in sources:
                for j in range(4):
                    quarter = 2 * (place_ref[0] ^ (j // 2)) + (place_ref[2] ^ (j % 2))
                    value = refs[4 * group + j][...].astype(F32)
                    low = pl.multiple_of(quarter * size, 8)
                    ref[pl.ds(low, size), column : column + D] = value[row : row + size]

    return local(kernel, outs_shape, place, flat)


def unpack(place, stacks, first, count, wide, names):
    owners = 2 * stacks[0].shape[0]

    def kernel(place_ref, refs, outs):
        vec_ref, wide_ref = outs
        lanes = lax.broadcasted_iota(jnp.int32, (16, owners * count), 1)
        total = jnp.zeros((16, owners * count), F32)
        codes = far_codes(owners // 2)
        for code in range(owners):
            owner = place_ref[1] ^ code
            rows = refs[code % 2][codes.index(code // 2), first : first + 16, :].astype(F32)
            row = jnp.pad(rows[:, :count], ((0, 0), (0, (owners - 1) * count)))
            total = total + pltpu.roll(row, owner * count, 1)
            wide_ref[:, pl.ds(pl.multiple_of(owner * wide, 128), wide)] = jnp.broadcast_to(
                rows[names : names + 1, :wide], (8, wide)
            )
        vec_ref[...] = total[:, :D]

    return local(
        kernel, [shape(16, D, dtype=F32), shape(8, owners * wide, dtype=F32)], place, stacks
    )


def small_total(place, attn, one, two, wide):
    def kernel(place_ref, refs, outs):
        both, first, second, broad = (ref[...] for ref in refs)
        rows = [both[0:2], first[0:3], second[1:3], second[0:1]]
        rows += [broad[0:1, j * D : (j + 1) * D] for j in range(FF // D)]
        rows += [both[2:5], first[3:4]]
        row = 0
        for part in rows:
            outs[0][row : row + part.shape[0], :] = part
            row += part.shape[0]

    return local(kernel, [shape(16, D, dtype=F32)], place, [attn, one, two, wide])[0]


def last_sums(parts):
    return sum(part.astype(F32) for part in parts).astype(BF16)


def tie(value, *before):
    return lax.optimization_barrier((value, *before))[0]


def in_order(value, order):
    return jnp.concatenate([lax.dynamic_slice_in_dim(value, order[i], 1) for i in range(value.shape[0])])


class Grid:
    def __init__(self, dp, fsdp):
        self.dp, self.fsdp = dp, fsdp
        self.dp_bits = [1 << i for i in range(dp.bit_length() - 1)]
        self.fsdp_bits = [1 << i for i in range(fsdp.bit_length() - 1)]

    def bit(self, axis, bit):
        return (lax.axis_index(axis) // bit) % 2

    def swap(self, value, dp_mask, fsdp_mask):
        if not dp_mask:
            return lax.ppermute(value, "fsdp", [(i, i ^ fsdp_mask) for i in range(self.fsdp)])
        if not fsdp_mask:
            return lax.ppermute(value, "dp", [(i, i ^ dp_mask) for i in range(self.dp)])
        pairs = [
            (i * self.fsdp + j, (i ^ dp_mask) * self.fsdp + (j ^ fsdp_mask))
            for i in range(self.dp)
            for j in range(self.fsdp)
        ]
        return lax.ppermute(value, ("dp", "fsdp"), pairs)

    def gather(self, piece):
        gathered = piece[None]
        for bit in self.fsdp_bits:
            gathered = jnp.concatenate([gathered, self.swap(gathered, 0, bit)])
        return gathered

    def joined(self, stack, bit, *before):
        other = self.swap(stack, 0, bit)
        return jnp.concatenate([stack, tie(other, *before) if before else other])

    def stages(self):
        dp_left, fsdp_left = self.dp_bits[1:], list(self.fsdp_bits)
        order = [[("dp", 1)]]
        while dp_left and fsdp_left:
            order.append([("dp", dp_left.pop(0)), ("fsdp", fsdp_left.pop(0))])
        order += [[("dp", bit)] for bit in dp_left]
        while fsdp_left:
            order.append([("fsdp", bit) for bit in fsdp_left[:2]])
            fsdp_left = fsdp_left[2:]
        return order

    def reduce(self, grads):
        rows, width = grads.shape[1:]
        left = list(reversed(self.fsdp_bits))
        value = grads.reshape((2,) * len(left) + (rows, width))
        halved = []
        for stage in self.stages():
            for axis, bit in stage:
                if axis == "dp":
                    value = value.reshape(value.shape[:-2] + (2, value.shape[-2] // 2, width))
                    halved.append(bit)
            spots = {}
            extra = len(left)
            for axis, bit in stage:
                if axis == "dp":
                    spots[(axis, bit)] = extra
                    extra += 1
                else:
                    spots[(axis, bit)] = left.index(bit)
            total = None
            for code in range(1 << len(stage)):
                starts = [0] * value.ndim
                sizes = list(value.shape)
                masks = {"dp": 0, "fsdp": 0}
                for place, (axis, bit) in enumerate(stage):
                    other = (code >> place) & 1
                    starts[spots[(axis, bit)]] = self.bit(axis, bit) ^ other
                    sizes[spots[(axis, bit)]] = 1
                    masks[axis] += bit * other
                part = lax.dynamic_slice(value, starts, sizes)
                if code:
                    part = self.swap(part, masks["dp"], masks["fsdp"])
                part = part.astype(F32)
                total = part if total is None else total + part
            total = jnp.squeeze(total, tuple(spots.values()))
            left = [bit for bit in left if ("fsdp", bit) not in spots]
            value = total.astype(BF16)
        for bit in reversed(halved):
            other = self.swap(value, bit, 0)
            first = self.bit("dp", bit) == 0
            value = jnp.concatenate([jnp.where(first, value, other), jnp.where(first, other, value)])
        return value.astype(F32)

    def total(self, value):
        masks = [(bit | 1, 0) for bit in reversed(self.dp_bits)] + [(1, bit) for bit in reversed(self.fsdp_bits)]
        for dp_mask, fsdp_mask in masks:
            value = value + self.swap(value, dp_mask, fsdp_mask)
        return value


def packed_vectors(rows, count, wide, names):
    owners = rows.shape[0]
    vec = rows[:, : names * count].reshape(owners, names, count)
    vec = jnp.swapaxes(vec, 0, 1).reshape(names, owners * count)[:, :D].astype(F32)
    b1 = rows[:, names * count : names * count + wide].reshape(1, -1)[:, :FF].astype(F32)
    return jnp.pad(vec, ((0, 16 - names), (0, 0))), jnp.broadcast_to(b1, (8, FF))


VECTORS = ("qb", "vb", "ob", "g1", "s1", "g2", "s2", "b2")


def vector_grads(small, weights, count, wide, d_max, ff_max):
    me = lax.axis_index("fsdp")
    rows = jnp.pad(small, ((0, 0), (0, d_max - D)))
    rows = lax.dynamic_slice(rows, (0, me * count), (small.shape[0], count))
    grads = {name: rows[i] for i, name in enumerate(VECTORS)}
    wide_at = len(VECTORS)
    b1 = jnp.pad(small[wide_at : wide_at + FF // D].reshape(-1), (0, ff_max - FF))
    grads["b1"] = lax.dynamic_slice(b1, (me * wide,), (wide,))
    sums = small[wide_at + FF // D :]
    total = sum(weight[:, :D].astype(F32) * sums[i : i + 1] for i, weight in enumerate(weights))
    within = me * count + jnp.arange(count, dtype=jnp.int32) < D
    grads["m"] = jnp.where(within, jnp.sum(total, axis=1), 0.0) + rows[-1]
    return grads


def in_columns(weight):
    return [weight[:, j * D : (j + 1) * D] for j in range(FF // D)]


def any_grid(grid, frames, cotangent, span_starts, matrices, vectors, up_bias):
    query, key, value, out, up, down = matrices
    count, wide = query.shape[0], down.shape[0]
    owners = grid.fsdp
    d_max, ff_max = count * owners, wide * owners
    me, core = lax.axis_index("fsdp"), lax.axis_index("dp") % 2
    codes = me ^ jnp.arange(owners, dtype=jnp.int32)

    def gathered(pieces):
        stack = in_order(grid.gather(jnp.concatenate(pieces)), codes)
        stack = stack.reshape(owners, len(pieces), -1, D)
        return [stack[:, i].reshape(-1, D) for i in range(len(pieces))]

    packed = jnp.concatenate(vectors + [up_bias]).reshape(1, -1)
    packed = in_order(grid.gather(packed)[:, 0], codes)
    vec, b1 = packed_vectors(packed, count, wide, len(vectors))
    wq, wk, wv, wo = gathered([piece[:, :D] for piece in (query, key, value, out)])
    up_blocks = gathered(in_columns(up))
    (w2,) = gathered([down[:, :D]])

    def unit(role_zero, role_one):
        first = core == 0
        return ([jnp.where(first, role_zero, role_one)[None]], [jnp.where(first, role_one, role_zero)[None]])

    quarter = lax.axis_index("dp") % 4
    stacked = jnp.stack([wq, wk, wv, wo])
    attn = [[lax.dynamic_slice_in_dim(stacked, quarter ^ flip, 1)] for flip in (0, 2, 1, 3)]
    up_unit = unit(jnp.concatenate(up_blocks[:2]), jnp.concatenate(up_blocks[2:]))
    down_unit = unit(w2[: ff_max // 2], w2[ff_max // 2 :])
    place = jnp.stack([core, jnp.zeros_like(core), quarter // 2])
    layer = Layer(place, span_starts[:, None, :], frames, vec, b1, d_max, ff_max, d_max, ff_max, False)
    q, k, v, o, lse, n1, rstd = layer.attn_forward(attn)
    hidden, slope = layer.ffn_up(up_unit, n1)
    output, dz, dr2, small2, down_grad = layer.ffn_down(down_unit, n1, hidden, cotangent, False)
    dr1, do, small1, wide_small, *up_out = layer.ffn_backward(
        attn, up_unit, down_unit, n1, rstd, dz, dr2, slope, o
    )
    dq, dk, dv, small_a, *qkv = layer.attn_backward(q, k, v, do, lse)
    frames_grad = layer.input_backward(attn, dr1, (dq, dk, dv))[0]
    small = grid.total(small_total(place, small_a, small1, small2, wide_small))

    def reduced(grads):
        total = grid.reduce(jnp.concatenate([grad.reshape(owners, -1, D) for grad in grads], axis=1))
        return [part for part in total.reshape(len(grads), -1, D)]

    def wide_rows(grad):
        return jnp.pad(grad, ((0, 0), (0, d_max - D)))

    sums = [wide_rows(grad) for grad in reduced(qkv)]
    up_out = reduced(up_out)
    sums.append(wide_rows(up_out[-1]))
    zeros = jnp.zeros((count, up.shape[1] - FF), F32)
    sums.append(jnp.concatenate(up_out[:-1] + [zeros], axis=1))
    sums.append(wide_rows(reduced([down_grad])[0]))
    return output, frames_grad, sums, vector_grads(small, matrices[:3], count, wide, d_max, ff_max)


def four_by_eight(grid, frames, cotangent, span_starts, matrices, vectors, up_bias):
    query, key, value, out, up, down = matrices
    count, wide = query.shape[0], down.shape[0]
    owners = grid.fsdp
    d_max, ff_max = count * owners, wide * owners
    me, dp_at = lax.axis_index("fsdp"), lax.axis_index("dp")
    core = dp_at % 2
    first = core == 0
    place = jnp.stack([core, me, dp_at // 2])

    packed = jnp.pad(jnp.stack(vectors), ((0, 0), (0, D - count)))
    packed = jnp.concatenate([packed, jnp.pad(up_bias, (0, D - wide))[None]])
    packed = jnp.pad(packed, ((0, 16 - packed.shape[0]), (0, 0)))
    half = wide // 2
    blocks = in_columns(up)
    attn_piece = jnp.where(
        dp_at < 2, jnp.where(first, query[:, :D], key[:, :D]), jnp.where(first, value[:, :D], out[:, :D])
    )
    up_piece = jnp.where(first, jnp.concatenate(blocks[:2]), jnp.concatenate(blocks[2:]))
    down_piece = jnp.where(first, down[:half, :D], down[half:, :D])

    def other_core(value):
        return grid.swap(value, 1, 0)

    high, low = 4, 2
    attn_pairs = grid.joined(attn_piece[None], high)
    attn_pairs = jnp.concatenate([attn_pairs, grid.joined(packed[None], high)], axis=1)
    far = grid.joined(attn_pairs, low)
    up_far = grid.joined(tie(up_piece, attn_pairs)[None], high)
    far = tie(far, up_far)
    far_along = grid.swap(far, 2, 0)
    near = grid.swap(far, 0, 1)
    up_pairs, up_more = up_far, grid.swap(tie(up_far, far), 0, low)
    near_along = grid.swap(tie(near, far_along, up_more), 2, 0)
    down_far = grid.joined(tie(down_piece, up_pairs)[None], high)
    attn = [[far, near], [far_along, near_along]]
    attn += [[other_core(far), other_core(near)], [other_core(far_along), other_core(tie(near_along, down_far))]]
    vec, b1 = unpack(place, [far, near], count, count, wide, len(vectors))
    up_far = jnp.concatenate([up_pairs, up_more])
    up_near = grid.swap(tie(up_far, near), 0, 1)

    layer = Layer(place, span_starts[:, None, :], frames, vec, b1, count, wide, d_max, ff_max, True)
    q, k, v, o, lse, n1, rstd = layer.attn_forward(attn, after=(up_far, down_far))
    down_far = grid.joined(tie(down_far, up_far), low, n1)
    down_near = grid.swap(tie(down_far, up_near), 0, 1)
    up_unit = [[up_far, up_near], [other_core(up_far), other_core(tie(up_near, down_far))]]
    hidden, slope = layer.ffn_up(up_unit, n1)
    down_unit = [[down_far, down_near], [other_core(down_far), other_core(tie(down_near, hidden))]]
    output, dz, dr2, small2, down_grad = layer.ffn_down(down_unit, n1, hidden, cotangent, False)
    down_sum = lax.psum_scatter(down_grad.reshape(owners, wide, D), "fsdp", scatter_dimension=0)
    dr1, do, small1, wide_small, *up_out = layer.ffn_backward(
        attn, up_unit, down_unit, n1, rstd, dz, dr2, slope, o
    )

    def spread(kept_half, received, from_hbm=False):
        parts = (first_sums_from_hbm if from_hbm else first_sums)(place, kept_half, received)
        return parts[0], [grid.swap(parts[j], 2 * (j % 2), j // 2) for j in range(1, 4)]

    def spread_far(parts):
        pieces = next_sums(place, parts, 4)
        return [pieces[0]] + [grid.swap(pieces[j], 0, 2 * j) for j in range(1, 4)]

    own_u, got_u = spread(up_out[0], other_core(up_out[1]))
    dq, dk, dv, _, *qkv = layer.attn_backward(
        q, k, v, do, lse, attn, (small1, small2, wide_small), after=(own_u,)
    )
    received_q = other_core(tie(qkv[1], *got_u))
    pair_u, sent_u = next_sums(place, [tie(own_u, qkv[1])] + got_u, 2)
    got_far_u = grid.swap(sent_u, 0, high)
    own_q, got_q = spread(tie(qkv[0], pair_u), received_q, True)
    def halved(value, mask):
        size = value.shape[0] // 2
        mine = (dp_at // mask) % 2
        return [lax.dynamic_slice_in_dim(value, at * size, size) for at in (mine, 1 - mine)]

    kept_part, sent = halved(tie(down_sum, own_q), 1)
    down_half = last_sums([kept_part, grid.swap(sent, 1, 0)])
    kept_part, sent = halved(down_half, 2)
    got_down = grid.swap(sent, 2, 0)
    frames_grad = layer.input_backward(attn, dr1, (dq, dk, dv), after=(pair_u, down_half))[0]
    far_q = spread_far([tie(own_q, frames_grad)] + got_q)
    pair_u = last_sums([pair_u, tie(got_far_u, frames_grad)])
    sum_u = last_sums([pair_u[0], tie(grid.swap(pair_u[1], 0, low), far_q[0])])
    down_part = last_sums([kept_part, tie(got_down, frames_grad)])
    sum_u = jnp.concatenate([sum_u, down_part])
    cross_u = grid.swap(sum_u, 3, 0)
    sum_q = last_sums([far_q[0]] + [tie(part, cross_u) for part in far_q[1:]])[0]
    along_q = grid.swap(sum_q, 2, 0)
    total_u = [sum_u, other_core(cross_u), other_core(sum_u), cross_u]
    quarter = count // 4
    blocks_up = FF // D
    up_sum, out_sum, down_out = finish(
        place, [total_u],
        [
            (count, up.shape[1], [(0, j * quarter, j * D) for j in range(blocks_up)]),
            (count, d_max, [(0, blocks_up * quarter, 0)]),
            (wide, d_max, [(0, (blocks_up + 1) * quarter, 0)]),
        ],
    )
    total_q = [sum_q, along_q, other_core(sum_q), other_core(tie(along_q, up_sum))]
    *qkv_sums, small = finish(
        place, [total_q],
        [(count, d_max, [(0, j * quarter, 0)]) for j in range(3)] + [(32, D, [(0, 3 * quarter, 0)])],
    )
    vectors_out = {name: small[i, :count] for i, name in enumerate(VECTORS + ("m",))}
    vectors_out["b1"] = small[len(VECTORS) + 1, :wide]
    return output, frames_grad, [*qkv_sums, out_sum, up_sum, down_out], vectors_out


def on_device(
    sizes, frames, cotangent, span_starts, query_weight, key_weight, value_weight, out_weight,
    query_bias, value_bias, out_bias, first_gain, first_shift, up_weight, up_bias, down_weight,
    down_bias, second_gain, second_shift, mask_vector,
):
    grid = Grid(*sizes)
    matrices = (query_weight, key_weight, value_weight, out_weight, up_weight, down_weight)
    vectors = [query_bias, value_bias, out_bias, first_gain, first_shift, mask_vector,
               second_gain, second_shift, down_bias]
    placed = sizes == (4, 8) and query_weight.shape[0] % 32 == 0
    program = four_by_eight if placed else any_grid
    output, frames_grad, sums, small = program(
        grid, frames, cotangent, span_starts, matrices, vectors, up_bias
    )
    return (
        output, frames_grad, *sums[:4], small["qb"], small["vb"], small["ob"], small["g1"], small["s1"],
        sums[4], small["b1"], sums[5], small["b2"], small["g2"], small["s2"], small["m"],
    )


def solution(mesh):
    sizes = (mesh.shape["dp"], mesh.shape["fsdp"])
    tokens = P(("dp", "fsdp"), None)
    matrix, vector = P("fsdp", None), P("fsdp")
    return jax.shard_map(
        functools.partial(on_device, sizes),
        mesh=mesh,
        in_specs=(tokens,) * 3 + (matrix,) * 4 + (vector,) * 5 + (matrix, vector, matrix) + (vector,) * 4,
        out_specs=(tokens,) * 2 + (matrix,) * 4 + (vector,) * 5 + (matrix, vector, matrix) + (vector,) * 4,
        check_vma=False,
    )
```

```python
import functools
import jax
import jax.numpy as jnp
from jax import lax
from jax.experimental import pallas as pl
from jax.experimental.pallas import tpu as pltpu
from jax.sharding import PartitionSpec as P

HEADS = 10
HEAD_DIM = 64
FF = 2560
D = 640
FRAMES = 400
SPAN = 10
PAIR = 2 * HEAD_DIM
EPS = 1e-05
F32 = jnp.float32
BF16 = jnp.bfloat16
VMEM_LIMIT = 60 * 1024 * 1024
HID = 256


def dot_nn(a, b):
    return lax.dot_general(a, b, (((1,), (0,)), ((), ())), preferred_element_type=F32)


def dot_nt(a, b):
    return lax.dot_general(a, b, (((1,), (1,)), ((), ())), preferred_element_type=F32)


def dot_tn(a, b):
    return lax.dot_general(a, b, (((0,), (0,)), ((), ())), preferred_element_type=F32)


def mean_last(a):
    return jnp.mean(a, axis=-1, keepdims=True)


def rows_sum(a):
    return jnp.sum(a, axis=0, keepdims=True)


def masked_frames(starts_ref):
    places = lax.broadcasted_iota(jnp.int32, (FRAMES, starts_ref.shape[-1]), 0)
    ahead = places - starts_ref[0]
    inside = jnp.where((ahead >= 0) & (ahead < SPAN), 1.0, 0.0)
    return jnp.max(inside, axis=1, keepdims=True) > 0.5


def far_codes(pieces):
    codes = [0]
    for bit in reversed(range(pieces.bit_length() - 1)):
        codes += [code | 1 << bit for code in codes]
    return codes


def fetch(place_ref, sem, *wanted, start=True, wait=True):
    def copies(unit, parts, role):
        flips = (0, 1) if len(unit) == 2 else (0, 2, 1, 3)
        for arrays, flip in zip(unit, flips):
            for group, source in enumerate(arrays):
                for piece, code in enumerate(far_codes(source.shape[0])):
                    owner = place_ref[1] ^ (code * len(arrays) + group)
                    for share, first, rows, stride, row, column, target in parts:
                        if share == (role % len(unit)) ^ flip:
                            low = pl.multiple_of(owner * stride + row, 16)
                            yield pltpu.make_async_copy(
                                source.at[piece, pl.ds(first, rows), :],
                                target.at[pl.ds(low, rows), pl.ds(column, D)],
                                sem,
                            )

    for role in range(max(len(unit) for unit, _ in wanted)):
        here = place_ref[0] == role % 2
        if any(len(unit) > 2 for unit, _ in wanted):
            here = here & (place_ref[2] == role // 2)

        @pl.when(here)
        def _(role=role):
            listed = [copy for unit, parts in wanted for copy in copies(unit, parts, role)]
            if start:
                for copy in listed:
                    copy.start()
            if wait:
                for copy in listed:
                    copy.wait()


def attn_parts(rows, *targets):
    return [(share, 0, rows, rows, 0, 0, target) for share, target in enumerate(targets) if target is not None]


def up_parts(target, rows):
    return [(j // 2, (j % 2) * rows, rows, rows, 0, j * D, target) for j in range(FF // D)]


def down_parts(target, rows):
    return [(core, 0, rows // 2, rows, core * (rows // 2), 0, target) for core in (0, 1)]


def attn_forward(
    place_ref, attn, starts_ref, frames_ref, vec_ref,
    q_ref, k_ref, v_ref, o_ref, lse_ref, n1_ref, rstd_ref,
    wq_ref, wk_ref, wv_ref, wo_ref, sem, *, rows,
):
    @pl.when(pl.program_id(0) == 0)
    def _():
        fetch(place_ref, sem, (attn, attn_parts(rows, wq_ref, wk_ref, wv_ref, wo_ref)))

    bq, bv, bo = vec_ref[0:1, :], vec_ref[1:2, :], vec_ref[2:3, :]
    x0 = jnp.where(masked_frames(starts_ref), vec_ref[5:6, :], frames_ref[...].astype(F32))
    h = x0.astype(BF16)
    scale = HEAD_DIM ** (-0.5)
    q_ref[...] = ((dot_nn(h, wq_ref[0:D, :]) + bq).astype(BF16).astype(F32) * scale).astype(BF16)
    k_ref[...] = dot_nn(h, wk_ref[0:D, :]).astype(BF16)
    v_ref[...] = (dot_nn(h, wv_ref[0:D, :]) + bv).astype(BF16)
    low_lanes = lax.broadcasted_iota(jnp.int32, (FRAMES, PAIR), 1) < HEAD_DIM
    lanes = lax.broadcasted_iota(jnp.int32, (FRAMES, 128), 1)
    lse = jnp.zeros((FRAMES, 128), F32)

    def scores_of(head):
        cols = slice(head // 2 * PAIR, (head // 2 + 1) * PAIR)
        keep = low_lanes if head % 2 == 0 else jnp.logical_not(low_lanes)
        qh = jnp.where(keep, q_ref[:, cols].astype(F32), 0.0).astype(BF16)
        return dot_nt(qh, k_ref[:, cols])

    ahead = scores_of(0)
    parts = []
    for head in range(HEADS):
        cols = slice(head // 2 * PAIR, (head // 2 + 1) * PAIR)
        scores = ahead
        if head + 1 < HEADS:
            ahead = scores_of(head + 1)
        top = jnp.max(scores, axis=-1, keepdims=True)
        expo = jnp.exp(scores - top)
        total = jnp.sum(expo, axis=-1, keepdims=True)
        parts.append(dot_nn(expo.astype(BF16), v_ref[:, cols]) * (1.0 / total))
        lse = jnp.where(lanes == head, top + jnp.log(total), lse)
        if head % 2:
            o_ref[:, cols] = jnp.where(low_lanes, parts[0], parts[1]).astype(BF16)
            parts = []
    lse_ref[0] = jnp.transpose(lse)[0:16, :]
    r1 = x0 + (dot_nn(o_ref[...], wo_ref[0:D, :]) + bo)
    center = r1 - mean_last(r1)
    rstd = lax.rsqrt(mean_last(center * center) + EPS)
    n1_ref[...] = center * rstd
    rstd_ref[...] = rstd


def gelu_parts(u):
    phi = 0.5 + 0.5 * lax.erf(u * 0.7071067811865476)
    return u * phi, phi + u * jnp.exp(u * u * -0.5) * 0.3989422804014327


def ffn_up(place_ref, up, n1_ref, vec_ref, b1_ref, hidden_ref, slope_ref, w1_ref, sem, *, rows):
    @pl.when(pl.program_id(0) == 0)
    def _():
        fetch(place_ref, sem, (up, up_parts(w1_ref, rows)))

    y1b = (vec_ref[3:4, :] * n1_ref[...] + vec_ref[4:5, :]).astype(BF16)
    for c in range(FF // HID):
        cols = slice(c * HID, (c + 1) * HID)
        u = dot_nn(y1b, w1_ref[0:D, cols]) + b1_ref[0:1, cols]
        act, slope = gelu_parts(u)
        hidden_ref[:, cols] = act.astype(BF16)
        slope_ref[:, cols] = slope.astype(BF16)


def ffn_down(
    place_ref, down, n1_ref, hidden_ref, cot_ref, vec_ref,
    out_ref, dz_ref, dr2_ref, small_ref, *rest, rows, halves,
):
    grads_refs, (acc, w2_ref, sem) = rest[:-3], rest[-3:]
    step = pl.program_id(0)

    @pl.when(step == 0)
    def _():
        small_ref[...] = jnp.zeros_like(small_ref)
        acc[...] = jnp.zeros_like(acc)
        fetch(place_ref, sem, (down, down_parts(w2_ref, rows)))

    g1, s1, g2, s2, b2 = (vec_ref[i : i + 1, :] for i in (3, 4, 6, 7, 8))
    y1 = g1 * n1_ref[...] + s1
    r2 = y1 + (dot_nn(hidden_ref[...], w2_ref[0:FF, :]) + b2)
    center = r2 - mean_last(r2)
    rstd = lax.rsqrt(mean_last(center * center) + EPS)
    n2 = center * rstd
    out_ref[...] = (n2 * g2 + s2).astype(BF16)
    dy = cot_ref[...].astype(F32)
    e = dy * g2
    dr2 = (e - mean_last(e) - n2 * mean_last(e * n2)) * rstd
    dz = dr2.astype(BF16)
    dr2_ref[...] = dr2
    dz_ref[...] = dz
    small_ref[0:1, :] += rows_sum(dz.astype(F32))
    small_ref[1:2, :] += rows_sum(dy * n2)
    small_ref[2:3, :] += rows_sum(dy)
    acc[0:FF, :] += dot_tn(hidden_ref[...], dz)

    @pl.when(step == pl.num_programs(0) - 1)
    def _():
        deliver(place_ref, grads_refs, [(acc, 0, rows)], halves)


def deliver(place_ref, refs, sources, halves, extra=None):
    if not halves:
        for ref, (acc, column, _) in zip(refs, sources):
            ref[...] = acc[:, column : column + ref.shape[1]].astype(BF16)
        return
    for ref, core in zip(refs, (place_ref[0], 1 - place_ref[0])):
        owners, parts, _, width = ref.shape
        for owner in range(owners):
            for part in range(parts):
                pieces = []
                for acc, column, rows in sources:
                    size = rows // 4
                    low = pl.multiple_of(owner * rows + (2 * core + part) * size, 8)
                    pieces.append(acc[pl.ds(low, size), column : column + width])
                if extra:
                    pieces.append(jnp.where(core == 0, extra(owner, part), 0.0))
                ref[owner, part] = jnp.concatenate(pieces, axis=0).astype(BF16)


def ffn_backward(
    place_ref, attn, up, down, starts_ref, n1_ref, rstd_ref, dz_ref, dr2_ref, slope_ref, o_ref, vec_ref,
    dr1_ref, do_ref, small_ref, db1_ref, *rest, rows, halves,
):
    grads_refs = rest[:-8]
    grad_pre, acc1, acco, w1_ref, w2_ref, wo_ref, sem, late_sem = rest[-8:]
    late = ((up, up_parts(w1_ref, rows[0])), (attn, attn_parts(rows[0], None, None, None, wo_ref)))
    step = pl.program_id(0)

    @pl.when(step == 0)
    def _():
        small_ref[...] = jnp.zeros_like(small_ref)
        db1_ref[...] = jnp.zeros_like(db1_ref)
        acc1[...] = jnp.zeros_like(acc1)
        acco[...] = jnp.zeros_like(acco)
        fetch(place_ref, sem, (down, down_parts(w2_ref, rows[1])), wait=False)
        fetch(place_ref, late_sem, *late, wait=False)
        fetch(place_ref, sem, (down, down_parts(w2_ref, rows[1])), start=False)

    g1, s1 = vec_ref[3:4, :], vec_ref[4:5, :]
    n1 = n1_ref[...]
    y1b = (g1 * n1 + s1).astype(BF16)
    dz = dz_ref[...]
    for c in range(FF // HID):
        cols = slice(c * HID, (c + 1) * HID)
        du = (dot_nt(dz, w2_ref[cols, :]) * slope_ref[:, cols].astype(F32)).astype(BF16)
        grad_pre[:, cols] = du
        db1_ref[0:1, cols] += rows_sum(du.astype(F32))
    acc1[0:D, :] += dot_tn(y1b, grad_pre[...])

    @pl.when(step == 0)
    def _():
        fetch(place_ref, late_sem, *late, start=False)

    dy1 = dot_nt(grad_pre[...], w1_ref[0:D, :]) + dr2_ref[...]
    e = dy1 * g1
    dr1 = (e - mean_last(e) - n1 * mean_last(e * n1)) * rstd_ref[...]
    dr1_ref[...] = dr1
    da = dr1.astype(BF16)
    small_ref[0:1, :] += rows_sum(da.astype(F32))
    small_ref[1:2, :] += rows_sum(dy1 * n1)
    small_ref[2:3, :] += rows_sum(dy1)
    small_ref[3:4, :] += rows_sum(jnp.where(masked_frames(starts_ref), dr1, 0.0))
    acco[0:D, :] += dot_tn(o_ref[...], da)
    do_ref[...] = dot_nt(da, wo_ref[0:D, :]).astype(BF16)

    @pl.when(step == pl.num_programs(0) - 1)
    def _():
        sources = [(acc1, j * D, rows[0]) for j in range(FF // D)] + [(acco, 0, rows[0])]
        deliver(place_ref, grads_refs, sources, halves)


def attn_backward(
    place_ref, *rest, rows, halves,
):
    if halves:
        attn, (one_ref, two_ref, wide_ref), rest = rest[0], rest[1:4], rest[4:]
        rest, (wq_ref, wk_ref, wv_ref, sem) = rest[:-4], rest[-4:]
    starts_ref, frames_ref, vec_ref, q_ref, k_ref, v_ref, do_ref, lse_ref, *rest = rest
    dq_ref, dk_ref, dv_ref, small_ref, *rest = rest
    grads_refs, (accq, acck, accv) = rest[:-3], rest[-3:]
    step = pl.program_id(0)

    @pl.when(step == 0)
    def _():
        small_ref[...] = jnp.zeros_like(small_ref)
        accq[...] = jnp.zeros_like(accq)
        acck[...] = jnp.zeros_like(acck)
        accv[...] = jnp.zeros_like(accv)
        if halves:
            fetch(place_ref, sem, (attn, attn_parts(rows, wq_ref, wk_ref, wv_ref)), wait=False)

    scale = HEAD_DIM ** (-0.5)
    low_lanes = lax.broadcasted_iota(jnp.int32, (FRAMES, PAIR), 1) < HEAD_DIM

    def products(head):
        cols = slice(head // 2 * PAIR, (head // 2 + 1) * PAIR)
        keep = low_lanes if head % 2 == 0 else jnp.logical_not(low_lanes)
        kh = jnp.where(keep, k_ref[:, cols].astype(F32), 0.0).astype(BF16)
        vh = jnp.where(keep, v_ref[:, cols].astype(F32), 0.0).astype(BF16)
        return dot_nt(kh, q_ref[:, cols]), dot_nt(vh, do_ref[:, cols])

    ahead = products(0)
    parts = []
    for head in range(HEADS):
        cols = slice(head // 2 * PAIR, (head // 2 + 1) * PAIR)
        scores, dprob = ahead
        if head + 1 < HEADS:
            ahead = products(head + 1)
        prob = jnp.exp(scores - lse_ref[0, head : head + 1, :])
        inner = jnp.sum(prob * dprob, axis=0, keepdims=True)
        dscore = (prob * (dprob - inner)).astype(BF16)
        parts.append(
            (
                dot_nn(prob.astype(BF16), do_ref[:, cols]),
                dot_nn(dscore, q_ref[:, cols]),
                dot_tn(dscore, k_ref[:, cols]) * scale,
            )
        )
        if head % 2:
            for ref, one, two in zip((dv_ref, dk_ref, dq_ref), *parts):
                ref[:, cols] = jnp.where(low_lanes, one, two).astype(BF16)
            parts = []
    masked = masked_frames(starts_ref)
    h = jnp.where(masked, vec_ref[5:6, :], frames_ref[...].astype(F32)).astype(BF16)
    accq[0:D, :] += dot_tn(h, dq_ref[...])
    acck[0:D, :] += dot_tn(h, dk_ref[...])
    accv[0:D, :] += dot_tn(h, dv_ref[...])
    small_ref[0:1, :] += rows_sum(dq_ref[...].astype(F32))
    small_ref[1:2, :] += rows_sum(dv_ref[...].astype(F32))
    for row, ref in enumerate((dq_ref, dk_ref, dv_ref), 2):
        small_ref[row : row + 1, :] += rows_sum(jnp.where(masked, ref[...].astype(F32), 0.0))

    @pl.when(step == pl.num_programs(0) - 1)
    def _():
        extra = None
        if halves:
            fetch(place_ref, sem, (attn, attn_parts(rows, wq_ref, wk_ref, wv_ref)), start=False)
            first, second, wide = one_ref[...], two_ref[...], wide_ref[0:1, :]
            mask_row = first[3:4]
            for row, weight in enumerate((wq_ref, wk_ref, wv_ref), 2):
                line = jnp.broadcast_to(small_ref[row : row + 1, :], (8, D))
                upper = line.astype(BF16)
                lower = (line - upper.astype(F32)).astype(BF16)
                product = dot_nt(upper, weight[0:D, :]) + dot_nt(lower, weight[0:D, :])
                mask_row = mask_row + product[0:1]
            owners = grads_refs[0].shape[0]
            lines = jnp.concatenate([small_ref[0:2, :], first[0:3], second[1:3], second[0:1]], axis=0)
            lines = jnp.concatenate([lines, jnp.zeros((8, owners * rows - D), F32)], axis=1)
            mask_row = jnp.concatenate([mask_row, jnp.zeros((1, owners * rows - D), F32)], axis=1)
            count = wide_ref.shape[1] // FF * rows * (FF // D)
            wide = jnp.concatenate([wide, jnp.zeros((1, owners * count - FF), F32)], axis=1)

            def filled(line):
                return jnp.concatenate([line, jnp.zeros((line.shape[0], D - line.shape[1]), F32)], axis=1)

            def extra(owner, part):
                if part == 0:
                    return filled(lines[:, owner * rows : (owner + 1) * rows])
                return jnp.concatenate(
                    [
                        filled(mask_row[:, owner * rows : (owner + 1) * rows]),
                        filled(wide[:, owner * count : (owner + 1) * count]),
                        jnp.zeros((6, D), F32),
                    ],
                    axis=0,
                )

        deliver(place_ref, grads_refs, [(acc, 0, rows) for acc in (accq, acck, accv)], halves, extra)


def input_backward(
    place_ref, attn, starts_ref, dr1_ref, *rest, rows,
):
    parts, (grad_ref, wq_ref, wk_ref, wv_ref, sem) = rest[:-5], rest[-5:]

    @pl.when(pl.program_id(0) == 0)
    def _():
        fetch(place_ref, sem, (attn, attn_parts(rows, wq_ref, wk_ref, wv_ref)))

    masked = masked_frames(starts_ref)
    dx0 = dr1_ref[...] + dot_nt(
        jnp.concatenate([part[...] for part in parts], axis=1),
        jnp.concatenate([ref[0:D, :] for ref in (wq_ref, wk_ref, wv_ref)], axis=1),
    )
    grad_ref[...] = jnp.where(masked, 0.0, dx0).astype(BF16)


def row_blocks(width):
    return pl.BlockSpec((FRAMES, width), lambda i, *_: (i, 0))


def kept(rows, cols):
    return pl.BlockSpec((rows, cols), lambda i, *_: (0, 0), pipeline_mode=pl.Buffered(1))


def held(*sizes):
    return pl.BlockSpec(sizes, lambda i, *_: (0,) * len(sizes))


def shape(*sizes, dtype=BF16):
    return jax.ShapeDtypeStruct(sizes, dtype)


SCALARS = pl.BlockSpec(memory_space=pltpu.SMEM)
WHOLE = pl.BlockSpec(memory_space=pl.ANY)
COPIES = pltpu.SemaphoreType.DMA(())


def call(
    body, steps, place, units, operands, in_specs, outputs, scratch=(), after=(), flops=0, moved=0,
):
    flat = [array for unit in units for arrays in unit for array in arrays]

    def kernel(place_ref, *refs):
        refs = refs[len(after) :]
        given = []
        for unit in units:
            given.append([])
            for arrays in unit:
                given[-1].append(refs[: len(arrays)])
                refs = refs[len(arrays) :]
        body(place_ref, *given, *refs)

    return pl.pallas_call(
        kernel,
        grid=(steps,),
        in_specs=[SCALARS] + [WHOLE] * (len(after) + len(flat)) + in_specs,
        out_specs=[spec for spec, _ in outputs],
        out_shape=[out for _, out in outputs],
        scratch_shapes=list(scratch),
        compiler_params=pltpu.CompilerParams(
            dimension_semantics=("arbitrary",), vmem_limit_bytes=VMEM_LIMIT
        ),
        cost_estimate=pl.CostEstimate(flops=int(flops), bytes_accessed=int(moved), transcendentals=0),
    )(place, *after, *flat, *operands)


def starts_spec(starts):
    return pl.BlockSpec((1, 1, starts.shape[-1]), lambda i: (i, 0, 0))


def lse_spec():
    return pl.BlockSpec((1, 16, FRAMES), lambda i: (i, 0, 0))


def weights(*sizes):
    return [pltpu.VMEM(size, BF16) for size in sizes] + [COPIES]


def by_rows(rows, width, dtype=BF16):
    return (row_blocks(width), shape(rows, width, dtype=dtype))


def summed(rows, width):
    return (held(rows, width), shape(rows, width, dtype=F32))


def grads_out(halves, sources, extra=0):
    if not halves:
        return [(held(rows, width), shape(rows, width)) for rows, width, _ in sources]
    rows, width, count = sources[0]
    sizes = (rows // count, 2, sum(part[2] for part in sources) // 4 + extra, width)
    return [(held(*sizes), shape(*sizes))] * 2


class Layer:
    def __init__(self, place, starts, frames, vec, b1, d_rows, ff_rows, d_max, ff_max, halves):
        self.place, self.starts, self.frames, self.vec, self.b1 = place, starts, frames, vec, b1
        self.d_rows, self.ff_rows, self.d_max, self.ff_max, self.halves = d_rows, ff_rows, d_max, ff_max, halves
        self.rows = frames.shape[0]
        self.steps = self.rows // FRAMES

    def attn_forward(self, attn, after=()):
        rows = self.rows
        return call(
            functools.partial(attn_forward, rows=self.d_rows), self.steps, self.place, (attn,),
            (self.starts, self.frames, self.vec), [starts_spec(self.starts), row_blocks(D), kept(16, D)],
            [by_rows(rows, D)] * 4
            + [(lse_spec(), shape(self.steps, 16, FRAMES, dtype=F32)), by_rows(rows, D, F32), by_rows(rows, 1, F32)],
            weights(*[(self.d_max, D)] * 4), after,
            flops=rows * D * D * 8 + rows * FRAMES * D * 16, moved=rows * D * 14,
        )

    def ffn_up(self, up, n1, after=()):
        rows = self.rows
        return call(
            functools.partial(ffn_up, rows=self.d_rows), self.steps, self.place, (up,),
            (n1, self.vec, self.b1), [row_blocks(D), kept(16, D), kept(8, FF)],
            [by_rows(rows, FF)] * 2, weights((self.d_max, FF)), after,
            flops=rows * D * FF * 4, moved=rows * FF * 6,
        )

    def ffn_down(self, down, n1, hidden, cotangent, halves, after=()):
        rows = self.rows
        return call(
            functools.partial(ffn_down, rows=self.ff_rows, halves=halves), self.steps, self.place, (down,),
            (n1, hidden, cotangent, self.vec), [row_blocks(D), row_blocks(FF), row_blocks(D), kept(16, D)],
            [by_rows(rows, D), by_rows(rows, D), by_rows(rows, D, F32), summed(8, D)]
            + grads_out(halves, [(self.ff_max, D, self.ff_rows)]),
            [pltpu.VMEM((self.ff_max, D), F32)] + weights((self.ff_max, D)), after,
            flops=rows * D * FF * 6, moved=rows * FF * 8,
        )

    def ffn_backward(self, attn, up, down, n1, rstd, dz, dr2, slope, o, after=()):
        rows = self.rows
        return call(
            functools.partial(ffn_backward, rows=(self.d_rows, self.ff_rows), halves=self.halves),
            self.steps, self.place, (attn, up, down),
            (self.starts, n1, rstd, dz, dr2, slope, o, self.vec),
            [starts_spec(self.starts)] + [row_blocks(w) for w in (D, 1, D, D, FF, D)] + [kept(16, D)],
            [by_rows(rows, D, F32), by_rows(rows, D), summed(8, D), summed(8, FF)]
            + grads_out(
                self.halves,
                [(self.d_max, D, self.d_rows)] * 5,
            ),
            [pltpu.VMEM((FRAMES, FF), BF16), pltpu.VMEM((self.d_max, FF), F32), pltpu.VMEM((self.d_max, D), F32)]
            + weights((self.d_max, FF), (self.ff_max, D), (self.d_max, D)) + [COPIES], after,
            flops=rows * D * FF * 8 + rows * D * D * 4, moved=rows * FF * 8,
        )

    def attn_backward(self, q, k, v, do, lse, attn=None, vectors=(), after=()):
        rows = self.rows
        own = [row_blocks(D)] * 4
        return call(
            functools.partial(attn_backward, rows=self.d_rows, halves=self.halves),
            self.steps, self.place, (attn,) if attn else (),
            (*vectors, self.starts, self.frames, self.vec, q, k, v, do, lse),
            [kept(*vector.shape) for vector in vectors]
            + [starts_spec(self.starts), row_blocks(D), kept(16, D)] + own + [lse_spec()],
            [by_rows(rows, D)] * 3 + [summed(8, D)]
            + grads_out(self.halves, [(self.d_max, D, self.d_rows)] * 3, 8),
            [pltpu.VMEM((self.d_max, D), F32)] * 3 + (weights(*[(self.d_max, D)] * 3) if attn else []), after,
            flops=rows * D * D * 6 + rows * FRAMES * D * 40, moved=rows * D * 14,
        )

    def input_backward(self, attn, dr1, parts, after=()):
        rows = self.rows
        return call(
            functools.partial(input_backward, rows=self.d_rows), self.steps, self.place, (attn,),
            (self.starts, dr1, *parts),
            [starts_spec(self.starts), row_blocks(D)] + [row_blocks(part.shape[1]) for part in parts],
            [by_rows(rows, D)], weights(*[(self.d_max, D)] * 3), after,
            flops=rows * D * D * 8, moved=rows * D * 12,
        )


def local(kernel, outputs, place, operands, wide=False):
    count = len(operands)

    def body(place_ref, *refs):
        sources, outs = refs[:count], refs[count : count + len(outputs)]
        held_refs, sems = refs[count + len(outputs) : -1], refs[-1]
        copies = [
            pltpu.make_async_copy(source, target, sems.at[i])
            for i, (source, target) in enumerate(zip(sources, held_refs))
        ]
        for copy in copies:
            copy.start()
        for copy in copies:
            copy.wait()
        kernel(place_ref, held_refs, outs)

    vmem = pl.BlockSpec(memory_space=pltpu.VMEM)
    return pl.pallas_call(
        body,
        in_specs=[SCALARS] + [WHOLE] * count,
        out_specs=[vmem] * len(outputs),
        out_shape=outputs,
        scratch_shapes=[pltpu.VMEM(array.shape, array.dtype) for array in operands]
        + [pltpu.SemaphoreType.DMA((count,))],
        compiler_params=pltpu.CompilerParams(
            vmem_limit_bytes=VMEM_LIMIT if wide else 4 * 2**20 + sum(4 * a.size for a in (*operands, *outputs))
        ),
        cost_estimate=pl.CostEstimate(flops=1000, bytes_accessed=4 * sum(a.size for a in operands), transcendentals=0),
    )(place, *operands)


def first_sums(place, kept_half, received):
    owners, _, rows, width = kept_half.shape

    def kernel(place_ref, refs, outs):
        for j in range(4):
            for z in range(owners // 2):
                owner, part = 2 * z + ((place_ref[1] % 2) ^ (j // 2)), place_ref[2] ^ (j % 2)
                outs[j][z] = (refs[0][owner, part].astype(F32) + refs[1][owner, part].astype(F32)).astype(BF16)

    return local(kernel, [shape(owners // 2, rows, width)] * 4, place, [kept_half, received])


def first_sums_from_hbm(place, kept_half, received):
    owners, _, rows, width = kept_half.shape
    steps = owners // 2

    def body(place_ref, kept_hbm, received_hbm, *refs):
        outs, (one, two), results, (in_sems, out_sems) = refs[:4], refs[4:6], refs[6:10], refs[10:]
        copies = []
        for z in range(steps):
            part = pl.ds(2 * z, 2)
            copies.append(
                [
                    pltpu.make_async_copy(source.at[part], target.at[part], in_sems.at[z, i])
                    for i, (source, target) in enumerate(((kept_hbm, one), (received_hbm, two)))
                ]
            )
            for copy in copies[-1]:
                copy.start()
        leaving = []
        for z in range(steps):
            for copy in copies[z]:
                copy.wait()
            for j in range(4):
                owner, part = 2 * z + ((place_ref[1] % 2) ^ (j // 2)), place_ref[2] ^ (j % 2)
                results[j][z] = (one[owner, part].astype(F32) + two[owner, part].astype(F32)).astype(BF16)
                leaving.append(pltpu.make_async_copy(results[j].at[z], outs[j].at[z], out_sems.at[z, j]))
                leaving[-1].start()
        for copy in leaving:
            copy.wait()

    out = shape(steps, rows, width)
    return pl.pallas_call(
        body,
        in_specs=[SCALARS, WHOLE, WHOLE],
        out_specs=[WHOLE] * 4,
        out_shape=[out] * 4,
        scratch_shapes=[pltpu.VMEM(kept_half.shape, BF16)] * 2
        + [pltpu.VMEM(out.shape, BF16)] * 4
        + [pltpu.SemaphoreType.DMA((steps, 2)), pltpu.SemaphoreType.DMA((steps, 4))],
        compiler_params=pltpu.CompilerParams(
            vmem_limit_bytes=VMEM_LIMIT
        ),
        cost_estimate=pl.CostEstimate(flops=1000, bytes_accessed=6 * kept_half.size, transcendentals=0),
    )(place, kept_half, received)


def next_sums(place, parts, arrays):
    def kernel(place_ref, refs, outs):
        for j in range(4):
            piece = (place_ref[1] // 2) ^ j
            total = refs[0][piece].astype(F32)
            for ref in refs[1:]:
                total = total + ref[piece].astype(F32)
            outs[j * arrays // 4][j % (4 // arrays)] = total.astype(BF16)

    return local(kernel, [shape(4 // arrays, *parts[0].shape[1:])] * arrays, place, parts)


def finish(place, groups, outputs):
    flat = [array for group in groups for array in group]
    outs_shape = [shape(rows, cols, dtype=F32) for rows, cols, _ in outputs]

    def kernel(place_ref, refs, outs):
        for ref, (rows, cols, sources) in zip(outs, outputs):
            filled = len(sources) * D
            if cols > filled:
                ref[:, filled:] = jnp.zeros((rows, cols - filled), F32)
            size = rows // 4
            for group, row, column in sources:
                for j in range(4):
                    quarter = 2 * (place_ref[0] ^ (j // 2)) + (place_ref[2] ^ (j % 2))
                    value = refs[4 * group + j][...].astype(F32)
                    low = pl.multiple_of(quarter * size, 8)
                    ref[pl.ds(low, size), column : column + D] = value[row : row + size]

    return local(kernel, outs_shape, place, flat)


def unpack(place, stacks, first, count, wide, names):
    owners = 2 * stacks[0].shape[0]

    def kernel(place_ref, refs, outs):
        vec_ref, wide_ref = outs
        lanes = lax.broadcasted_iota(jnp.int32, (16, owners * count), 1)
        total = jnp.zeros((16, owners * count), F32)
        codes = far_codes(owners // 2)
        for code in range(owners):
            owner = place_ref[1] ^ code
            rows = refs[code % 2][codes.index(code // 2), first : first + 16, :].astype(F32)
            row = jnp.pad(rows[:, :count], ((0, 0), (0, (owners - 1) * count)))
            total = total + pltpu.roll(row, owner * count, 1)
            wide_ref[:, pl.ds(pl.multiple_of(owner * wide, 128), wide)] = jnp.broadcast_to(
                rows[names : names + 1, :wide], (8, wide)
            )
        vec_ref[...] = total[:, :D]

    return local(
        kernel, [shape(16, D, dtype=F32), shape(8, owners * wide, dtype=F32)], place, stacks
    )


def small_total(place, attn, one, two, wide):
    def kernel(place_ref, refs, outs):
        both, first, second, broad = (ref[...] for ref in refs)
        rows = [both[0:2], first[0:3], second[1:3], second[0:1]]
        rows += [broad[0:1, j * D : (j + 1) * D] for j in range(FF // D)]
        rows += [both[2:5], first[3:4]]
        row = 0
        for part in rows:
            outs[0][row : row + part.shape[0], :] = part
            row += part.shape[0]

    return local(kernel, [shape(16, D, dtype=F32)], place, [attn, one, two, wide])[0]


def last_sums(parts):
    return sum(part.astype(F32) for part in parts).astype(BF16)


def tie(value, *before):
    return lax.optimization_barrier((value, *before))[0]


def in_order(value, order):
    return jnp.concatenate([lax.dynamic_slice_in_dim(value, order[i], 1) for i in range(value.shape[0])])


class Grid:
    def __init__(self, dp, fsdp):
        self.dp, self.fsdp = dp, fsdp
        self.dp_bits = [1 << i for i in range(dp.bit_length() - 1)]
        self.fsdp_bits = [1 << i for i in range(fsdp.bit_length() - 1)]

    def bit(self, axis, bit):
        return (lax.axis_index(axis) // bit) % 2

    def swap(self, value, dp_mask, fsdp_mask):
        if not dp_mask:
            return lax.ppermute(value, "fsdp", [(i, i ^ fsdp_mask) for i in range(self.fsdp)])
        if not fsdp_mask:
            return lax.ppermute(value, "dp", [(i, i ^ dp_mask) for i in range(self.dp)])
        pairs = [
            (i * self.fsdp + j, (i ^ dp_mask) * self.fsdp + (j ^ fsdp_mask))
            for i in range(self.dp)
            for j in range(self.fsdp)
        ]
        return lax.ppermute(value, ("dp", "fsdp"), pairs)

    def gather(self, piece):
        gathered = piece[None]
        for bit in self.fsdp_bits:
            gathered = jnp.concatenate([gathered, self.swap(gathered, 0, bit)])
        return gathered

    def joined(self, stack, bit, *before):
        other = self.swap(stack, 0, bit)
        return jnp.concatenate([stack, tie(other, *before) if before else other])

    def stages(self):
        dp_left, fsdp_left = self.dp_bits[1:], list(self.fsdp_bits)
        order = [[("dp", 1)]]
        while dp_left and fsdp_left:
            order.append([("dp", dp_left.pop(0)), ("fsdp", fsdp_left.pop(0))])
        order += [[("dp", bit)] for bit in dp_left]
        while fsdp_left:
            order.append([("fsdp", bit) for bit in fsdp_left[:2]])
            fsdp_left = fsdp_left[2:]
        return order

    def reduce(self, grads):
        rows, width = grads.shape[1:]
        left = list(reversed(self.fsdp_bits))
        value = grads.reshape((2,) * len(left) + (rows, width))
        halved = []
        for stage in self.stages():
            for axis, bit in stage:
                if axis == "dp":
                    value = value.reshape(value.shape[:-2] + (2, value.shape[-2] // 2, width))
                    halved.append(bit)
            spots = {}
            extra = len(left)
            for axis, bit in stage:
                if axis == "dp":
                    spots[(axis, bit)] = extra
                    extra += 1
                else:
                    spots[(axis, bit)] = left.index(bit)
            total = None
            for code in range(1 << len(stage)):
                starts = [0] * value.ndim
                sizes = list(value.shape)
                masks = {"dp": 0, "fsdp": 0}
                for place, (axis, bit) in enumerate(stage):
                    other = (code >> place) & 1
                    starts[spots[(axis, bit)]] = self.bit(axis, bit) ^ other
                    sizes[spots[(axis, bit)]] = 1
                    masks[axis] += bit * other
                part = lax.dynamic_slice(value, starts, sizes)
                if code:
                    part = self.swap(part, masks["dp"], masks["fsdp"])
                part = part.astype(F32)
                total = part if total is None else total + part
            total = jnp.squeeze(total, tuple(spots.values()))
            left = [bit for bit in left if ("fsdp", bit) not in spots]
            value = total.astype(BF16)
        for bit in reversed(halved):
            other = self.swap(value, bit, 0)
            first = self.bit("dp", bit) == 0
            value = jnp.concatenate([jnp.where(first, value, other), jnp.where(first, other, value)])
        return value.astype(F32)

    def total(self, value):
        masks = [(bit | 1, 0) for bit in reversed(self.dp_bits)] + [(1, bit) for bit in reversed(self.fsdp_bits)]
        for dp_mask, fsdp_mask in masks:
            value = value + self.swap(value, dp_mask, fsdp_mask)
        return value


def packed_vectors(rows, count, wide, names):
    owners = rows.shape[0]
    vec = rows[:, : names * count].reshape(owners, names, count)
    vec = jnp.swapaxes(vec, 0, 1).reshape(names, owners * count)[:, :D].astype(F32)
    b1 = rows[:, names * count : names * count + wide].reshape(1, -1)[:, :FF].astype(F32)
    return jnp.pad(vec, ((0, 16 - names), (0, 0))), jnp.broadcast_to(b1, (8, FF))


VECTORS = ("qb", "vb", "ob", "g1", "s1", "g2", "s2", "b2")


def vector_grads(small, weights, count, wide, d_max, ff_max):
    me = lax.axis_index("fsdp")
    rows = jnp.pad(small, ((0, 0), (0, d_max - D)))
    rows = lax.dynamic_slice(rows, (0, me * count), (small.shape[0], count))
    grads = {name: rows[i] for i, name in enumerate(VECTORS)}
    wide_at = len(VECTORS)
    b1 = jnp.pad(small[wide_at : wide_at + FF // D].reshape(-1), (0, ff_max - FF))
    grads["b1"] = lax.dynamic_slice(b1, (me * wide,), (wide,))
    sums = small[wide_at + FF // D :]
    total = sum(weight[:, :D].astype(F32) * sums[i : i + 1] for i, weight in enumerate(weights))
    within = me * count + jnp.arange(count, dtype=jnp.int32) < D
    grads["m"] = jnp.where(within, jnp.sum(total, axis=1), 0.0) + rows[-1]
    return grads


def in_columns(weight):
    return [weight[:, j * D : (j + 1) * D] for j in range(FF // D)]


def any_grid(grid, frames, cotangent, span_starts, matrices, vectors, up_bias):
    query, key, value, out, up, down = matrices
    count, wide = query.shape[0], down.shape[0]
    owners = grid.fsdp
    d_max, ff_max = count * owners, wide * owners
    me, core = lax.axis_index("fsdp"), lax.axis_index("dp") % 2
    codes = me ^ jnp.arange(owners, dtype=jnp.int32)

    def gathered(pieces):
        stack = in_order(grid.gather(jnp.concatenate(pieces)), codes)
        stack = stack.reshape(owners, len(pieces), -1, D)
        return [stack[:, i].reshape(-1, D) for i in range(len(pieces))]

    packed = jnp.concatenate(vectors + [up_bias]).reshape(1, -1)
    packed = in_order(grid.gather(packed)[:, 0], codes)
    vec, b1 = packed_vectors(packed, count, wide, len(vectors))
    wq, wk, wv, wo = gathered([piece[:, :D] for piece in (query, key, value, out)])
    up_blocks = gathered(in_columns(up))
    (w2,) = gathered([down[:, :D]])

    def unit(role_zero, role_one):
        first = core == 0
        return ([jnp.where(first, role_zero, role_one)[None]], [jnp.where(first, role_one, role_zero)[None]])

    quarter = lax.axis_index("dp") % 4
    stacked = jnp.stack([wq, wk, wv, wo])
    attn = [[lax.dynamic_slice_in_dim(stacked, quarter ^ flip, 1)] for flip in (0, 2, 1, 3)]
    up_unit = unit(jnp.concatenate(up_blocks[:2]), jnp.concatenate(up_blocks[2:]))
    down_unit = unit(w2[: ff_max // 2], w2[ff_max // 2 :])
    place = jnp.stack([core, jnp.zeros_like(core), quarter // 2])
    layer = Layer(place, span_starts[:, None, :], frames, vec, b1, d_max, ff_max, d_max, ff_max, False)
    q, k, v, o, lse, n1, rstd = layer.attn_forward(attn)
    hidden, slope = layer.ffn_up(up_unit, n1)
    output, dz, dr2, small2, down_grad = layer.ffn_down(down_unit, n1, hidden, cotangent, False)
    dr1, do, small1, wide_small, *up_out = layer.ffn_backward(
        attn, up_unit, down_unit, n1, rstd, dz, dr2, slope, o
    )
    dq, dk, dv, small_a, *qkv = layer.attn_backward(q, k, v, do, lse)
    frames_grad = layer.input_backward(attn, dr1, (dq, dk, dv))[0]
    small = grid.total(small_total(place, small_a, small1, small2, wide_small))

    def reduced(grads):
        total = grid.reduce(jnp.concatenate([grad.reshape(owners, -1, D) for grad in grads], axis=1))
        return [part for part in total.reshape(len(grads), -1, D)]

    def wide_rows(grad):
        return jnp.pad(grad, ((0, 0), (0, d_max - D)))

    sums = [wide_rows(grad) for grad in reduced(qkv)]
    up_out = reduced(up_out)
    sums.append(wide_rows(up_out[-1]))
    zeros = jnp.zeros((count, up.shape[1] - FF), F32)
    sums.append(jnp.concatenate(up_out[:-1] + [zeros], axis=1))
    sums.append(wide_rows(reduced([down_grad])[0]))
    return output, frames_grad, sums, vector_grads(small, matrices[:3], count, wide, d_max, ff_max)


def four_by_eight(grid, frames, cotangent, span_starts, matrices, vectors, up_bias):
    query, key, value, out, up, down = matrices
    count, wide = query.shape[0], down.shape[0]
    owners = grid.fsdp
    d_max, ff_max = count * owners, wide * owners
    me, dp_at = lax.axis_index("fsdp"), lax.axis_index("dp")
    core = dp_at % 2
    first = core == 0
    place = jnp.stack([core, me, dp_at // 2])

    packed = jnp.pad(jnp.stack(vectors), ((0, 0), (0, D - count)))
    packed = jnp.concatenate([packed, jnp.pad(up_bias, (0, D - wide))[None]])
    packed = jnp.pad(packed, ((0, 16 - packed.shape[0]), (0, 0)))
    half = wide // 2
    blocks = in_columns(up)
    attn_piece = jnp.where(
        dp_at < 2, jnp.where(first, query[:, :D], key[:, :D]), jnp.where(first, value[:, :D], out[:, :D])
    )
    up_piece = jnp.where(first, jnp.concatenate(blocks[:2]), jnp.concatenate(blocks[2:]))
    down_piece = jnp.where(first, down[:half, :D], down[half:, :D])

    def other_core(value):
        return grid.swap(value, 1, 0)

    high, low = 4, 2
    attn_pairs = grid.joined(attn_piece[None], high)
    attn_pairs = jnp.concatenate([attn_pairs, grid.joined(packed[None], high)], axis=1)
    far = grid.joined(attn_pairs, low)
    up_far = grid.joined(tie(up_piece, attn_pairs)[None], high)
    far = tie(far, up_far)
    far_along = grid.swap(far, 2, 0)
    near = grid.swap(far, 0, 1)
    up_pairs, up_more = up_far, grid.swap(tie(up_far, far), 0, low)
    near_along = grid.swap(tie(near, far_along, up_more), 2, 0)
    down_far = grid.joined(tie(down_piece, up_pairs)[None], high)
    attn = [[far, near], [far_along, near_along]]
    attn += [[other_core(far), other_core(near)], [other_core(far_along), other_core(tie(near_along, down_far))]]
    vec, b1 = unpack(place, [far, near], count, count, wide, len(vectors))
    up_far = jnp.concatenate([up_pairs, up_more])
    up_near = grid.swap(tie(up_far, near), 0, 1)

    layer = Layer(place, span_starts[:, None, :], frames, vec, b1, count, wide, d_max, ff_max, True)
    q, k, v, o, lse, n1, rstd = layer.attn_forward(attn, after=(up_far, down_far))
    down_far = grid.joined(tie(down_far, up_far), low, n1)
    down_near = grid.swap(tie(down_far, up_near), 0, 1)
    up_unit = [[up_far, up_near], [other_core(up_far), other_core(tie(up_near, down_far))]]
    hidden, slope = layer.ffn_up(up_unit, n1)
    down_unit = [[down_far, down_near], [other_core(down_far), other_core(tie(down_near, hidden))]]
    output, dz, dr2, small2, down_grad = layer.ffn_down(down_unit, n1, hidden, cotangent, False)
    down_sum = lax.psum_scatter(down_grad.reshape(owners, wide, D), "fsdp", scatter_dimension=0)
    dr1, do, small1, wide_small, *up_out = layer.ffn_backward(
        attn, up_unit, down_unit, n1, rstd, dz, dr2, slope, o
    )

    def spread(kept_half, received, from_hbm=False):
        parts = (first_sums_from_hbm if from_hbm else first_sums)(place, kept_half, received)
        return parts[0], [grid.swap(parts[j], 2 * (j % 2), j // 2) for j in range(1, 4)]

    def spread_far(parts):
        pieces = next_sums(place, parts, 4)
        return [pieces[0]] + [grid.swap(pieces[j], 0, 2 * j) for j in range(1, 4)]

    own_u, got_u = spread(up_out[0], other_core(up_out[1]))
    dq, dk, dv, _, *qkv = layer.attn_backward(
        q, k, v, do, lse, attn, (small1, small2, wide_small), after=(own_u,)
    )
    received_q = other_core(tie(qkv[1], *got_u))
    pair_u, sent_u = next_sums(place, [tie(own_u, qkv[1])] + got_u, 2)
    got_far_u = grid.swap(sent_u, 0, high)
    own_q, got_q = spread(tie(qkv[0], pair_u), received_q, True)
    def halved(value, mask):
        size = value.shape[0] // 2
        mine = (dp_at // mask) % 2
        return [lax.dynamic_slice_in_dim(value, at * size, size) for at in (mine, 1 - mine)]

    kept_part, sent = halved(tie(down_sum, own_q), 1)
    down_half = last_sums([kept_part, grid.swap(sent, 1, 0)])
    kept_part, sent = halved(down_half, 2)
    got_down = grid.swap(sent, 2, 0)
    frames_grad = layer.input_backward(attn, dr1, (dq, dk, dv), after=(pair_u, down_half))[0]
    far_q = spread_far([tie(own_q, frames_grad)] + got_q)
    pair_u = last_sums([pair_u, tie(got_far_u, frames_grad)])
    sum_u = last_sums([pair_u[0], tie(grid.swap(pair_u[1], 0, low), far_q[0])])
    down_part = last_sums([kept_part, tie(got_down, frames_grad)])
    sum_u = jnp.concatenate([sum_u, down_part])
    cross_u = grid.swap(sum_u, 3, 0)
    sum_q = last_sums([far_q[0]] + [tie(part, cross_u) for part in far_q[1:]])[0]
    along_q = grid.swap(sum_q, 2, 0)
    total_u = [sum_u, other_core(cross_u), other_core(sum_u), cross_u]
    quarter = count // 4
    blocks_up = FF // D
    up_sum, out_sum, down_out = finish(
        place, [total_u],
        [
            (count, up.shape[1], [(0, j * quarter, j * D) for j in range(blocks_up)]),
            (count, d_max, [(0, blocks_up * quarter, 0)]),
            (wide, d_max, [(0, (blocks_up + 1) * quarter, 0)]),
        ],
    )
    total_q = [sum_q, along_q, other_core(sum_q), other_core(tie(along_q, up_sum))]
    *qkv_sums, small = finish(
        place, [total_q],
        [(count, d_max, [(0, j * quarter, 0)]) for j in range(3)] + [(32, D, [(0, 3 * quarter, 0)])],
    )
    vectors_out = {name: small[i, :count] for i, name in enumerate(VECTORS + ("m",))}
    vectors_out["b1"] = small[len(VECTORS) + 1, :wide]
    return output, frames_grad, [*qkv_sums, out_sum, up_sum, down_out], vectors_out


def on_device(
    sizes, frames, cotangent, span_starts, query_weight, key_weight, value_weight, out_weight,
    query_bias, value_bias, out_bias, first_gain, first_shift, up_weight, up_bias, down_weight,
    down_bias, second_gain, second_shift, mask_vector,
):
    grid = Grid(*sizes)
    matrices = (query_weight, key_weight, value_weight, out_weight, up_weight, down_weight)
    vectors = [query_bias, value_bias, out_bias, first_gain, first_shift, mask_vector,
               second_gain, second_shift, down_bias]
    placed = sizes == (4, 8) and query_weight.shape[0] % 32 == 0
    program = four_by_eight if placed else any_grid
    output, frames_grad, sums, small = program(
        grid, frames, cotangent, span_starts, matrices, vectors, up_bias
    )
    return (
        output, frames_grad, *sums[:4], small["qb"], small["vb"], small["ob"], small["g1"], small["s1"],
        sums[4], small["b1"], sums[5], small["b2"], small["g2"], small["s2"], small["m"],
    )


def solution(mesh):
    sizes = (mesh.shape["dp"], mesh.shape["fsdp"])
    tokens = P(("dp", "fsdp"), None)
    matrix, vector = P("fsdp", None), P("fsdp")
    return jax.shard_map(
        functools.partial(on_device, sizes),
        mesh=mesh,
        in_specs=(tokens,) * 3 + (matrix,) * 4 + (vector,) * 5 + (matrix, vector, matrix) + (vector,) * 4,
        out_specs=(tokens,) * 2 + (matrix,) * 4 + (vector,) * 5 + (matrix, vector, matrix) + (vector,) * 4,
        check_vma=False,
    )
```
